32 devices in a mesh: dp: 8 (over z, y), tensor: 4 (over x, core).
Axes of the slice: x: 2, y: 2, z: 4, core: 2. Of those that a mesh axis runs over, the one named last changes fastest.
Arguments:
- tokens: bfloat16 [16384, 512], P(('dp', 'tensor')), may hold values from -6 to 6
- norm_gain: float32 [512], replicated, may hold values from 0.1 to 1.9
- norm_shift: float32 [512], replicated, may hold values from -3 to 3
- heads_weight: bfloat16 [512, 3, 512], P(None, None, 'tensor'), may hold values from -0.25 to 0.25
- output_weight: bfloat16 [512, 512], P('tensor'), may hold values from -2 to 2
- output_bias: float32 [512], replicated, may hold values from -3 to 3
- gate_weight: bfloat16 [512, 512], replicated, may hold values from -0.25 to 0.25
- gate_bias: float32 [512], replicated, may hold values from -3 to 3
- second_gain: float32 [512], replicated, may hold values from 0.1 to 1.9
- second_shift: float32 [512], replicated, may hold values from -3 to 3
- up_weight: bfloat16 [512, 2048], P(None, 'tensor'), may hold values from -0.25 to 0.25
- up_bias: bfloat16 [2048], P('tensor'), may hold values from -3 to 3
- down_weight: bfloat16 [2048, 512], P('tensor'), may hold values from -0.125 to 0.125
- down_bias: float32 [512], replicated, may hold values from -3 to 3
- pass_weight: bfloat16 [512, 512], replicated, may hold values from -0.25 to 0.25
- pass_bias: float32 [512], replicated, may hold values from -3 to 3
- lengths: int32 [16], replicated, may hold values from 0 to 2048, as said below
- owners: int32 [16], replicated, may hold values from 0 to 7, as said below
- cotangent: bfloat16 [16384, 512], P(('dp', 'tensor')), may hold values from -6 to 6
Outputs:
- output: bfloat16 [16384, 512], P(('dp', 'tensor'))
- tokens_grad: bfloat16 [16384, 512], P(('dp', 'tensor'))
- norm_gain_grad: float32 [512], replicated
- norm_shift_grad: float32 [512], replicated
- heads_weight_grad: float32 [512, 3, 512], P(None, None, 'tensor')
- output_weight_grad: float32 [512, 512], P('tensor')
- output_bias_grad: float32 [512], replicated
- gate_weight_grad: float32 [512, 512], replicated
- gate_bias_grad: float32 [512], replicated
- second_gain_grad: float32 [512], replicated
- second_shift_grad: float32 [512], replicated
- up_weight_grad: float32 [512, 2048], P(None, 'tensor')
- up_bias_grad: float32 [2048], P('tensor')
- down_weight_grad: float32 [2048, 512], P('tensor')
- down_bias_grad: float32 [512], replicated
- pass_weight_grad: float32 [512, 512], replicated
- pass_bias_grad: float32 [512], replicated
The draws below stay inside these ranges and needn't reach their ends.
Inputs may be any that keep to these rules, and one draw needn't show every extreme that they name: A length of 0 marks an unused entry. The entries of one index of dp sum to at most 2048; in every draw some index holds a single sequence of exactly 2048; the other nonzero lengths lie in 512 to 1024. `owners`: every index of dp owns 2 entries, used or not.
All inputs are finite; a program needn't handle non-finite values.
Results may differ from the reference program's by a relative error of at most 0.012.
Values may be sent and summed in bfloat16 or wider, within the bound.
No kernel may reach another device: no remote copies, remote signals or barrier semaphores. Data moves between devices by JAX's collectives and lax.ppermute only.
A program may use at most 128 MiB of HBM per device.

```python
from functools import partial
import jax
import jax.numpy as jnp
from jax import lax

D = 512
HEADS = 8
HD = 64
FF = 2048
TOK_DEV = 2048
SHORT = 512
SEQ_DEV = 2
TOKENS = 16384
N_DP = 8


def draw_plan(key):
    count_key, length_key, order_key, shift_key = jax.random.split(key, 4)
    offset = jax.random.randint(shift_key, (), 0, 8)
    device_ids = jnp.arange(N_DP, dtype=jnp.int32)
    long_device = (device_ids + offset) % 8 == 0
    counts = jax.random.randint(count_key, (N_DP,), 2, SEQ_DEV + 1)
    entry_slot = jnp.arange(SEQ_DEV, dtype=jnp.int32)
    short_lengths = jax.random.randint(length_key, (N_DP, SEQ_DEV), SHORT, 2 * SHORT + 1)
    short_lengths = jnp.where(entry_slot[None, :] < counts[:, None], short_lengths, 0)
    long_lengths = jnp.where(entry_slot == 0, TOK_DEV, 0)
    all_lengths = jnp.where(long_device[:, None], long_lengths[None, :], short_lengths).astype(jnp.int32)
    owner_table = jnp.broadcast_to(device_ids[:, None], (N_DP, SEQ_DEV)).astype(jnp.int32)
    order = jax.random.permutation(order_key, N_DP * SEQ_DEV)
    return (all_lengths.reshape(-1)[order], owner_table.reshape(-1)[order])


def draw_lengths(key, part):
    return draw_plan(key)[0]


def draw_owners(key, part):
    return draw_plan(key)[1]


def block_levels(key, extent, cuts, least, largest):
    gain = 1.0
    for dim, parts in cuts:
        heights = jax.random.uniform(jax.random.fold_in(jax.random.fold_in(key, 6), dim), (parts,), jnp.float32, least / len(cuts), largest / len(cuts))
        gain = gain * jnp.repeat(jnp.exp(heights), extent[dim] // parts).reshape((-1,) + (1,) * (len(extent) - 1 - dim))
    return gain


def gaussian(own_key, extent, width, most, cuts=(), kind=jnp.bfloat16):
    gain = block_levels(own_key, extent, cuts, -0.22, 0.18) if cuts else 1.0
    values = jax.random.normal(own_key, extent, jnp.float32) * width * gain
    return jnp.minimum(jnp.maximum(values, -most), most).astype(kind)


def setup_inputs(seed: int = 0) -> dict:
    keys = jax.random.split(jax.random.key(seed), 20)
    return {
        "tokens": gaussian(keys[0], (TOKENS, D), 1.0, 6.0, ((0, 32),)),
        "norm_gain": jnp.clip(1.0 + 0.18 * jax.random.normal(keys[1], (D,), jnp.float32), 0.1, 1.9),
        "norm_shift": gaussian(keys[2], (D,), 0.5, 3.0, (), jnp.float32),
        "heads_weight": gaussian(keys[3], (D, 3, D), D ** -0.5, 0.25, ((2, 4),)),
        "output_weight": gaussian(keys[4], (D, D), (D // 64) ** -0.5, 2.0, ((0, 4),)),
        "output_bias": gaussian(keys[5], (D,), 0.5, 3.0, (), jnp.float32),
        "gate_weight": gaussian(keys[6], (D, D), D ** -0.5, 0.25),
        "gate_bias": gaussian(keys[7], (D,), 1.0, 3.0, (), jnp.float32),
        "second_gain": jnp.clip(1.0 + 0.18 * jax.random.normal(keys[8], (D,), jnp.float32), 0.1, 1.9),
        "second_shift": gaussian(keys[9], (D,), 0.5, 3.0, (), jnp.float32),
        "up_weight": gaussian(keys[10], (D, FF), D ** -0.5, 0.25, ((1, 4),)),
        "up_bias": gaussian(keys[11], (FF,), 0.5, 3.0, ((0, 4),)),
        "down_weight": gaussian(keys[12], (FF, D), FF ** -0.5, 0.125, ((0, 4),)),
        "down_bias": gaussian(keys[13], (D,), 0.5, 3.0, (), jnp.float32),
        "pass_weight": gaussian(keys[14], (D, D), D ** -0.5, 0.25),
        "pass_bias": gaussian(keys[15], (D,), 1.0, 3.0, (), jnp.float32),
        "lengths": draw_lengths(jax.random.fold_in(keys[19], 71), 0),
        "owners": draw_owners(jax.random.fold_in(keys[19], 71), 0),
        "cotangent": gaussian(keys[18], (TOKENS, D), 1.0, 6.0, ((0, 32),)),
    }


EPS = 1e-05
SCALE = 0.125
NEGATIVE = -1e+30
GELU_C = 0.7978845608028654
HIGH = lax.Precision.HIGHEST

@jax.custom_vjp
def low(v):
    return lax.optimization_barrier(v.astype(jnp.bfloat16)).astype(jnp.float32)

@jax.custom_vjp
def low_back(v):
    return v

def low_keep(v):
    return (low(v), None)

def low_pass(kept, grad):
    return (grad,)

def back_keep(v):
    return (v, None)

def back_low(kept, grad):
    return (low(grad),)
low.defvjp(low_keep, low_pass)
low_back.defvjp(back_keep, back_low)

def layer_norm(values, gain_row, shift_row):
    centred = values - lax.optimization_barrier(jnp.mean(values, axis=-1, keepdims=True))
    spread = lax.optimization_barrier(jnp.mean(centred * centred, axis=-1, keepdims=True))
    return centred * lax.rsqrt(spread + EPS) * gain_row + shift_row

def gelu_tanh(values):
    return 0.5 * values * (1.0 + jnp.tanh(GELU_C * (values + 0.044715 * values * values * values)))

def layout(lengths, owners, device, slot_count):
    owned_entry = owners == device
    own_lengths = jnp.where(owned_entry, lengths, 0).astype(jnp.int32)
    end_slots = jnp.cumsum(own_lengths).astype(jnp.int32)
    starts = (end_slots - own_lengths).astype(jnp.int32)
    places = jnp.arange(slot_count, dtype=jnp.int32)
    inside = ((places[:, None] >= starts[None, :]) & (places[:, None] < end_slots[None, :])).astype(jnp.int32)
    entries = jnp.arange(lengths.shape[0], dtype=jnp.int32)
    live_rows = lax.optimization_barrier(jnp.sum(inside, axis=1)).astype(jnp.int32)
    labels = lax.optimization_barrier(jnp.sum(inside * entries[None, :], axis=1)).astype(jnp.int32)
    labels = jnp.where(live_rows > 0, labels, -1 - places)
    return (labels, live_rows)

def attend_block(queries, key_rows, value_rows, query_labels, key_labels, first_row):
    scores = low_back(jnp.einsum('qhd,khd->hqk', queries, key_rows, precision=HIGH) * SCALE)
    query_places = first_row + jnp.arange(queries.shape[0], dtype=jnp.int32)
    key_places = jnp.arange(key_rows.shape[0], dtype=jnp.int32)
    allowed = (query_labels[:, None] == key_labels[None, :]) & (key_places[None, :] <= query_places[:, None])
    scores = jnp.where(allowed[None], scores, NEGATIVE)
    maximum = lax.optimization_barrier(jnp.max(scores, axis=2, keepdims=True))
    exponent = jnp.exp(scores - maximum)
    weights = low(exponent / lax.optimization_barrier(jnp.sum(exponent, axis=2, keepdims=True)))
    return jnp.einsum('hqk,khd->qhd', weights, value_rows, precision=HIGH)

def forward(block_rows, params, labels, live_rows):
    norm_gain, norm_shift, heads_weight, output_weight, output_bias, gate_weight, gate_bias, second_gain, second_shift, up_weight, up_bias, down_weight, down_bias, pass_weight, pass_bias = params
    row_count = block_rows.shape[0]
    norm_one = low(layer_norm(block_rows, norm_gain, norm_shift))
    projected = low(low_back(jnp.dot(norm_one, heads_weight.reshape(D, 3 * D), precision=HIGH)))
    queries = projected[:, :D].reshape(row_count, HEADS, HD)
    key_rows = projected[:, D:2 * D].reshape(row_count, HEADS, HD)
    value_rows = projected[:, 2 * D:].reshape(row_count, HEADS, HD)
    block_size = min(512, row_count)
    pieces = []
    for first_row in range(0, row_count, block_size):
        last_row = first_row + block_size
        attend = jax.checkpoint(partial(attend_block, first_row=first_row))
        pieces.append(attend(queries[first_row:last_row], key_rows[:last_row], value_rows[:last_row], labels[first_row:last_row], labels[:last_row]))
    attention = low(low_back(jnp.concatenate(pieces, axis=0).reshape(row_count, D)))
    mixed_out = low_back(jnp.dot(attention, output_weight, precision=HIGH)) + output_bias
    gate_one = jax.nn.sigmoid(low_back(jnp.dot(norm_one, gate_weight, precision=HIGH)) + gate_bias)
    y_one = gate_one * mixed_out + (1.0 - gate_one) * block_rows
    norm_two = low(layer_norm(y_one, second_gain, second_shift))
    hidden = low(gelu_tanh(low_back(jnp.dot(norm_two, up_weight, precision=HIGH)) + up_bias))
    ffn_out = low_back(jnp.dot(hidden, down_weight, precision=HIGH)) + down_bias
    gate_two = jax.nn.sigmoid(low_back(jnp.dot(norm_two, pass_weight, precision=HIGH)) + pass_bias)
    result = gate_two * ffn_out + (1.0 - gate_two) * y_one
    return result * live_rows[:, None]

def reference(tokens, norm_gain, norm_shift, heads_weight, output_weight, output_bias, gate_weight, gate_bias, second_gain, second_shift, up_weight, up_bias, down_weight, down_bias, pass_weight, pass_bias, lengths, owners, cotangent):
    params = tuple((item.astype(jnp.float32) for item in (norm_gain, norm_shift, heads_weight, output_weight, output_bias, gate_weight, gate_bias, second_gain, second_shift, up_weight, up_bias, down_weight, down_bias, pass_weight, pass_bias)))
    blocks = tokens.astype(jnp.float32).reshape(N_DP, TOK_DEV, D)
    upstream = cotangent.astype(jnp.float32).reshape(N_DP, TOK_DEV, D)

    def one_block(totals, inputs):
        block_rows, block_cot, device = inputs
        labels, live_rows = layout(lengths, owners, device, TOK_DEV)
        live_float = live_rows.astype(jnp.float32)

        def apply_layer(values, weights):
            return forward(values, weights, labels, live_float)
        result, pull_back = jax.vjp(apply_layer, block_rows, params)
        rows_grad, params_grad = pull_back(block_cot)
        totals = jax.tree.map(lambda left, right: left + right, totals, params_grad)
        return (totals, (result.astype(jnp.bfloat16), rows_grad.astype(jnp.bfloat16)))
    zeros = jax.tree.map(jnp.zeros_like, params)
    totals, (outputs, row_grads) = lax.scan(one_block, zeros, (blocks, upstream, jnp.arange(N_DP, dtype=jnp.int32)))
    return (outputs.reshape(TOKENS, D), row_grads.reshape(TOKENS, D), totals[0], totals[1], totals[2], totals[3], totals[4], totals[5], totals[6], totals[7], totals[8], totals[9], totals[10], totals[11], totals[12], totals[13], totals[14])
```

```python
import functools

import jax
import jax.numpy as jnp
from jax import lax
from jax.experimental import pallas as pl
from jax.experimental.pallas import tpu as pltpu
from jax.sharding import PartitionSpec as P

HD = 64
EPS = 1e-05
NEGATIVE = -1e30
GELU_C = 0.7978845608028654
F32 = jnp.float32
BF16 = jnp.bfloat16
VMEM = pl.BlockSpec(memory_space=pltpu.VMEM)
SMEM = pl.BlockSpec(memory_space=pltpu.SMEM)
PARAMS = pltpu.CompilerParams(vmem_limit_bytes=48 << 20)
PARTS = 8


def dot(left, right, left_dim=1, right_dim=0):
    return lax.dot_general(
        left, right, (((left_dim,), (right_dim,)), ((), ())), preferred_element_type=F32
    )


def column_sum(values):
    return jnp.sum(values, axis=0, keepdims=True)


def row_mean(values):
    return jnp.mean(values, axis=-1, keepdims=True)


def normalized(values):
    centred = values - row_mean(values)
    scale = lax.rsqrt(row_mean(centred * centred) + EPS)
    return centred * scale, scale


def place(index, size):
    return pl.multiple_of(index * size, size)


def start_of(row, first, total):
    return jnp.where(row < first, 0, jnp.where(row < total, first, row))


def call(body, name, operands, outs, scratch=(), scalars=1):
    return pl.pallas_call(
        body,
        out_shape=outs,
        in_specs=[SMEM] * scalars + [VMEM] * (len(operands) - scalars),
        out_specs=[VMEM] * len(outs),
        scratch_shapes=list(scratch),
        compiler_params=PARAMS,
        name=name,
    )(*operands)


def shape(*dims, dtype=BF16):
    return jax.ShapeDtypeStruct(dims, dtype)


def attend_forward(
    info, t0, t1, t2, t3, gain, shift, weights,
    unit_out, q_out, k_out, v_out, qt_out, kt_out, ot_out, lse_out, a0, a1, a2, a3,
    vt, acc, top_row, sum_row,
):
    me, first, total = info[0], info[1], info[2]
    rows = t0.shape[0]
    block = rows
    for k, tok in enumerate((t0, t1, t2, t3)):
        at = place(me ^ k, rows)
        unit, _ = normalized(tok[...].astype(F32))
        unit_out[pl.ds(at, rows), :] = unit.astype(BF16)
        normed = (unit * gain[...] + shift[...]).astype(BF16)
        q = dot(normed, weights[0]).astype(BF16)
        key = dot(normed, weights[1]).astype(BF16)
        v = dot(normed, weights[2]).astype(BF16)
        q_out[pl.ds(at, rows), :] = q
        k_out[pl.ds(at, rows), :] = key
        v_out[pl.ds(at, rows), :] = v
        qt_out[:, pl.ds(at, rows)] = q.T
        kt_out[:, pl.ds(at, rows)] = key.T
        vt[:, pl.ds(at, rows)] = v.T
    width = q_out.shape[1]
    heads = width // HD
    head = lax.broadcasted_iota(jnp.int32, (width, block), 0) // HD
    for i in range(4):
        base = i * block
        scaled = qt_out[:, base : base + block] * BF16(0.125)
        q_heads = [jnp.where(head == h, scaled, BF16(0)) for h in range(heads)]
        row = base + lax.broadcasted_iota(jnp.int32, (1, block), 1)
        start = start_of(row, first, total)

        def step(at, begin, masked, q_heads=q_heads, row=row, start=start):
            keys = k_out[pl.ds(at, block), :]
            for h in range(heads):
                part = slice(HD * h, HD * h + HD)
                scores = dot(keys, q_heads[h])
                if masked:
                    col = at + lax.broadcasted_iota(jnp.int32, (block, block), 0)
                    scores = jnp.where((col >= start) & (col <= row), scores, NEGATIVE)
                top = jnp.max(scores, axis=0, keepdims=True)
                if not begin:
                    before = top_row[h : h + 1, :]
                    top = jnp.maximum(before, top)
                    fade = jnp.exp(before - top)
                exponent = jnp.exp(scores - top)
                summed = column_sum(exponent)
                mixed = dot(vt[part, pl.ds(at, block)], exponent.astype(BF16))
                if begin:
                    sum_row[h : h + 1, :] = summed
                    acc[part, :] = mixed
                else:
                    sum_row[h : h + 1, :] = sum_row[h : h + 1, :] * fade + summed
                    acc[part, :] = acc[part, :] * fade + mixed
                top_row[h : h + 1, :] = top

        step(base, True, True)
        if i:
            last_start = start_of(base + block - 1, first, total)

            def loop(j, carry, step=step, last_start=last_start):
                at = place(j, block)

                @pl.when(at >= last_start)
                def _():
                    step(at, False, False)

                @pl.when(at < last_start)
                def _():
                    step(at, False, True)

                return carry

            lax.fori_loop(start_of(base, first, total) // block, i, loop, 0)
        for h in range(heads):
            part = slice(HD * h, HD * h + HD)
            ot_out[part, base : base + block] = acc[part, :] / sum_row[h : h + 1, :]
            lse_out[h : h + 1, base : base + block] = top_row[h : h + 1, :] + jnp.log(
                sum_row[h : h + 1, :]
            )
    for k, out in enumerate((a0, a1, a2, a3)):
        at = place(me ^ k, rows)
        out[...] = ot_out[:, pl.ds(at, rows)].T.astype(BF16)


def middle(
    info, p0, p1, p2, p3, tok, cot, w0, w1, w2, w3, gain, shift, gate_w, gate_b, out_b,
    gain2, shift2, pass_w, pass_b, down_b,
    out, g0, g1, g2, g3, hid, pre_low, ffn_low, z2_low, n2_out, z1_low, mixed_low, carry, vec,
    slope,
):
    me, total = info[0], info[2]
    rows, width = tok.shape
    packs = (w0, w1, w2, w3)
    up = [w.at[0:width] for w in packs]
    down = [w.at[width : 2 * width] for w in packs]
    heads = p0.shape[1]
    proj = [w.at[2 * width : 2 * width + heads] for w in packs]
    bias = [w.at[2 * width + heads : 2 * width + heads + 16] for w in packs]
    live = (
        (me * rows + lax.broadcasted_iota(jnp.int32, (rows, 1), 0)) < total
    ).astype(F32)
    x = tok[...].astype(F32)
    unit, _ = normalized(x)
    n1 = (unit * gain[...] + shift[...]).astype(BF16)
    mixed = out_b[...]
    for p, w in zip((p0, p1, p2, p3), proj):
        mixed = mixed + dot(p[...], w[...])
    gate = jax.nn.sigmoid(dot(n1, gate_w[...]) + gate_b[...])
    y = gate * mixed + (1.0 - gate) * x
    unit2, scale2 = normalized(y)
    n2 = (unit2 * gain2[...] + shift2[...]).astype(BF16)
    n2_out[...] = n2
    gate2 = jax.nn.sigmoid(dot(n2, pass_w[...]) + pass_b[...])
    ffn = down_b[...]
    for k in range(4):
        pre = dot(n2, up[k][...]) + bias[k][0:1, :].astype(F32)
        square = pre * pre
        th = jnp.tanh(GELU_C * pre * (1.0 + 0.044715 * square))
        half = 0.5 * (1.0 + th)
        hidden = (pre * half).astype(BF16)
        slope[k] = half + 0.5 * GELU_C * pre * (1.0 - th * th) * (1.0 + 0.134145 * square)
        hid[k] = hidden
        ffn = ffn + dot(hidden, down[k][...])
    out[...] = ((gate2 * ffn + (1.0 - gate2) * y) * live).astype(BF16)
    gy = cot[...].astype(F32) * live
    gf = gy * gate2
    gf_low = gf.astype(BF16)
    ffn_low[...] = gf_low
    vec[0:1, :] = column_sum(gf)
    z2 = gf * (ffn - y) * (1.0 - gate2)
    vec[1:2, :] = column_sum(z2)
    z2l = z2.astype(BF16)
    z2_low[...] = z2l
    gn2 = dot(z2l, pass_w[...], 1, 1)
    for k in range(4):
        g_pre = dot(gf_low, down[k][...], 1, 1) * slope[k]
        vec[pl.ds(8 + (me ^ k), 1), :] = column_sum(g_pre)
        low = g_pre.astype(BF16)
        pre_low[k] = low
        gn2 = gn2 + dot(low, up[k][...], 1, 1)
    vec[2:3, :] = column_sum(gn2)
    vec[3:4, :] = column_sum(gn2 * unit2)
    g = gn2 * gain2[...]
    gy1 = gy * (1.0 - gate2) + scale2 * (g - row_mean(g) - unit2 * row_mean(g * unit2))
    gm = gy1 * gate
    vec[4:5, :] = column_sum(gm)
    z1 = gm * (mixed - x) * (1.0 - gate)
    vec[5:6, :] = column_sum(z1)
    vec[6:8, :] = jnp.zeros((2, width), F32)
    vec[12:16, :] = jnp.zeros((4, width), F32)
    z1_low[...] = z1.astype(BF16)
    gml = gm.astype(BF16)
    mixed_low[...] = gml
    carry[...] = gy1 * (1.0 - gate)
    for g_out, w in zip((g0, g1, g2, g3), proj):
        g_out[...] = dot(gml, w[...], 1, 1).astype(BF16)


ORDER = [int(f"{p:03b}"[::-1], 2) for p in range(PARTS)]


def weight_grads(
    info, hid, pre_low, ffn_low, z2_low, n2, z1_low, mixed_low, tok, gain, shift, gate_w,
    p0, p1, p2, p3, vec_in,
    keep, send, local, vec,
):
    me, mine = info[0], info[3]
    width = tok.shape[1]
    heads = p0.shape[1]
    unit, _ = normalized(tok[...].astype(F32))
    n1 = (unit * gain[...] + shift[...]).astype(BF16)
    z1l = z1_low[...]
    step = width // PARTS
    small = heads // PARTS
    rows_a = step + small
    rows_b = step + 2 * small
    first_b = 2 * PARTS * rows_a
    n2_turned = n2[...].T
    n1_turned = n1.T
    z2l = z2_low[...]

    def put_a(k, big, little):
        buf = (keep, send)[k % 2]
        base = (k // 2) * PARTS * rows_a
        for p in range(PARTS):
            pos = reverse(p ^ mine)
            at = pl.multiple_of(base + pos * rows_a, 16)
            buf[pl.ds(at, step), :] = big[p * step : (p + 1) * step].astype(BF16)
            buf[pl.ds(pl.multiple_of(at + step, 16), small), :] = little[
                p * small : (p + 1) * small
            ].astype(BF16)

    def put_b(k, big, one, two):
        buf = (keep, send)[k % 2]
        for p in range(PARTS):
            pos = reverse(p ^ mine)
            half, inner = pos // (PARTS // 2), pos % (PARTS // 2)
            at = first_b + ((half * 2 + k // 2) * (PARTS // 2) + inner) * rows_b
            at = pl.multiple_of(at, 16)
            buf[pl.ds(at, step), :] = big[p * step : (p + 1) * step].astype(BF16)
            buf[pl.ds(pl.multiple_of(at + step, 16), small), :] = one[
                p * small : (p + 1) * small
            ].astype(BF16)
            buf[pl.ds(pl.multiple_of(at + step + small, 16), small), :] = two[
                p * small : (p + 1) * small
            ].astype(BF16)

    gml = mixed_low[...]
    gfl = ffn_low[...]
    pieces = (p0, p1, p2, p3)
    gate_grad = dot(n1_turned, z1l)
    pass_grad = dot(n2_turned, z2l)
    scratch_gate, scratch_pass = local.at[1], local.at[2]
    scratch_gate[...] = gate_grad
    scratch_pass[...] = pass_grad
    for k in range(4):
        down_grad = dot(hid[k], gfl, 0, 0)
        out_grad = dot(pieces[k][...], gml, 0, 0)
        put_a(k, down_grad, out_grad)
        up_grad = dot(n2_turned, pre_low[k])
        at = place(me ^ k, heads)
        put_b(k, up_grad, scratch_gate[pl.ds(at, heads), :], scratch_pass[pl.ds(at, heads), :])
    dz = dot(z1l, gate_w[...], 1, 1)
    local[0] = dz
    vec[...] = vec_in[...]
    vec[6:7, :] = column_sum(dz * unit)
    vec[7:8, :] = column_sum(dz)


def reverse(part):
    return ((part & 1) << 2) | (part & 2) | ((part >> 2) & 1)


def attend_backward(
    info, q, k, v, qt, kt, ot, lse, g0, g1, g2, g3, unit_low, weights, gain, shift, vec_in,
    heads_out, keep, send,
    up, upt, dqt, dk, dv, dots, moment, total_cols,
):
    me, first, total, mine = info[0], info[1], info[2], info[3]
    rows = g0.shape[0]
    block = rows
    width = q.shape[1]
    heads = width // HD
    for n, g in enumerate((g0, g1, g2, g3)):
        at = place(me ^ n, rows)
        up[pl.ds(at, rows), :] = g[...]
        upt[:, pl.ds(at, rows)] = g[...].T
    weighted = upt[...].astype(F32) * ot[...]
    for h in range(heads):
        dots[h : h + 1, :] = column_sum(weighted[HD * h : HD * h + HD])
    dqt[...] = jnp.zeros_like(dqt)
    moment[...] = jnp.zeros_like(moment)
    total_cols[...] = jnp.zeros_like(total_cols)
    lane_head = lax.broadcasted_iota(jnp.int32, (block, width), 1) // HD
    row_head = lax.broadcasted_iota(jnp.int32, (width, block), 0) // HD
    for j in range(4):
        at_k = j * block
        keys = k[at_k : at_k + block, :]
        values = v[at_k : at_k + block, :]
        dk[...] = jnp.zeros_like(dk)
        dv[...] = jnp.zeros_like(dv)

        def step(at, masked, keys=keys, values=values, at_k=at_k):
            cols = pl.ds(at, block)
            scaled_t = qt[:, cols] * BF16(0.125)
            scaled = q[pl.ds(at, block), :] * BF16(0.125)
            ups = up[pl.ds(at, block), :]
            ups_t = upt[:, cols]
            for h in range(heads):
                part = slice(HD * h, HD * h + HD)
                scores = dot(keys, jnp.where(row_head == h, scaled_t, BF16(0)))
                probs = jnp.exp(scores - lse[h : h + 1, cols])
                if masked:
                    row = at + lax.broadcasted_iota(jnp.int32, (1, block), 1)
                    start = start_of(row, first, total)
                    col = at_k + lax.broadcasted_iota(jnp.int32, (block, block), 0)
                    probs = jnp.where((col >= start) & (col <= row), probs, 0.0)
                grads = dot(values, jnp.where(row_head == h, ups_t, BF16(0)))
                score_grad = (probs * (grads - dots[h : h + 1, cols])).astype(BF16)
                dv[...] += dot(probs.astype(BF16), jnp.where(lane_head == h, ups, BF16(0)))
                dk[...] += dot(score_grad, jnp.where(lane_head == h, scaled, BF16(0)))
                dqt[part, cols] += dot(kt[part, at_k : at_k + block], score_grad)

        step(at_k, True)
        if j < 3:

            def loop(i, carry, step=step, at_k=at_k):
                at = place(i, block)
                begin = start_of(at, first, total)
                last_start = start_of(at + block - 1, first, total)

                @pl.when(at_k >= last_start)
                def _():
                    step(at, False)

                @pl.when((at_k < last_start) & (at_k + block > begin))
                def _():
                    step(at, True)

                return carry

            lax.fori_loop(j + 1, 4, loop, 0)
        grads_t = (
            (dqt[:, at_k : at_k + block] * 0.125).astype(BF16),
            dk[...].T.astype(BF16),
            dv[...].T.astype(BF16),
        )
        unit_rows = unit_low[at_k : at_k + block, :]
        spread = 0.0
        for c in range(3):
            spread = spread + dot(grads_t[c], weights[c], 0, 1)
            moment[c] += dot(grads_t[c], unit_rows)
            total_cols[c] += jnp.sum(grads_t[c].astype(F32), axis=1, keepdims=True)
        spread = spread.astype(BF16)
        which = me ^ j
        at_row = place(which // 2, rows)

        @pl.when(which % 2 == 0)
        def _(spread=spread, at_row=at_row):
            keep[pl.ds(at_row, rows), :] = spread

        @pl.when(which % 2 == 1)
        def _(spread=spread, at_row=at_row):
            send[pl.ds(at_row, rows), :] = spread

    step_rows = unit_low.shape[1] // PARTS
    part_rows = 3 * step_rows + 16
    gain_grad = 0.0
    shift_grad = 0.0
    for c in range(3):
        turned = weights[c].astype(F32).T
        gain_grad = gain_grad + column_sum(turned * moment[c])
        shift_grad = shift_grad + column_sum(turned * total_cols[c])
        grad = (moment[c] * gain[...] + total_cols[c] * shift[...]).T.astype(BF16)
        for p in range(PARTS):
            at = pl.multiple_of(reverse(p ^ mine) * part_rows + c * step_rows, 16)
            heads_out[pl.ds(at, step_rows), :] = grad[p * step_rows : (p + 1) * step_rows]
    pick = lax.broadcasted_iota(jnp.int32, vec_in.shape, 0)
    sums = vec_in[...] + jnp.where(pick == 6, gain_grad, 0.0) + jnp.where(pick == 7, shift_grad, 0.0)
    pieces = sums.shape[1] // width
    for p in range(PARTS):
        at = pl.multiple_of(reverse(p ^ mine) * part_rows + 3 * step_rows, 16)
        value = sums[:, p * width : (p + 1) * width] if p < pieces else jnp.zeros((16, width), F32)
        heads_out[pl.ds(at, 16), :] = value.astype(BF16)


def tokens_backward(tok, own, got, local, carry, gain, out):
    unit, scale = normalized(tok[...].astype(F32))
    grad = own[...].astype(F32) + got[...].astype(F32) + local[0]
    h = grad * gain[...]
    out[...] = (
        carry[...] + scale * (h - row_mean(h) - unit * row_mean(h * unit))
    ).astype(BF16)


def each_part(info, refs, rows):
    pos = 0
    for ref in refs:
        for n in range(ref.shape[0] // rows):
            yield ORDER[pos] ^ info[3], ref, n * rows
            pos += 1


def unpack_down(info, s0, s1, s2, s3, down, out):
    step, small = down.shape[0] // PARTS, out.shape[0] // PARTS
    for p, ref, at in each_part(info, (s0, s1, s2, s3), step + small):
        down[pl.ds(place(p, step), step), :] = ref[at : at + step].astype(F32)
        out[pl.ds(place(p, small), small), :] = ref[at + step : at + step + small].astype(F32)


def unpack_up(info, s0, s1, s2, s3, up, gates):
    step, small = up.shape[0] // PARTS, gates.shape[0] // (2 * PARTS)
    for p, ref, at in each_part(info, (s0, s1, s2, s3), step + 2 * small):
        up[pl.ds(place(p, step), step), :] = ref[at : at + step].astype(F32)
        middle_at = at + step + small
        gates[pl.ds(place(p, small), small), :] = ref[at + step : middle_at]
        gates[pl.ds(pl.multiple_of((PARTS + p) * small, small), small), :] = ref[
            middle_at : middle_at + small
        ]


def unpack_heads(info, s0, s1, s2, s3, heads, vec):
    step = heads.shape[1] // PARTS
    for p, ref, at in each_part(info, (s0, s1, s2, s3), 3 * step + 16):
        for c in range(3):
            heads[c, pl.ds(place(p, step), step), :] = ref[at + c * step : at + (c + 1) * step].astype(F32)
        vec[pl.ds(place(p, 16), 16), :] = ref[at + 3 * step : at + 3 * step + 16].astype(F32)


def unpack_gates(info, s0, s1, s2, s3, gate, passed):
    rows = gate.shape[0] // 4
    for k, ref in enumerate((s0, s1, s2, s3)):
        at = place(info[0] ^ k, rows)
        gate[pl.ds(at, rows), :] = ref[0:rows].astype(F32)
        passed[pl.ds(at, rows), :] = ref[rows : 2 * rows].astype(F32)


def unpack_vectors(info, one, two, *outs):
    width = one.shape[1]
    sums = one[...] + two[...]
    for p in range(sums.shape[0] // 16):
        piece = sums[16 * p : 16 * p + 16]
        for n in range(8):
            outs[n][:, p * width : (p + 1) * width] = piece[n : n + 1]
        pick = lax.broadcasted_iota(jnp.int32, piece.shape, 0) == 8 + info[0]
        outs[8][:, p * width : (p + 1) * width] = column_sum(jnp.where(pick, piece, 0.0))


def swap_tensor(values, mask):
    return lax.ppermute(values, "tensor", [(i, i ^ mask) for i in range(4)])


def swap_dp(values, mask):
    return lax.ppermute(values, "dp", [(i, i ^ mask) for i in range(lax.axis_size("dp"))])


def fold(values, got):
    return (values.astype(F32) + got.astype(F32)).astype(BF16)


def scatter_dp(values, mask):
    half = values.shape[0] // 2
    got = swap_dp(values[half:], mask)
    return fold(values[:half], got)


def spread_rest(values):
    mask = PARTS
    while mask < lax.axis_size("dp"):
        values = fold(values, swap_dp(values, mask))
        mask *= 2
    return values


def gather_dp(values):
    s1 = swap_dp(values, 4)
    s2 = swap_dp(jnp.concatenate([values, s1]), 2)
    s3 = swap_dp(jnp.concatenate([values, s1, s2]), 1)
    return (values, s1, s2, s3)


def body(
    tokens,
    norm_gain,
    norm_shift,
    heads_weight,
    output_weight,
    output_bias,
    gate_weight,
    gate_bias,
    second_gain,
    second_shift,
    up_weight,
    up_bias,
    down_weight,
    down_bias,
    pass_weight,
    pass_bias,
    lengths,
    owners,
    cotangent,
):
    rows, width = tokens.shape
    total_rows = 4 * rows
    head_width = heads_weight.shape[2]
    me = lax.axis_index("tensor")
    dp = lax.axis_index("dp")
    entries = jnp.arange(lengths.shape[0], dtype=jnp.int32)
    owned = owners == dp
    own_lengths = jnp.where(owned, lengths, 0)
    first_entry = jnp.min(jnp.where(owned, entries, lengths.shape[0]))
    first = jnp.sum(jnp.where(entries == first_entry, own_lengths, 0))
    info = jnp.stack([me, first, jnp.sum(own_lengths), dp % PARTS]).astype(jnp.int32)
    row = lambda v: v.reshape(1, -1)
    gain, shift = row(norm_gain), row(norm_shift)
    split_heads = heads_weight.transpose(1, 0, 2)

    tok2 = swap_tensor(tokens, 2)
    tok1 = swap_tensor(tokens, 1)
    tok3 = swap_tensor(tok2, 1)
    bias_rows = jnp.broadcast_to(up_bias[None, :], (16, width))
    pack0 = jnp.concatenate([up_weight, down_weight, output_weight, bias_rows])
    pack1 = swap_tensor(pack0, 1)
    held, tok3 = lax.optimization_barrier((pack0, tok3))
    pack2 = swap_tensor(held, 2)
    pack3 = swap_tensor(pack2, 1)

    unit, q, key, v, qt, kt, ot, lse, a0, a1, a2, a3 = call(
        attend_forward,
        "attend_forward",
        (info, tokens, tok1, tok2, tok3, gain, shift, split_heads),
        [shape(total_rows, width)]
        + [shape(total_rows, head_width)] * 3
        + [shape(head_width, total_rows)] * 2
        + [shape(head_width, total_rows, dtype=F32), shape(head_width // HD, total_rows, dtype=F32)]
        + [shape(rows, head_width)] * 4,
        [
            pltpu.VMEM((head_width, total_rows), BF16),
            pltpu.VMEM((head_width, rows), F32),
            pltpu.VMEM((8, rows), F32),
            pltpu.VMEM((8, rows), F32),
        ],
    )
    p0, p1, p2, p3 = a0, swap_tensor(a1, 1), swap_tensor(a2, 2), swap_tensor(a3, 3)
    square = shape(rows, width)
    hidden_shape = shape(4, rows, width)
    output, g0, g1, g2, g3, hid, pre_low, ffn_low, z2_low, n2, z1_low, mixed_low, carry, vec = call(
        middle,
        "middle",
        (info, p0, p1, p2, p3, tokens, cotangent, pack0, pack1, pack2, pack3, gain, shift)
        + (gate_weight, row(gate_bias), row(output_bias), row(second_gain), row(second_shift))
        + (pass_weight, row(pass_bias), row(down_bias)),
        [square]
        + [shape(rows, head_width)] * 4
        + [hidden_shape, hidden_shape]
        + [square] * 5
        + [shape(rows, width, dtype=F32), shape(16, width, dtype=F32)],
        [pltpu.VMEM((4, rows, width), F32)],
    )
    g1, g2, g3 = swap_tensor(g1, 1), swap_tensor(g2, 2), swap_tensor(g3, 3)
    rows_a = width + head_width
    rows_b = width + 2 * head_width
    keep, send, local, vec = call(
        weight_grads,
        "weight_grads",
        (info, hid, pre_low, ffn_low, z2_low, n2, z1_low, mixed_low, tokens, gain, shift)
        + (gate_weight, p0, p1, p2, p3, vec),
        [shape(2 * (rows_a + rows_b), width)] * 2
        + [shape(3, rows, width, dtype=F32), shape(16, width, dtype=F32)],
    )
    got = swap_tensor(send, 1)
    part_a = 2 * rows_a
    a_keep = fold(keep[:rows_a], got[:rows_a])
    a_send = fold(keep[rows_a:part_a], got[rows_a:part_a])
    b_keep = fold(keep[part_a : part_a + rows_b], got[part_a : part_a + rows_b])
    b_send = fold(keep[part_a + rows_b :], got[part_a + rows_b :])
    part = fold(a_keep, swap_tensor(a_send, 2))
    for mask in (1, 2, 4):
        part = scatter_dp(part, mask)
    down_grad, out_grad = call(
        unpack_down,
        "unpack_down",
        (info,) + gather_dp(spread_rest(part)),
        [shape(width, width, dtype=F32), shape(head_width, width, dtype=F32)],
    )
    part = fold(b_keep, swap_dp(b_send, 1))
    half = part.shape[0] // 2
    part = fold(part[:half], swap_tensor(part[half:], 2))
    for mask in (2, 4):
        part = scatter_dp(part, mask)
    up_grad, gates0 = call(
        unpack_up,
        "unpack_up",
        (info,) + gather_dp(spread_rest(part)),
        [shape(width, width, dtype=F32), shape(2 * head_width, width)],
    )
    gates2 = swap_tensor(gates0, 2)
    gates1 = swap_tensor(gates0, 1)
    gates3 = swap_tensor(gates2, 1)
    gate_grad, pass_grad = call(
        unpack_gates,
        "unpack_gates",
        (info, gates0, gates1, gates2, gates3),
        [shape(width, width, dtype=F32)] * 2,
    )

    part_rows = 3 * (width // PARTS) + 16
    heads_sum, rows_keep, rows_send = call(
        attend_backward,
        "attend_backward",
        (info, q, key, v, qt, kt, ot, lse, g0, g1, g2, g3, unit, split_heads, gain, shift, vec),
        [shape(PARTS * part_rows, head_width)] + [shape(2 * rows, width)] * 2,
        [
            pltpu.VMEM((total_rows, head_width), BF16),
            pltpu.VMEM((head_width, total_rows), BF16),
            pltpu.VMEM((head_width, total_rows), F32),
            pltpu.VMEM((rows, head_width), F32),
            pltpu.VMEM((rows, head_width), F32),
            pltpu.VMEM((8, total_rows), F32),
            pltpu.VMEM((3, head_width, width), F32),
            pltpu.VMEM((3, head_width, 1), F32),
        ],
    )
    rows_got = swap_tensor(rows_send, 1)
    far = swap_tensor(fold(rows_keep[rows:], rows_got[rows:]), 2)
    near = fold(rows_keep[:rows], rows_got[:rows])
    for mask in (1, 2, 4):
        heads_sum = scatter_dp(heads_sum, mask)
    (tokens_grad,) = call(
        tokens_backward,
        "tokens_backward",
        (tokens, near, far, local, carry, gain),
        [square],
        scalars=0,
    )
    heads_grad, vec = call(
        unpack_heads,
        "unpack_heads",
        (info,) + gather_dp(spread_rest(heads_sum)),
        [shape(3, width, head_width, dtype=F32), shape(PARTS * 16, head_width, dtype=F32)],
    )
    vec = vec[: 16 * (width // head_width)]
    vec = vec + swap_tensor(vec, 1)
    vectors = call(
        unpack_vectors,
        "unpack_vectors",
        (info, vec, swap_tensor(vec, 2)),
        [shape(1, width, dtype=F32)] * 9,
    )
    (
        down_bias_grad,
        pass_bias_grad,
        second_shift_grad,
        second_gain_grad,
        output_bias_grad,
        gate_bias_grad,
        norm_gain_grad,
        norm_shift_grad,
        up_bias_grad,
    ) = [v.reshape(width) for v in vectors]
    return (
        output,
        tokens_grad,
        norm_gain_grad,
        norm_shift_grad,
        heads_grad.transpose(1, 0, 2),
        out_grad,
        output_bias_grad,
        gate_grad,
        gate_bias_grad,
        second_gain_grad,
        second_shift_grad,
        up_grad,
        up_bias_grad,
        down_grad,
        down_bias_grad,
        pass_grad,
        pass_bias_grad,
    )


def solution(mesh):
    placed = (
        P(("dp", "tensor"), None),
        P(),
        P(),
        P(None, None, "tensor"),
        P("tensor", None),
        P(),
        P(),
        P(),
        P(),
        P(),
        P(None, "tensor"),
        P("tensor"),
        P("tensor", None),
        P(),
        P(),
        P(),
        P(),
        P(),
        P(("dp", "tensor"), None),
    )
    return jax.shard_map(
        body,
        mesh=mesh,
        in_specs=placed,
        out_specs=(
            P(("dp", "tensor"), None),
            P(("dp", "tensor"), None),
            P(),
            P(),
            P(None, None, "tensor"),
            P("tensor", None),
            P(),
            P(),
            P(),
            P(),
            P(),
            P(None, "tensor"),
            P("tensor"),
            P("tensor", None),
            P(),
            P(),
            P(),
        ),
        check_vma=False,
    )
```

```python
import functools

import jax
import jax.numpy as jnp
from jax import lax
from jax.experimental import pallas as pl
from jax.experimental.pallas import tpu as pltpu
from jax.sharding import PartitionSpec as P

HD = 64
EPS = 1e-05
NEGATIVE = -1e30
GELU_C = 0.7978845608028654
F32 = jnp.float32
BF16 = jnp.bfloat16
VMEM = pl.BlockSpec(memory_space=pltpu.VMEM)
SMEM = pl.BlockSpec(memory_space=pltpu.SMEM)
PARTS = 8


def dot(left, right, left_dim=1, right_dim=0):
    return lax.dot_general(
        left, right, (((left_dim,), (right_dim,)), ((), ())), preferred_element_type=F32
    )


def column_sum(values):
    return jnp.sum(values, axis=0, keepdims=True)


def row_mean(values):
    return jnp.mean(values, axis=-1, keepdims=True)


def normalized(values):
    centred = values - row_mean(values)
    scale = lax.rsqrt(row_mean(centred * centred) + EPS)
    return centred * scale, scale


def place(index, size):
    return pl.multiple_of(index * size, size)


def start_of(row, first, total):
    return jnp.where(row < first, 0, jnp.where(row < total, first, row))


def call(body, name, operands, outs, scratch=(), scalars=1, micros=2, mib=12):
    return pl.pallas_call(
        body,
        cost_estimate=pl.CostEstimate(flops=int(micros * 1.1e9), bytes_accessed=0, transcendentals=0),
        out_shape=outs,
        in_specs=[SMEM] * scalars + [VMEM] * (len(operands) - scalars),
        out_specs=[VMEM] * len(outs),
        scratch_shapes=list(scratch),
        compiler_params=pltpu.CompilerParams(vmem_limit_bytes=mib << 20),
        name=name,
    )(*operands)


def shape(*dims, dtype=BF16):
    return jax.ShapeDtypeStruct(dims, dtype)


def attend_forward(
    info, t0, t1, t2, t3, params, weights,
    unit_out, q_out, k_out, v_out, qt_out, kt_out, ot_out, lse_out, a0, a1, a2, a3,
    vt, acc, top_row, sum_row,
):
    me, first, total = info[0], info[1], info[2]
    gain, shift = params[0:1, :], params[1:2, :]
    rows = t0.shape[0]
    block = rows
    for k, tok in enumerate((t0, t1, t2, t3)):
        at = place(me ^ k, rows)
        unit, _ = normalized(tok[...].astype(F32))
        unit_out[pl.ds(at, rows), :] = unit.astype(BF16)
        normed = (unit * gain + shift).astype(BF16)
        q = dot(normed, weights[0]).astype(BF16)
        key = dot(normed, weights[1]).astype(BF16)
        v = dot(normed, weights[2]).astype(BF16)
        q_out[pl.ds(at, rows), :] = q
        k_out[pl.ds(at, rows), :] = key
        v_out[pl.ds(at, rows), :] = v
        qt_out[:, pl.ds(at, rows)] = q.T
        kt_out[:, pl.ds(at, rows)] = key.T
        vt[:, pl.ds(at, rows)] = v.T
    width = q_out.shape[1]
    heads = width // HD
    head = lax.broadcasted_iota(jnp.int32, (width, block), 0) // HD

    def query_block(i, unused):
        base = place(i, block)
        scaled = qt_out[:, pl.ds(base, block)] * BF16(0.125)
        q_heads = [jnp.where(head == h, scaled, BF16(0)) for h in range(heads)]
        row = base + lax.broadcasted_iota(jnp.int32, (1, block), 1)
        start = start_of(row, first, total)
        last_start = start_of(base + block - 1, first, total)
        acc[...] = jnp.zeros_like(acc)
        sum_row[...] = jnp.zeros_like(sum_row)
        top_row[...] = jnp.full_like(top_row, NEGATIVE)

        def step(at, masked):
            keys = k_out[pl.ds(at, block), :]
            for h in range(heads):
                part = slice(HD * h, HD * h + HD)
                scores = dot(keys, q_heads[h])
                if masked:
                    col = at + lax.broadcasted_iota(jnp.int32, (block, block), 0)
                    scores = jnp.where((col >= start) & (col <= row), scores, NEGATIVE)
                before = top_row[h : h + 1, :]
                top = jnp.maximum(before, jnp.max(scores, axis=0, keepdims=True))
                fade = jnp.exp(before - top)
                exponent = jnp.exp(scores - top)
                mixed = dot(vt[part, pl.ds(at, block)], exponent.astype(BF16))
                sum_row[h : h + 1, :] = sum_row[h : h + 1, :] * fade + column_sum(exponent)
                acc[part, :] = acc[part, :] * fade + mixed
                top_row[h : h + 1, :] = top

        def loop(n, carry):
            at = place(i - n, block)
            masked = (n == 0) | (at < last_start)

            @pl.when(masked)
            def _():
                step(at, True)

            @pl.when(jnp.logical_not(masked))
            def _():
                step(at, False)

            return carry

        lax.fori_loop(0, i + 1 - start_of(base, first, total) // block, loop, 0)
        for h in range(heads):
            part = slice(HD * h, HD * h + HD)
            summed = sum_row[h : h + 1, :]
            ot_out[part, pl.ds(base, block)] = acc[part, :] / summed
            lse_out[h : h + 1, pl.ds(base, block)] = top_row[h : h + 1, :] + jnp.log(summed)
        return unused

    lax.fori_loop(0, 4, query_block, 0)
    for k, out in enumerate((a0, a1, a2, a3)):
        at = place(me ^ k, rows)
        out[...] = ot_out[:, pl.ds(at, rows)].T.astype(BF16)


def middle(
    info, p0, p1, p2, p3, tok, cot, w0, w1, w2, w3, params, gate_w, pass_w,
    out, g0, g1, g2, g3, hid, pre_low, ffn_low, z2_low, n2_out, z1_low, mixed_low, carry, vec,
    slope,
):
    me, total = info[0], info[2]
    gain, shift, out_b, gate_b, gain2, shift2, down_b, pass_b = [
        params[n : n + 1, :] for n in range(8)
    ]
    rows, width = tok.shape
    packs = (w0, w1, w2, w3)
    up = [w.at[0:width] for w in packs]
    down = [w.at[width : 2 * width] for w in packs]
    heads = p0.shape[1]
    proj = [w.at[2 * width : 2 * width + heads] for w in packs]
    bias = [w.at[2 * width + heads : 2 * width + heads + 16] for w in packs]
    live = (
        (me * rows + lax.broadcasted_iota(jnp.int32, (rows, 1), 0)) < total
    ).astype(F32)
    x = tok[...].astype(F32)
    unit, _ = normalized(x)
    n1 = (unit * gain + shift).astype(BF16)
    mixed = out_b
    for p, w in zip((p0, p1, p2, p3), proj):
        mixed = mixed + dot(p[...], w[...])
    gate = jax.nn.sigmoid(dot(n1, gate_w[...]) + gate_b)
    y = gate * mixed + (1.0 - gate) * x
    unit2, scale2 = normalized(y)
    n2 = (unit2 * gain2 + shift2).astype(BF16)
    n2_out[...] = n2
    gate2 = jax.nn.sigmoid(dot(n2, pass_w[...]) + pass_b)
    ffn = down_b
    for k in range(4):
        pre = dot(n2, up[k][...]) + bias[k][0:1, :].astype(F32)
        square = pre * pre
        th = jnp.tanh(GELU_C * pre * (1.0 + 0.044715 * square))
        half = 0.5 * (1.0 + th)
        hidden = (pre * half).astype(BF16)
        slope[k] = half + 0.5 * GELU_C * pre * (1.0 - th * th) * (1.0 + 0.134145 * square)
        hid[k] = hidden
        ffn = ffn + dot(hidden, down[k][...])
    out[...] = ((gate2 * ffn + (1.0 - gate2) * y) * live).astype(BF16)
    gy = cot[...].astype(F32) * live
    gf = gy * gate2
    gf_low = gf.astype(BF16)
    ffn_low[...] = gf_low
    vec[0:1, :] = column_sum(gf)
    z2 = gf * (ffn - y) * (1.0 - gate2)
    vec[1:2, :] = column_sum(z2)
    z2l = z2.astype(BF16)
    z2_low[...] = z2l
    gn2 = dot(z2l, pass_w[...], 1, 1)
    for k in range(4):
        g_pre = dot(gf_low, down[k][...], 1, 1) * slope[k]
        vec[pl.ds(8 + (me ^ k), 1), :] = column_sum(g_pre)
        low = g_pre.astype(BF16)
        pre_low[k] = low
        gn2 = gn2 + dot(low, up[k][...], 1, 1)
    vec[2:3, :] = column_sum(gn2)
    vec[3:4, :] = column_sum(gn2 * unit2)
    g = gn2 * gain2
    gy1 = gy * (1.0 - gate2) + scale2 * (g - row_mean(g) - unit2 * row_mean(g * unit2))
    gm = gy1 * gate
    vec[4:5, :] = column_sum(gm)
    z1 = gm * (mixed - x) * (1.0 - gate)
    vec[5:6, :] = column_sum(z1)
    vec[6:8, :] = jnp.zeros((2, width), F32)
    vec[12:16, :] = jnp.zeros((4, width), F32)
    z1_low[...] = z1.astype(BF16)
    gml = gm.astype(BF16)
    mixed_low[...] = gml
    carry[...] = gy1 * (1.0 - gate)
    for g_out, w in zip((g0, g1, g2, g3), proj):
        g_out[...] = dot(gml, w[...], 1, 1).astype(BF16)


ORDER = [int(f"{p:03b}"[::-1], 2) for p in range(PARTS)]


def weight_grads(
    info, hid, pre_low, ffn_low, z2_low, n2, z1_low, mixed_low, tok, params, gate_w,
    p0, p1, p2, p3, vec_in,
    keep, send, local, vec,
    scratch_gate, scratch_pass,
):
    me, mine = info[0], info[3]
    gain, shift = params[0:1, :], params[1:2, :]
    width = tok.shape[1]
    heads = p0.shape[1]
    unit, _ = normalized(tok[...].astype(F32))
    n1 = (unit * gain + shift).astype(BF16)
    z1l = z1_low[...]
    step = width // PARTS
    small = heads // PARTS
    rows_a = step + 2 * small
    rows_b = step + small
    first_b = 2 * PARTS * rows_a
    n2_turned = n2[...].T
    n1_turned = n1.T
    z2l = z2_low[...]

    def put_a(k, big, one, two):
        buf = (keep, send)[k % 2]
        base = (k // 2) * PARTS * rows_a
        for p in range(PARTS):
            at = pl.multiple_of(base + reverse(p ^ mine) * rows_a, 16)
            buf[pl.ds(at, step), :] = big[p * step : (p + 1) * step].astype(BF16)
            at = pl.multiple_of(at + step, 16)
            buf[pl.ds(at, small), :] = one[p * small : (p + 1) * small].astype(BF16)
            at = pl.multiple_of(at + small, 16)
            buf[pl.ds(at, small), :] = two[p * small : (p + 1) * small].astype(BF16)

    def put_b(k, big, little):
        buf = (keep, send)[k % 2]
        for p in range(PARTS):
            pos = reverse(p ^ mine)
            half, inner = pos // (PARTS // 2), pos % (PARTS // 2)
            at = first_b + ((half * 2 + k // 2) * (PARTS // 2) + inner) * rows_b
            at = pl.multiple_of(at, 16)
            buf[pl.ds(at, step), :] = big[p * step : (p + 1) * step].astype(BF16)
            at = pl.multiple_of(at + step, 16)
            buf[pl.ds(at, small), :] = little[p * small : (p + 1) * small].astype(BF16)

    gml = mixed_low[...]
    ffn_turned = ffn_low[...].T
    pieces = (p0, p1, p2, p3)
    scratch_gate[...] = dot(n1_turned, z1l)
    scratch_pass[...] = dot(n2_turned, z2l)
    for k in range(4):
        down_grad = dot(ffn_turned, hid[k])
        at = place(me ^ k, heads)
        put_a(k, down_grad, scratch_gate[pl.ds(at, heads), :], scratch_pass[pl.ds(at, heads), :])
        up_grad = dot(n2_turned, pre_low[k])
        out_grad = dot(pieces[k][...], gml, 0, 0)
        put_b(k, up_grad, out_grad)
    dz = dot(z1l, gate_w[...], 1, 1)
    local[...] = dz
    vec[...] = vec_in[...]
    vec[6:7, :] = column_sum(dz * unit)
    vec[7:8, :] = column_sum(dz)


def reverse(part):
    return ((part & 1) << 2) | (part & 2) | ((part >> 2) & 1)


def attend_backward(
    info, q, k, v, qt, kt, ot, lse, g0, g1, g2, g3, unit_low, weights, params, vec_in,
    heads_out, vec, keep, send,
    up, upt, dqt, dk, dv, dots, moment, total_cols,
):
    me, first, total, mine = info[0], info[1], info[2], info[3]
    gain, shift = params[0:1, :], params[1:2, :]
    rows = g0.shape[0]
    block = rows
    width = q.shape[1]
    heads = width // HD
    for n, g in enumerate((g0, g1, g2, g3)):
        at = place(me ^ n, rows)
        up[pl.ds(at, rows), :] = g[...]
        upt[:, pl.ds(at, rows)] = g[...].T
    weighted = upt[...].astype(F32) * ot[...]
    for h in range(heads):
        dots[h : h + 1, :] = column_sum(weighted[HD * h : HD * h + HD])
    dqt[...] = jnp.zeros_like(dqt)
    moment[...] = jnp.zeros_like(moment)
    total_cols[...] = jnp.zeros_like(total_cols)
    lane_head = lax.broadcasted_iota(jnp.int32, (block, width), 1) // HD
    row_head = lax.broadcasted_iota(jnp.int32, (width, block), 0) // HD

    def key_block(j, unused):
        at_k = place(j, block)
        keys = k[pl.ds(at_k, block), :]
        values = v[pl.ds(at_k, block), :]
        dk[...] = jnp.zeros_like(dk)
        dv[...] = jnp.zeros_like(dv)

        def step(at, masked):
            cols = pl.ds(at, block)
            scaled_t = qt[:, cols] * BF16(0.125)
            scaled = q[pl.ds(at, block), :] * BF16(0.125)
            ups = up[pl.ds(at, block), :]
            ups_t = upt[:, cols]
            for h in range(heads):
                part = slice(HD * h, HD * h + HD)
                scores = dot(keys, jnp.where(row_head == h, scaled_t, BF16(0)))
                if masked:
                    row = at + lax.broadcasted_iota(jnp.int32, (1, block), 1)
                    start = start_of(row, first, total)
                    col = at_k + lax.broadcasted_iota(jnp.int32, (block, block), 0)
                    scores = jnp.where((col >= start) & (col <= row), scores, NEGATIVE)
                probs = jnp.exp(scores - lse[h : h + 1, cols])
                grads = dot(values, jnp.where(row_head == h, ups_t, BF16(0)))
                score_grad = (probs * (grads - dots[h : h + 1, cols])).astype(BF16)
                dv[...] += dot(probs.astype(BF16), jnp.where(lane_head == h, ups, BF16(0)))
                dk[...] += dot(score_grad, jnp.where(lane_head == h, scaled, BF16(0)))
                dqt[part, cols] += dot(kt[part, pl.ds(at_k, block)], score_grad)

        def loop(i, carry):
            at = place(i, block)
            begin = start_of(at, first, total)
            last_start = start_of(at + block - 1, first, total)
            whole = (i > j) & (at_k >= last_start)

            @pl.when(whole)
            def _():
                step(at, False)

            @pl.when(jnp.logical_not(whole) & (at_k + block > begin))
            def _():
                step(at, True)

            return carry

        lax.fori_loop(j, 4, loop, 0)
        grads_t = (
            (dqt[:, pl.ds(at_k, block)] * 0.125).astype(BF16),
            dk[...].T.astype(BF16),
            dv[...].T.astype(BF16),
        )
        unit_rows = unit_low[pl.ds(at_k, block), :]
        spread = 0.0
        for c in range(3):
            spread = spread + dot(grads_t[c], weights[c], 0, 1)
            moment[c] += dot(grads_t[c], unit_rows)
            total_cols[c] += jnp.sum(grads_t[c].astype(F32), axis=1, keepdims=True)
        spread = spread.astype(BF16)
        which = me ^ j
        at_row = place(which // 2, rows)

        @pl.when(which % 2 == 0)
        def _():
            keep[pl.ds(at_row, rows), :] = spread

        @pl.when(which % 2 == 1)
        def _():
            send[pl.ds(at_row, rows), :] = spread

        return unused

    lax.fori_loop(0, 4, key_block, 0)
    step_rows = width // PARTS
    part_rows = 3 * step_rows
    gain_grad = 0.0
    shift_grad = 0.0
    for c in range(3):
        turned = weights[c].astype(F32).T
        gain_grad = gain_grad + column_sum(turned * moment[c])
        shift_grad = shift_grad + column_sum(turned * total_cols[c])
        grad = (moment[c] * gain + total_cols[c] * shift).astype(BF16)
        for p in range(PARTS):
            at = pl.multiple_of(reverse(p ^ mine) * part_rows + c * step_rows, 16)
            heads_out[pl.ds(at, step_rows), :] = grad[p * step_rows : (p + 1) * step_rows]
    pick = lax.broadcasted_iota(jnp.int32, vec_in.shape, 0)
    sums = vec_in[...] + jnp.where(pick == 6, gain_grad, 0.0) + jnp.where(pick == 7, shift_grad, 0.0)
    vec[...] = sums.astype(BF16)


def tokens_backward(tok, own, got, local, carry, params, out):
    unit, scale = normalized(tok[...].astype(F32))
    grad = own[...].astype(F32) + got[...].astype(F32) + local[...]
    h = grad * params[0:1, :]
    out[...] = (
        carry[...] + scale * (h - row_mean(h) - unit * row_mean(h * unit))
    ).astype(BF16)


def each_part(info, refs, rows):
    pos = 0
    for ref in refs:
        for n in range(ref.shape[0] // rows):
            yield ORDER[pos] ^ info[3], ref, n * rows
            pos += 1


def unpack_down(info, s0, s1, s2, s3, down, gates, turned):
    step, small = down.shape[0] // PARTS, gates.shape[0] // (2 * PARTS)
    for p, ref, at in each_part(info, (s0, s1, s2, s3), step + 2 * small):
        turned[pl.ds(place(p, step), step), :] = ref[at : at + step].astype(F32)
        middle_at = at + step + small
        gates[pl.ds(place(p, small), small), :] = ref[at + step : middle_at]
        gates[pl.ds(pl.multiple_of((PARTS + p) * small, small), small), :] = ref[
            middle_at : middle_at + small
        ]
    down[...] = turned[...].T


def unpack_up(info, s0, s1, s2, s3, up, out):
    step, small = up.shape[0] // PARTS, out.shape[0] // PARTS
    for p, ref, at in each_part(info, (s0, s1, s2, s3), step + small):
        up[pl.ds(place(p, step), step), :] = ref[at : at + step].astype(F32)
        out[pl.ds(place(p, small), small), :] = ref[at + step : at + step + small].astype(F32)


def unpack_heads(info, s0, s1, s2, s3, heads, turned):
    step = heads.shape[2] // PARTS
    for p, ref, at in each_part(info, (s0, s1, s2, s3), 3 * step):
        for c in range(3):
            turned[c, pl.ds(place(p, step), step), :] = ref[at + c * step : at + (c + 1) * step].astype(F32)
    for c in range(3):
        heads[c] = turned[c].T


def unpack_gates(info, s0, s1, s2, s3, gate, passed):
    rows = gate.shape[0] // 4
    for k, ref in enumerate((s0, s1, s2, s3)):
        at = place(info[0] ^ k, rows)
        gate[pl.ds(at, rows), :] = ref[0:rows].astype(F32)
        passed[pl.ds(at, rows), :] = ref[rows : 2 * rows].astype(F32)


def unpack_vectors(info, one, two, *outs):
    sums = one[...] + two[...]
    for n in range(8):
        outs[n][...] = sums[n : n + 1]
    pick = lax.broadcasted_iota(jnp.int32, sums.shape, 0) == 8 + info[0]
    outs[8][...] = column_sum(jnp.where(pick, sums, 0.0))


def swap_tensor(values, mask):
    return lax.ppermute(values, "tensor", [(i, i ^ mask) for i in range(4)])


def swap_dp(values, mask):
    return lax.ppermute(values, "dp", [(i, i ^ mask) for i in range(lax.axis_size("dp"))])


def fold(values, got):
    return (values.astype(F32) + got.astype(F32)).astype(BF16)


def scatter_dp(values, mask):
    half = values.shape[0] // 2
    got = swap_dp(values[half:], mask)
    return fold(values[:half], got)


def spread_rest(values):
    mask = PARTS
    while mask < lax.axis_size("dp"):
        values = fold(values, swap_dp(values, mask))
        mask *= 2
    return values


def gather_dp(values):
    s1 = swap_dp(values, 4)
    s2 = swap_dp(jnp.concatenate([values, s1]), 2)
    s3 = swap_dp(jnp.concatenate([values, s1, s2]), 1)
    return (values, s1, s2, s3)


def body(
    tokens,
    norm_gain,
    norm_shift,
    heads_weight,
    output_weight,
    output_bias,
    gate_weight,
    gate_bias,
    second_gain,
    second_shift,
    up_weight,
    up_bias,
    down_weight,
    down_bias,
    pass_weight,
    pass_bias,
    lengths,
    owners,
    cotangent,
):
    rows, width = tokens.shape
    total_rows = 4 * rows
    head_width = heads_weight.shape[2]
    me = lax.axis_index("tensor")
    dp = lax.axis_index("dp")
    entries = jnp.arange(lengths.shape[0], dtype=jnp.int32)
    owned = owners == dp
    own_lengths = jnp.where(owned, lengths, 0)
    first_entry = jnp.min(jnp.where(owned, entries, lengths.shape[0]))
    first = jnp.sum(jnp.where(entries == first_entry, own_lengths, 0))
    info = jnp.stack([me, first, jnp.sum(own_lengths), dp % PARTS]).astype(jnp.int32)
    params = jnp.stack(
        [norm_gain, norm_shift, output_bias, gate_bias, second_gain, second_shift]
        + [down_bias, pass_bias]
    )
    split_heads = heads_weight.transpose(1, 0, 2)

    tok2 = swap_tensor(tokens, 2)
    tok1 = swap_tensor(tokens, 1)
    bias_rows = jnp.broadcast_to(up_bias[None, :], (16, width))
    pack0 = jnp.concatenate([up_weight, down_weight, output_weight, bias_rows])
    pack1 = swap_tensor(pack0, 1)
    held, tok1, pack1, params, info, tok2 = lax.optimization_barrier(
        (pack0, tok1, pack1, params, info, tok2)
    )
    pack2 = swap_tensor(held, 2)
    tok3 = swap_tensor(tok2, 1)

    unit, q, key, v, qt, kt, ot, lse, a0, a1, a2, a3 = call(
        attend_forward,
        "attend_forward",
        (info, tokens, tok1, tok2, tok3, params, split_heads),
        [shape(total_rows, width)]
        + [shape(total_rows, head_width)] * 3
        + [shape(head_width, total_rows)] * 2
        + [shape(head_width, total_rows, dtype=F32), shape(head_width // HD, total_rows, dtype=F32)]
        + [shape(rows, head_width)] * 4,
        [
            pltpu.VMEM((head_width, total_rows), BF16),
            pltpu.VMEM((head_width, rows), F32),
            pltpu.VMEM((8, rows), F32),
            pltpu.VMEM((8, rows), F32),
        ],
        micros=14,
        mib=24,
    )
    p0, p1, p2, p3 = a0, swap_tensor(a1, 1), swap_tensor(a2, 2), swap_tensor(a3, 3)
    p1, p2, p3, pack2 = lax.optimization_barrier((p1, p2, p3, pack2))
    pack3 = swap_tensor(pack2, 1)
    square = shape(rows, width)
    hidden_shape = shape(4, rows, width)
    output, g0, g1, g2, g3, hid, pre_low, ffn_low, z2_low, n2, z1_low, mixed_low, carry, vec = call(
        middle,
        "middle",
        (info, p0, p1, p2, p3, tokens, cotangent, pack0, pack1, pack2, pack3, params)
        + (gate_weight, pass_weight),
        [square]
        + [shape(rows, head_width)] * 4
        + [hidden_shape, hidden_shape]
        + [square] * 5
        + [shape(rows, width, dtype=F32), shape(16, width, dtype=F32)],
        [pltpu.VMEM((4, rows, width), F32)],
        micros=12,
        mib=40,
    )
    g1, g2, g3 = swap_tensor(g1, 1), swap_tensor(g2, 2), swap_tensor(g3, 3)
    rows_a = width + 2 * head_width
    rows_b = width + head_width
    keep, send, local, vec = call(
        weight_grads,
        "weight_grads",
        (info, hid, pre_low, ffn_low, z2_low, n2, z1_low, mixed_low, tokens, params)
        + (gate_weight, p0, p1, p2, p3, vec),
        [shape(2 * (rows_a + rows_b), width)] * 2
        + [shape(rows, width, dtype=F32), shape(16, width, dtype=F32)],
        [pltpu.VMEM((width, width), F32)] * 2,
        micros=8,
        mib=32,
    )
    got = swap_tensor(send, 1)
    g1, g2, g3, got = lax.optimization_barrier((g1, g2, g3, got))
    part_a = 2 * rows_a
    a_keep = fold(keep[:rows_a], got[:rows_a])
    a_send = fold(keep[rows_a:part_a], got[rows_a:part_a])
    b_keep = fold(keep[part_a : part_a + rows_b], got[part_a : part_a + rows_b])
    b_send = fold(keep[part_a + rows_b :], got[part_a + rows_b :])
    a_keep, a_send, b_keep, b_send, vec = lax.optimization_barrier((a_keep, a_send, b_keep, b_send, vec))
    a_got, b_got = swap_tensor(a_send, 2), swap_dp(b_send, 1)
    heads_sum, vec, rows_keep, rows_send = call(
        attend_backward,
        "attend_backward",
        (info, q, key, v, qt, kt, ot, lse, g0, g1, g2, g3, unit, split_heads, params, vec),
        [shape(3 * head_width, width), shape(16, width)] + [shape(2 * rows, width)] * 2,
        [
            pltpu.VMEM((total_rows, head_width), BF16),
            pltpu.VMEM((head_width, total_rows), BF16),
            pltpu.VMEM((head_width, total_rows), F32),
            pltpu.VMEM((rows, head_width), F32),
            pltpu.VMEM((rows, head_width), F32),
            pltpu.VMEM((8, total_rows), F32),
            pltpu.VMEM((3, head_width, width), F32),
            pltpu.VMEM((3, head_width, 1), F32),
        ],
        micros=19,
        mib=28,
    )
    a_got, b_got, heads_sum, vec, rows_keep, rows_send = lax.optimization_barrier(
        (a_got, b_got, heads_sum, vec, rows_keep, rows_send)
    )
    for mask in (1, 2, 4):
        half = heads_sum.shape[0] // 2
        got = swap_dp(jnp.concatenate([heads_sum[half:], vec]), mask)
        heads_sum, vec = fold(heads_sum[:half], got[:half]), fold(vec, got[half:])
    heads_sum, vec = spread_rest(heads_sum), spread_rest(vec).astype(F32)
    (heads_grad,) = call(
        unpack_heads,
        "unpack_heads",
        (info,) + gather_dp(heads_sum),
        [shape(3, width, head_width, dtype=F32)],
        [pltpu.VMEM((3, head_width, width), F32)],
    )
    vec = vec + swap_tensor(vec, 1)
    vectors = call(
        unpack_vectors,
        "unpack_vectors",
        (info, vec, swap_tensor(vec, 2)),
        [shape(1, width, dtype=F32)] * 9,
    )
    (
        down_bias_grad,
        pass_bias_grad,
        second_shift_grad,
        second_gain_grad,
        output_bias_grad,
        gate_bias_grad,
        norm_gain_grad,
        norm_shift_grad,
        up_bias_grad,
    ) = [v.reshape(width) for v in vectors]
    rows_got = swap_tensor(rows_send, 1)
    far = swap_tensor(fold(rows_keep[rows:], rows_got[rows:]), 2)
    near = fold(rows_keep[:rows], rows_got[:rows])
    (tokens_grad,) = call(
        tokens_backward,
        "tokens_backward",
        (tokens, near, far, local, carry, params),
        [square],
        scalars=0,
    )
    part = fold(a_keep, a_got)
    for mask in (1, 2, 4):
        part = scatter_dp(part, mask)
    down_grad, gates0 = call(
        unpack_down,
        "unpack_down",
        (info,) + gather_dp(spread_rest(part)),
        [shape(width, width, dtype=F32), shape(2 * head_width, width)],
        [pltpu.VMEM((width, width), F32)],
    )
    gates2 = swap_tensor(gates0, 2)
    gates1 = swap_tensor(gates0, 1)
    gates3 = swap_tensor(gates2, 1)
    gate_grad, pass_grad = call(
        unpack_gates,
        "unpack_gates",
        (info, gates0, gates1, gates2, gates3),
        [shape(width, width, dtype=F32)] * 2,
    )
    part = fold(b_keep, b_got)
    half = part.shape[0] // 2
    part = fold(part[:half], swap_tensor(part[half:], 2))
    for mask in (2, 4):
        part = scatter_dp(part, mask)
    s0, s1, s2, s3 = gather_dp(spread_rest(part))
    s3, tokens_grad, heads_grad = lax.optimization_barrier((s3, tokens_grad, heads_grad))
    up_grad, out_grad = call(
        unpack_up,
        "unpack_up",
        (info, s0, s1, s2, s3),
        [shape(width, width, dtype=F32), shape(head_width, width, dtype=F32)],
    )
    return (
        output,
        tokens_grad,
        norm_gain_grad,
        norm_shift_grad,
        heads_grad.transpose(1, 0, 2),
        out_grad,
        output_bias_grad,
        gate_grad,
        gate_bias_grad,
        second_gain_grad,
        second_shift_grad,
        up_grad,
        up_bias_grad,
        down_grad,
        down_bias_grad,
        pass_grad,
        pass_bias_grad,
    )


def solution(mesh):
    placed = (
        P(("dp", "tensor"), None),
        P(),
        P(),
        P(None, None, "tensor"),
        P("tensor", None),
        P(),
        P(),
        P(),
        P(),
        P(),
        P(None, "tensor"),
        P("tensor"),
        P("tensor", None),
        P(),
        P(),
        P(),
        P(),
        P(),
        P(("dp", "tensor"), None),
    )
    return jax.shard_map(
        body,
        mesh=mesh,
        in_specs=placed,
        out_specs=(
            P(("dp", "tensor"), None),
            P(("dp", "tensor"), None),
            P(),
            P(),
            P(None, None, "tensor"),
            P("tensor", None),
            P(),
            P(),
            P(),
            P(),
            P(),
            P(None, "tensor"),
            P("tensor"),
            P("tensor", None),
            P(),
            P(),
            P(),
        ),
        check_vma=False,
    )
```

```python
import functools

import jax
import jax.numpy as jnp
from jax import lax
from jax.experimental import pallas as pl
from jax.experimental.pallas import tpu as pltpu
from jax.sharding import PartitionSpec as P

HD = 64
EPS = 1e-05
NEGATIVE = -1e30
GELU_C = 0.7978845608028654
F32 = jnp.float32
BF16 = jnp.bfloat16
VMEM = pl.BlockSpec(memory_space=pltpu.VMEM)
HBM = pl.BlockSpec(memory_space=pltpu.HBM)
SMEM = pl.BlockSpec(memory_space=pltpu.SMEM)
PARTS = 8
WEIGHT_PARTS = 4


def dot(left, right, left_dim=1, right_dim=0):
    return lax.dot_general(
        left, right, (((left_dim,), (right_dim,)), ((), ())), preferred_element_type=F32
    )


def column_sum(values):
    return jnp.sum(values, axis=0, keepdims=True)


def row_mean(values):
    return jnp.mean(values, axis=-1, keepdims=True)


def normalized(values):
    centred = values - row_mean(values)
    scale = lax.rsqrt(row_mean(centred * centred) + EPS)
    return centred * scale, scale


def place(index, size):
    return pl.multiple_of(index * size, size)


def start_of(row, first, total):
    return jnp.where(row < first, 0, jnp.where(row < total, first, row))


def call(body, name, operands, outs, scratch=(), scalars=1, micros=2, mib=12, far=()):
    return pl.pallas_call(
        body,
        cost_estimate=pl.CostEstimate(flops=int(micros * 1.1e9), bytes_accessed=0, transcendentals=0),
        out_shape=[
            pltpu.HBM(item.shape, item.dtype) if n in far else item for n, item in enumerate(outs)
        ],
        in_specs=[SMEM] * scalars + [VMEM] * (len(operands) - scalars),
        out_specs=[
            HBM if n in far else SMEM if item.dtype == jnp.int32 else VMEM
            for n, item in enumerate(outs)
        ],
        scratch_shapes=list(scratch),
        compiler_params=pltpu.CompilerParams(vmem_limit_bytes=mib << 20),
        name=name,
    )(*operands)


def shape(*dims, dtype=BF16):
    return jax.ShapeDtypeStruct(dims, dtype)


def project(tok, params, weights):
    unit, _ = normalized(tok[...].astype(F32))
    normed = (unit * params[0:1, :] + params[1:2, :]).astype(BF16)
    q, key, v = [dot(normed, weights[c]).astype(BF16) for c in range(3)]
    return unit.astype(BF16), q * BF16(0.125), key, v


def attend(info, i, count, last, fresh, block, queries_t, keys, values_t, state):
    first, total = info[1], info[2]
    acc, sum_row, top_row = state
    width = acc.shape[0]
    base = i * block
    head = lax.broadcasted_iota(jnp.int32, (width, block), 0) // HD
    q_heads = [jnp.where(head == h, queries_t, BF16(0)) for h in range(width // HD)]
    row = base + lax.broadcasted_iota(jnp.int32, (1, block), 1)
    start = start_of(row, first, total)
    last_start = start_of(base + block - 1, first, total)

    @pl.when(fresh)
    def _():
        acc[...] = jnp.zeros_like(acc)
        sum_row[...] = jnp.zeros_like(sum_row)
        top_row[...] = jnp.full_like(top_row, NEGATIVE)

    def step(j, masked):
        at = place(j, block)
        key_rows = keys(j)
        for h in range(width // HD):
            part = slice(HD * h, HD * h + HD)
            scores = dot(key_rows, q_heads[h])
            if masked:
                col = at + lax.broadcasted_iota(jnp.int32, (block, block), 0)
                scores = jnp.where((col >= start) & (col <= row), scores, NEGATIVE)
            before = top_row[h : h + 1, :]
            top = jnp.maximum(before, jnp.max(scores, axis=0, keepdims=True))
            fade = jnp.exp(before - top)
            exponent = jnp.exp(scores - top)
            mixed = dot(values_t(part, j), exponent.astype(BF16))
            sum_row[h : h + 1, :] = sum_row[h : h + 1, :] * fade + column_sum(exponent)
            acc[part, :] = acc[part, :] * fade + mixed
            top_row[h : h + 1, :] = top

    def loop(n, carry):
        j = last - n
        masked = (j == i) | (j * block < last_start)

        @pl.when(masked)
        def _():
            step(j, True)

        @pl.when(jnp.logical_not(masked))
        def _():
            step(j, False)

        return carry

    lax.fori_loop(0, count, loop, 0)


def lowest_block(info, i, block):
    return start_of(i * block, info[1], info[2]) // block


def sequences(lengths, owners, info):
    here = lax.axis_index("dp")

    def entry(e, carry):
        first, seen, total = carry
        mine = owners[e] == here
        length = jnp.where(mine, lengths[e], 0)
        first = jnp.where(seen == 0, length, first)
        return first, seen + mine.astype(jnp.int32), total + length

    zero = jnp.int32(0)
    first, seen, total = lax.fori_loop(0, lengths.shape[0], entry, (zero, zero, zero))
    info[0] = lax.axis_index("tensor")
    info[1] = first
    info[2] = total
    info[3] = here % PARTS


def attend_near(
    lengths, owners, t0, t1, params, weights,
    info, unit_out, q_out, k_out, v_out, qt_out, kt_out, vt_out, acc, sum_row, top_row,
):
    sequences(lengths, owners, info)
    me = info[0]
    rows = t0.shape[0]
    for k, tok in enumerate((t0, t1)):
        at = place((me ^ k) % 2, rows)
        unit, q, key, v = project(tok, params, weights)
        unit_out[pl.ds(at, rows), :] = unit
        for out, turned, value in ((q_out, qt_out, q), (k_out, kt_out, key), (v_out, vt_out, v)):
            out[pl.ds(at, rows), :] = value
            turned[:, pl.ds(at, rows)] = value.T
    base = me // 2 * 2
    for n in range(2):
        i = base + n
        lanes = slice(n * rows, (n + 1) * rows)
        attend(
            info,
            i,
            i + 1 - jnp.maximum(lowest_block(info, i, rows), base),
            i,
            True,
            rows,
            qt_out[:, lanes],
            lambda j: k_out[pl.ds(place(j - base, rows), rows), :],
            lambda part, j: vt_out[part, pl.ds(place(j - base, rows), rows)],
            [ref.at[:, lanes] for ref in (acc, sum_row, top_row)],
        )


def attend_far(
    info, t2, t3, params, weights,
    unit_in, q_in, k_in, v_in, qt_in, kt_in, vt_in, acc_in, sum_in, top_in,
    unit_far, q_far, k_far, v_far, qt_far, kt_far, ot_far, lse_out, a0, a1, a2, a3,
    unit_new, q_new, k_new, v_new, qt_new, kt_new, keys, qt, vt, ot, acc, sum_row, top_row, done,
):
    me = info[0]
    rows = t2.shape[0]
    own = me // 2
    for k, tok in ((2, t2), (3, t3)):
        at = place((me ^ k) % 2, rows)
        unit, q, key, v = project(tok, params, weights)
        unit_new[pl.ds(at, rows), :] = unit
        q_new[pl.ds(at, rows), :] = q
        k_new[pl.ds(at, rows), :] = key
        v_new[pl.ds(at, rows), :] = v
        qt_new[:, pl.ds(at, rows)] = q.T
        kt_new[:, pl.ds(at, rows)] = key.T
        vt[:, pl.ds(place(me ^ k, rows), rows)] = v.T
    copies = []
    both = 2 * rows
    here, there = pl.ds(place(own, both), both), pl.ds(place(1 - own, both), both)
    for old, new, far in (
        (unit_in, unit_new, unit_far),
        (q_in, q_new, q_far),
        (k_in, k_new, k_far),
        (v_in, v_new, v_far),
    ):
        copies.append((old, far.at[here]))
        copies.append((new, far.at[there]))
    for old, new, far in ((qt_in, qt_new, qt_far), (kt_in, kt_new, kt_far)):
        copies.append((old, far.at[:, here]))
        copies.append((new, far.at[:, there]))
    copies.append((ot, ot_far))
    copies = [pltpu.make_async_copy(a, b, done.at[n]) for n, (a, b) in enumerate(copies)]
    for copy in copies[:-1]:
        copy.start()
    keys[here, :] = k_in[...]
    keys[there, :] = k_new[...]
    qt[:, here] = qt_in[...]
    qt[:, there] = qt_new[...]
    vt[:, here] = vt_in[...]

    def query_block(i, unused):
        other = i // 2 != own
        lanes = pl.ds(place(i, rows), rows)
        old = pl.ds(place(i % 2, rows), rows)
        lowest = lowest_block(info, i, rows)

        @pl.when(jnp.logical_not(other))
        def _():
            acc[...] = acc_in[:, old]
            sum_row[...] = sum_in[:, old]
            top_row[...] = top_in[:, old]

        attend(
            info,
            i,
            jnp.where(other, i + 1 - lowest, jnp.where(own == 1, jnp.maximum(2 - lowest, 0), 0)),
            jnp.where(other, i, 1),
            other,
            rows,
            qt[:, lanes],
            lambda j: keys[pl.ds(place(j, rows), rows), :],
            lambda part, j: vt[part, pl.ds(place(j, rows), rows)],
            (acc, sum_row, top_row),
        )
        for h in range(acc.shape[0] // HD):
            part = slice(HD * h, HD * h + HD)
            summed = sum_row[h : h + 1, :]
            ot[part, lanes] = acc[part, :] / summed
            lse_out[h : h + 1, lanes] = top_row[h : h + 1, :] + jnp.log(summed)
        return unused

    lax.fori_loop(0, 4, query_block, 0)
    copies[-1].start()
    for k, out in enumerate((a0, a1, a2, a3)):
        at = place(me ^ k, rows)
        out[...] = ot[:, pl.ds(at, rows)].T.astype(BF16)
    for copy in copies:
        copy.wait()


def live_rows(info, rows):
    row = info[0] * rows + lax.broadcasted_iota(jnp.int32, (rows, 1), 0)
    return (row < info[2]).astype(F32)


def put_parts(buf, base, grad, index, step, order, stride=None):
    for p in range(PARTS):
        at = base + order(p ^ index) * (step if stride is None else stride)
        buf[pl.ds(pl.multiple_of(at, 16), step), :] = grad[p * step : (p + 1) * step]


def hidden_block(pack, width, n2, gf_low):
    up, down = pack.at[0:width], pack.at[width + 16 : 2 * width + 16]
    pre = dot(n2, up[...]) + pack[width : width + 1, :].astype(F32)
    square = pre * pre
    th = jnp.tanh(GELU_C * pre * (1.0 + 0.044715 * square))
    half = 0.5 * (1.0 + th)
    hidden = (pre * half).astype(BF16)
    slope = half + 0.5 * GELU_C * pre * (1.0 - th * th) * (1.0 + 0.134145 * square)
    grad = dot(gf_low, down[...], 1, 1) * slope
    low = grad.astype(BF16)
    return hidden, low, column_sum(grad), dot(hidden, down[...]), dot(low, up[...], 1, 1)


def middle_first(
    info, p0, p1, p2, p3, o0, o1, o2, o3, tok, cot, w0, w1, params, gate_w, pass_w,
    n2_out, ffn_low, y_out, gate2_out, gate_out, mixed_out, ffn_out, gn2_out, vec, keep, send,
):
    me, index = info[0], info[3]
    gain, shift, out_b, gate_b, gain2, shift2, down_b, pass_b = [
        params[n : n + 1, :] for n in range(8)
    ]
    rows, width = tok.shape
    x = tok[...].astype(F32)
    unit, _ = normalized(x)
    n1 = (unit * gain + shift).astype(BF16)
    mixed = out_b
    for p, w in zip((p0, p1, p2, p3), (o0, o1, o2, o3)):
        mixed = mixed + dot(p[...], w[...])
    mixed_out[...] = mixed
    gate = jax.nn.sigmoid(dot(n1, gate_w[...]) + gate_b)
    gate_out[...] = gate
    y = gate * mixed + (1.0 - gate) * x
    y_out[...] = y
    unit2, _ = normalized(y)
    n2 = (unit2 * gain2 + shift2).astype(BF16)
    n2_out[...] = n2
    gate2 = jax.nn.sigmoid(dot(n2, pass_w[...]) + pass_b)
    gate2_out[...] = gate2
    gf = cot[...].astype(F32) * live_rows(info, rows) * gate2
    vec[...] = jnp.zeros_like(vec)
    vec[0:1, :] = column_sum(gf)
    gf_low = gf.astype(BF16)
    ffn_low[...] = gf_low
    n2_turned = n2.T
    ffn_turned = gf_low.T
    ffn, gn2 = down_b, 0.0
    for k, (pack, buf) in enumerate(((w0, keep), (w1, send))):
        hidden, low, columns, more_ffn, more_gn2 = hidden_block(pack, width, n2, gf_low)
        vec[pl.ds(8 + (me ^ k), 1), :] = columns
        ffn = ffn + more_ffn
        gn2 = gn2 + more_gn2
        step = width // PARTS
        put_parts(buf, 0, dot(ffn_turned, hidden).astype(BF16), index, step, reverse)
        put_parts(buf, width, dot(n2_turned, low).astype(BF16), index, step, reverse)
    ffn_out[...] = ffn
    gn2_out[...] = gn2


def middle_second(
    info, o0, o1, o2, o3, tok, cot, w2, w3, params, pass_w,
    n2_in, ffn_low, y_in, gate2_in, gate_in, mixed_in, ffn_in, gn2_in, vec_in,
    out, g0, g1, g2, g3, hid, pre_low, z2_low, z1_low, mixed_low, carry, vec,
    whole2, whole3,
):
    me = info[0]
    quarter = w2.shape[0] // WEIGHT_PARTS
    for part in range(WEIGHT_PARTS):
        at = place((info[3] ^ part) % WEIGHT_PARTS, quarter)
        for whole, parts in ((whole2, w2), (whole3, w3)):
            whole[pl.ds(at, quarter), :] = parts[part * quarter : (part + 1) * quarter]
    gain2 = params[4:5, :]
    rows, width = tok.shape
    n2, gf_low = n2_in[...], ffn_low[...]
    ffn, gn2 = ffn_in[...], gn2_in[...]
    vec[...] = vec_in[...]
    for n, pack in enumerate((whole2, whole3)):
        hidden, low, columns, more_ffn, more_gn2 = hidden_block(pack, width, n2, gf_low)
        hid[n] = hidden
        pre_low[n] = low
        vec[pl.ds(8 + (me ^ (2 + n)), 1), :] = columns
        ffn = ffn + more_ffn
        gn2 = gn2 + more_gn2
    live = live_rows(info, rows)
    gate2, y = gate2_in[...], y_in[...]
    out[...] = ((gate2 * ffn + (1.0 - gate2) * y) * live).astype(BF16)
    gy = cot[...].astype(F32) * live
    z2 = gy * gate2 * (ffn - y) * (1.0 - gate2)
    vec[1:2, :] = column_sum(z2)
    z2l = z2.astype(BF16)
    z2_low[...] = z2l
    gn2 = gn2 + dot(z2l, pass_w[...], 1, 1)
    unit2, scale2 = normalized(y)
    vec[2:3, :] = column_sum(gn2)
    vec[3:4, :] = column_sum(gn2 * unit2)
    g = gn2 * gain2
    gy1 = gy * (1.0 - gate2) + scale2 * (g - row_mean(g) - unit2 * row_mean(g * unit2))
    gate = gate_in[...]
    gm = gy1 * gate
    vec[4:5, :] = column_sum(gm)
    z1 = gm * (mixed_in[...] - tok[...].astype(F32)) * (1.0 - gate)
    vec[5:6, :] = column_sum(z1)
    z1_low[...] = z1.astype(BF16)
    gml = gm.astype(BF16)
    mixed_low[...] = gml
    carry[...] = gy1 * (1.0 - gate)
    for g_out, w in zip((g0, g1, g2, g3), (o0, o1, o2, o3)):
        g_out[...] = dot(gml, w[...], 1, 1).astype(BF16)


ORDER = [int(f"{p:03b}"[::-1], 2) for p in range(PARTS)]
REST_ORDER = [((p >> 1) & 1) | ((p >> 2) << 1) | ((p & 1) << 2) for p in range(PARTS)]


def weight_grads(
    info, hid, pre_low, ffn_low, z2_low, n2, z1_low, mixed_low, tok, params, gate_w,
    p0, p1, p2, p3, vec_in,
    keep, send, local, vec,
    scratch_gate, scratch_pass,
):
    me, mine = info[0], info[3]
    gain, shift = params[0:1, :], params[1:2, :]
    width = tok.shape[1]
    heads = p0.shape[1]
    unit, _ = normalized(tok[...].astype(F32))
    n1 = (unit * gain + shift).astype(BF16)
    z1l = z1_low[...]
    step = width // PARTS
    small = heads // PARTS
    n2_turned = n2[...].T
    n1_turned = n1.T
    z2l = z2_low[...]
    gml = mixed_low[...]
    ffn_turned = ffn_low[...].T
    pieces = (p0, p1, p2, p3)
    scratch_gate[...] = dot(n1_turned, z1l)
    scratch_pass[...] = dot(n2_turned, z2l)
    for n, buf in enumerate((keep, send)):
        grad = dot(ffn_turned, hid[n]).astype(BF16)
        put_parts(buf, 0, grad, mine, step, reverse)
        grad = dot(n2_turned, pre_low[n]).astype(BF16)
        put_parts(buf, width, grad, mine, step, reverse)
    for k in range(4):
        buf = (keep, send)[k % 2]
        out_grad = dot(pieces[k][...], gml, 0, 0).astype(BF16)
        at = place(me ^ k, heads)
        rest = (out_grad,) + tuple(
            ref[pl.ds(at, heads), :].astype(BF16) for ref in (scratch_gate, scratch_pass)
        )
        for n, grad in enumerate(rest):
            base = 2 * width + (3 * (k // 2) + n) * small
            put_parts(buf, base, grad, mine, small, reverse_rest, 6 * small)
    dz = dot(z1l, gate_w[...], 1, 1)
    local[...] = dz
    vec[...] = vec_in[...]
    vec[6:7, :] = column_sum(dz * unit)
    vec[7:8, :] = column_sum(dz)


def reverse_rest(part):
    return ((part & 2) << 1) | ((part & 1) << 1) | ((part >> 2) & 1)


def reverse(part):
    return ((part & 1) << 2) | (part & 2) | ((part >> 2) & 1)


def backward_blocks(lowest, info, q, k, v, qt, kt, lse, unit_low, weights, keep, send,
    up, upt, dqt, dk, dv, dots, moment, total_cols):
    me, first, total = info[0], info[1], info[2]
    rows = keep.shape[0]
    block = rows
    width = q.shape[1]
    heads = width // HD
    lane_head = lax.broadcasted_iota(jnp.int32, (block, width), 1) // HD
    row_head = lax.broadcasted_iota(jnp.int32, (width, block), 0) // HD

    def key_block(j, unused):
        at_k = place(j, block)
        keys = k[pl.ds(at_k, block), :]
        values = v[pl.ds(at_k, block), :]
        dk[...] = jnp.zeros_like(dk)
        dv[...] = jnp.zeros_like(dv)

        def step(at, masked):
            cols = pl.ds(at, block)
            scaled_t = qt[:, cols]
            scaled = q[pl.ds(at, block), :]
            ups = up[pl.ds(at, block), :]
            ups_t = upt[:, cols]
            for h in range(heads):
                part = slice(HD * h, HD * h + HD)
                scores = dot(keys, jnp.where(row_head == h, scaled_t, BF16(0)))
                if masked:
                    row = at + lax.broadcasted_iota(jnp.int32, (1, block), 1)
                    start = start_of(row, first, total)
                    col = at_k + lax.broadcasted_iota(jnp.int32, (block, block), 0)
                    scores = jnp.where((col >= start) & (col <= row), scores, NEGATIVE)
                probs = jnp.exp(scores - lse[h : h + 1, cols])
                grads = dot(values, jnp.where(row_head == h, ups_t, BF16(0)))
                score_grad = (probs * (grads - dots[h : h + 1, cols])).astype(BF16)
                dv[...] += dot(probs.astype(BF16), jnp.where(lane_head == h, ups, BF16(0)))
                dk[...] += dot(score_grad, jnp.where(lane_head == h, scaled, BF16(0)))
                dqt[part, cols] += dot(kt[part, pl.ds(at_k, block)], score_grad)

        def loop(i, carry):
            at = place(i, block)
            begin = start_of(at, first, total)
            last_start = start_of(at + block - 1, first, total)
            whole = (i > j) & (at_k >= last_start)

            @pl.when(whole)
            def _():
                step(at, False)

            @pl.when(jnp.logical_not(whole) & (at_k + block > begin))
            def _():
                step(at, True)

            return carry

        lax.fori_loop(j, 4, loop, 0)
        grads_t = (
            (dqt[:, pl.ds(at_k, block)] * 0.125).astype(BF16),
            dk[...].T.astype(BF16),
            dv[...].T.astype(BF16),
        )
        unit_rows = unit_low[pl.ds(at_k, block), :]
        spread = 0.0
        for c in range(3):
            spread = spread + dot(grads_t[c], weights[c], 0, 1)
            moment[c] += dot(grads_t[c], unit_rows)
            total_cols[c] += jnp.sum(grads_t[c].astype(F32), axis=1, keepdims=True)
        spread = spread.astype(BF16)
        even = (me ^ j) % 2 == 0

        @pl.when(even)
        def _():
            keep[...] = spread

        @pl.when(jnp.logical_not(even))
        def _():
            send[...] = spread

        return unused

    lax.fori_loop(lowest, lowest + 2, key_block, 0)


def attend_backward_first(
    info, q, k, v, qt, kt, ot, lse, g0, g1, g2, g3, unit_low, weights,
    keep, send, up, upt, dots, dqt, moment, total_cols,
    dk, dv,
):
    me = info[0]
    rows = g0.shape[0]
    for n, g in enumerate((g0, g1, g2, g3)):
        at = place(me ^ n, rows)
        up[pl.ds(at, rows), :] = g[...]
        upt[:, pl.ds(at, rows)] = g[...].T
    weighted = upt[...].astype(F32) * ot[...]
    for h in range(dots.shape[0]):
        dots[h : h + 1, :] = column_sum(weighted[HD * h : HD * h + HD])
    dqt[...] = jnp.zeros_like(dqt)
    moment[...] = jnp.zeros_like(moment)
    total_cols[...] = jnp.zeros_like(total_cols)
    backward_blocks(0, info, q, k, v, qt, kt, lse, unit_low, weights, keep, send,
        up, upt, dqt, dk, dv, dots, moment, total_cols)


def attend_backward_second(
    info, q, k, v, qt, kt, lse, unit_low, weights, up, upt, dots, dqt_in, moment_in, cols_in,
    params, vec_in,
    keep, send, heads_out, vec,
    dk, dv, dqt, moment, total_cols,
):
    mine = info[3]
    gain, shift = params[0:1, :], params[1:2, :]
    width = q.shape[1]
    half = dqt.shape[1] // 2
    dqt[:, half:] = dqt_in[:, half:]
    moment[...] = moment_in[...]
    total_cols[...] = cols_in[...]
    backward_blocks(2, info, q, k, v, qt, kt, lse, unit_low, weights, keep, send,
        up, upt, dqt, dk, dv, dots, moment, total_cols)
    step_rows = width // PARTS
    part_rows = 3 * step_rows
    gain_grad = 0.0
    shift_grad = 0.0
    for c in range(3):
        turned = weights[c].astype(F32).T
        gain_grad = gain_grad + column_sum(turned * moment[c])
        shift_grad = shift_grad + column_sum(turned * total_cols[c])
        grad = (moment[c] * gain + total_cols[c] * shift).astype(BF16)
        for p in range(PARTS):
            at = pl.multiple_of(reverse(p ^ mine) * part_rows + c * step_rows, 16)
            heads_out[pl.ds(at, step_rows), :] = grad[p * step_rows : (p + 1) * step_rows]
    pick = lax.broadcasted_iota(jnp.int32, vec_in.shape, 0)
    sums = vec_in[...] + jnp.where(pick == 6, gain_grad, 0.0) + jnp.where(pick == 7, shift_grad, 0.0)
    vec[...] = sums.astype(BF16)


def tokens_backward(tok, own, got, local, carry, params, out):
    unit, scale = normalized(tok[...].astype(F32))
    grad = own[...].astype(F32) + got[...].astype(F32) + local[...]
    h = grad * params[0:1, :]
    out[...] = (
        carry[...] + scale * (h - row_mean(h) - unit * row_mean(h * unit))
    ).astype(BF16)


def each_part(info, refs, rows, order=ORDER):
    pos = 0
    for ref in refs:
        for n in range(ref.shape[0] // rows):
            yield order[pos] ^ info[3], ref, n * rows
            pos += 1


def unpack_down(info, s0, s1, s2, down, turned):
    step = down.shape[0] // PARTS
    for p, ref, at in each_part(info, (s0, s1, s2), step):
        turned[pl.ds(place(p, step), step), :] = ref[at : at + step].astype(F32)
    down[...] = turned[...].T


def unpack_up(info, s0, s1, s2, up):
    step = up.shape[0] // PARTS
    for p, ref, at in each_part(info, (s0, s1, s2), step):
        up[pl.ds(place(p, step), step), :] = ref[at : at + step].astype(F32)


def unpack_rest(info, s0, s1, s2, out, gates):
    rows = out.shape[0]
    step = rows // PARTS
    for p, ref, at in each_part(info, (s0, s1, s2), 5 * step, REST_ORDER):
        out[pl.ds(place(p, step), step), :] = ref[at : at + step].astype(F32)
        for n in range(4):
            first = at + (n + 1) * step
            gates[pl.ds(pl.multiple_of(n * rows + p * step, step), step), :] = ref[
                first : first + step
            ]


def unpack_heads(info, s0, s1, s2, heads, turned):
    step = heads.shape[2] // PARTS
    for p, ref, at in each_part(info, (s0, s1, s2), 3 * step):
        for c in range(3):
            turned[c, pl.ds(place(p, step), step), :] = ref[at + c * step : at + (c + 1) * step].astype(F32)
    for c in range(3):
        heads[c] = turned[c].T


def unpack_gates(info, mine, other, gate, passed):
    rows = gate.shape[0] // 4
    for k in range(4):
        ref = (mine, other)[k % 2]
        first = (k // 2) * 2 * rows
        at = place(info[0] ^ k, rows)
        gate[pl.ds(at, rows), :] = ref[first : first + rows].astype(F32)
        passed[pl.ds(at, rows), :] = ref[first + rows : first + 2 * rows].astype(F32)


def unpack_vectors(info, one, two, *outs):
    sums = one[...] + two[...]
    for n in range(8):
        outs[n][...] = sums[n : n + 1]
    pick = lax.broadcasted_iota(jnp.int32, sums.shape, 0) == 8 + info[0]
    outs[8][...] = column_sum(jnp.where(pick, sums, 0.0))


def swap_tensor(values, mask):
    return lax.ppermute(values, "tensor", [(i, i ^ mask) for i in range(4)])


def swap_dp(values, mask):
    return lax.ppermute(values, "dp", [(i, i ^ mask) for i in range(lax.axis_size("dp"))])


def fold(values, got):
    return (values.astype(F32) + got.astype(F32)).astype(BF16)


def scatter(values, axis, mask):
    half = values.shape[0] // 2
    got = yield values[half:], axis, mask
    return fold(values[:half], got)


def reduce_dp(values, masks, more=None):
    extra = 0 if more is None else more.shape[0]
    for mask in masks:
        half = values.shape[0] // 2
        sent = values[half:]
        if extra:
            sent = jnp.concatenate([sent, more])
        got = yield sent, "dp", mask
        values = fold(values[:half], got[:half])
        if extra:
            more = fold(more, got[half:])
    mask = 4
    while mask < lax.axis_size("dp"):
        size = values.shape[0]
        if mask == 4:
            sent = [values[size // 2 :], values[: size // 2]]
        else:
            sent = [values]
        if extra:
            sent = sent + [more]
        got = yield jnp.concatenate(sent), "dp", mask
        values = fold(values, got[:size])
        if extra:
            more = fold(more, got[size:])
        mask *= 2
    return (values, more) if extra else values


def gather_dp(values, masks=(2, 1)):
    s2 = yield values, "dp", masks[0]
    s3 = yield jnp.concatenate([values, s2]), "dp", masks[1]
    return values, s2, s3


def middle_of_rest(values):
    step = values.shape[0] // (6 * (PARTS // 2))
    sent, kept = [], []
    for n in range(0, 6 * (PARTS // 2), 6):
        share = lambda a, b: values[(n + a) * step : (n + b) * step]
        sent += [share(3, 6), share(1, 3)]
        kept += [share(0, 3), share(4, 6)]
    return jnp.concatenate(sent), jnp.concatenate(kept)


def run_chains(chains):
    results = [None] * len(chains)
    waiting = [None] * len(chains)
    alive = list(range(len(chains)))
    while alive:
        for n in list(alive):
            try:
                values, axis, mask = chains[n].send(waiting[n])
            except StopIteration as stop:
                results[n] = stop.value
                alive.remove(n)
                continue
            waiting[n] = (swap_dp if axis == "dp" else swap_tensor)(values, mask)
    return results


def body(
    tokens,
    norm_gain,
    norm_shift,
    heads_weight,
    output_weight,
    output_bias,
    gate_weight,
    gate_bias,
    second_gain,
    second_shift,
    up_weight,
    up_bias,
    down_weight,
    down_bias,
    pass_weight,
    pass_bias,
    lengths,
    owners,
    cotangent,
):
    rows, width = tokens.shape
    total_rows = 4 * rows
    head_width = heads_weight.shape[2]
    me = lax.axis_index("tensor")
    params = jnp.stack(
        [norm_gain, norm_shift, output_bias, gate_bias, second_gain, second_shift]
        + [down_bias, pass_bias]
    )
    split_heads = heads_weight.transpose(1, 0, 2)

    def kept(count):
        kinds = [shape(count, width)] + [shape(count, head_width)] * 3
        return kinds + [shape(head_width, count)] * 2

    tok2 = swap_tensor(tokens, 2)
    tok1 = swap_tensor(tokens, 1)
    state = [(head_width, 2 * rows), (8, 2 * rows), (8, 2 * rows)]
    info, *near = call(
        attend_near,
        "attend_near",
        (lengths, owners, tokens, tok1, params, split_heads),
        [shape(4, dtype=jnp.int32)]
        + kept(2 * rows)
        + [shape(head_width, 2 * rows)]
        + [shape(*dims, dtype=F32) for dims in state],
        scalars=2,
        micros=6,
        mib=12,
    )
    bias_rows = jnp.broadcast_to(up_bias[None, :], (16, width))
    pack0 = jnp.concatenate([up_weight, bias_rows, down_weight, jnp.zeros((48, width), BF16)])
    quarter = pack0.shape[0] // WEIGHT_PARTS
    sent = lax.dynamic_slice_in_dim(
        pack0, lax.axis_index("dp") % WEIGHT_PARTS * quarter, quarter, 0
    )
    pack1 = swap_tensor(pack0, 1)
    out1 = swap_tensor(output_weight, 1)
    sent, out_held, pack1, out1, tok2, *near = lax.optimization_barrier(
        (sent, output_weight, pack1, out1, tok2, *near)
    )
    out2 = swap_tensor(out_held, 2)
    part0 = swap_tensor(sent, 2)
    tok3 = swap_tensor(tok2, 1)

    later = kept(total_rows) + [shape(head_width, total_rows, dtype=F32)]
    unit, q, key, v, qt, kt, ot, lse, a0, a1, a2, a3 = call(
        attend_far,
        "attend_far",
        (info, tok2, tok3, params, split_heads) + tuple(near),
        later
        + [shape(head_width // HD, total_rows, dtype=F32)]
        + [shape(rows, head_width)] * 4,
        [pltpu.VMEM(item.shape, item.dtype) for item in kept(2 * rows)]
        + [
            pltpu.VMEM((total_rows, head_width), BF16),
            pltpu.VMEM((head_width, total_rows), BF16),
            pltpu.VMEM((head_width, total_rows), BF16),
            pltpu.VMEM((head_width, total_rows), F32),
        ]
        + [pltpu.VMEM((dims[0], rows), F32) for dims in state]
        + [pltpu.SemaphoreType.DMA((13,))],
        micros=10,
        mib=20,
        far=range(len(later)),
    )
    a0, a1, a2, a3, out2, part0 = lax.optimization_barrier((a0, a1, a2, a3, out2, part0))
    out3 = swap_tensor(out2, 1)
    p0, p1, p2, p3 = a0, swap_tensor(a1, 1), swap_tensor(a2, 2), swap_tensor(a3, 3)
    part1, part2 = swap_dp(part0, 1), swap_dp(part0, 2)
    p1, p2, p3, out3, part1, part2 = lax.optimization_barrier((p1, p2, p3, out3, part1, part2))
    part3 = swap_dp(part2, 1)
    outs = (output_weight, out1, out2, out3)
    square, square32 = shape(rows, width), shape(rows, width, dtype=F32)
    n2, ffn_low, y, gate2, gate, mixed, ffn, gn2, vec, keep0, send0 = call(
        middle_first,
        "middle_first",
        (info, p0, p1, p2, p3) + outs + (tokens, cotangent, pack0, pack1, params)
        + (gate_weight, pass_weight),
        [square] * 2
        + [square32] * 6
        + [shape(16, width, dtype=F32)]
        + [shape(2 * width, width)] * 2,
        micros=9,
        mib=20,
    )
    n2, part3, send0 = lax.optimization_barrier((n2, part3, send0))
    parts2 = jnp.concatenate([part0, part1, part2, part3])
    parts3 = swap_tensor(parts2, 1)
    got0 = swap_tensor(send0, 1)
    output, g0, g1, g2, g3, hid, pre_low, z2_low, z1_low, mixed_low, carry, vec = call(
        middle_second,
        "middle_second",
        (info,) + outs + (tokens, cotangent, parts2, parts3, params, pass_weight)
        + (n2, ffn_low, y, gate2, gate, mixed, ffn, gn2, vec),
        [square]
        + [shape(rows, head_width)] * 4
        + [shape(2, rows, width)] * 2
        + [square] * 3
        + [square32, shape(16, width, dtype=F32)],
        [pltpu.VMEM(pack0.shape, BF16)] * 2,
        micros=7,
        mib=20,
    )
    g1, g2, g3 = swap_tensor(g1, 1), swap_tensor(g2, 2), swap_tensor(g3, 3)
    keep, send, local, vec = call(
        weight_grads,
        "weight_grads",
        (info, hid, pre_low, ffn_low, z2_low, n2, z1_low, mixed_low, tokens, params)
        + (gate_weight, p0, p1, p2, p3, vec),
        [shape(2 * width + 6 * head_width, width)] * 2
        + [square32, shape(16, width, dtype=F32)],
        [pltpu.VMEM((width, width), F32)] * 2,
        micros=4,
        mib=14,
    )
    g1, g2, g3, got0, keep, send, vec = lax.optimization_barrier(
        (g1, g2, g3, got0, keep, send, vec)
    )
    got = swap_tensor(send, 1)
    near = fold(keep0, got0)
    total = fold(keep, got)
    half = width // 2
    down0, up_keep = near[:width], near[width:]
    down2, up_send = total[:width], total[width : 2 * width]
    rest = total[2 * width :]
    down_send = jnp.concatenate([down0[half:], down2[half:]])
    down_keep = jnp.concatenate([down0[:half], down2[:half]])
    half = rest.shape[0] // 2
    down_send, up_send, rest_send, vec = lax.optimization_barrier(
        (down_send, up_send, rest[half:], vec)
    )
    down_got = swap_dp(down_send, 1)
    up_got = swap_tensor(up_send, 2)
    rest_got = swap_dp(rest_send, 2)
    blocks = [pltpu.VMEM((rows, head_width), F32)] * 2
    totals = [(head_width, total_rows), (3, head_width, width), (3, head_width, 1)]
    keep0, send0, up, upt, dots, dqt, moment, total_cols = call(
        attend_backward_first,
        "attend_backward_first",
        (info, q, key, v, qt, kt, ot, lse, g0, g1, g2, g3, unit, split_heads),
        [square] * 2
        + [shape(total_rows, head_width), shape(head_width, total_rows)]
        + [shape(head_width // HD, total_rows, dtype=F32)]
        + [shape(*dims, dtype=F32) for dims in totals],
        blocks,
        micros=12,
        mib=12,
    )
    keep0, send0, dqt, down_got, up_got, rest_got = lax.optimization_barrier(
        (keep0, send0, dqt, down_got, up_got, rest_got)
    )
    down_part = fold(down_keep, down_got)
    up_part = fold(up_keep, up_got)
    rest = fold(rest[:half], rest_got)
    half = down_part.shape[0] // 2
    down_send, up_send, dqt = lax.optimization_barrier((down_part[half:], up_part[half:], dqt))
    down_got = swap_tensor(down_send, 2)
    up_got = swap_dp(up_send, 1)
    rest_sent, rest_kept = middle_of_rest(rest)
    rest_got = swap_tensor(rest_sent, 2)
    got0 = swap_tensor(send0, 1)
    keep1, send1, heads_sum, vec = call(
        attend_backward_second,
        "attend_backward_second",
        (info, q, key, v, qt, kt, lse, unit, split_heads, up, upt, dots, dqt, moment)
        + (total_cols, params, vec),
        [square] * 2 + [shape(3 * head_width, width), shape(16, width)],
        blocks + [pltpu.VMEM(dims, F32) for dims in totals],
        micros=7,
        mib=12,
    )
    down_got, up_got, rest_got, got0, heads_sum, vec, keep1, send1 = lax.optimization_barrier(
        (down_got, up_got, rest_got, got0, heads_sum, vec, keep1, send1)
    )

    def heads_chain(values, vec):
        values, vec = yield from reduce_dp(values, (1, 2), vec)
        vec = vec.astype(F32)
        s2 = yield values, "dp", 2
        got = yield vec, "tensor", 1
        vec = vec + got
        got = yield vec, "tensor", 2
        vectors = call(
            unpack_vectors,
            "unpack_vectors",
            (info, vec, got),
            [shape(1, width, dtype=F32)] * 9,
        )
        s3 = yield jnp.concatenate([values, s2]), "dp", 1
        (heads_grad,) = call(
            unpack_heads,
            "unpack_heads",
            (info, values, s2, s3),
            [shape(3, width, head_width, dtype=F32)],
            [pltpu.VMEM((3, head_width, width), F32)],
        )
        return heads_grad, [v.reshape(width) for v in vectors]

    def rows_chain():
        got = yield send1, "tensor", 1
        lower, upper = fold(keep0, got0), fold(keep1, got)
        is_lower = me < 2
        near = jnp.where(is_lower, lower, upper)
        far = yield jnp.where(is_lower, upper, lower), "tensor", 2
        return call(
            tokens_backward,
            "tokens_backward",
            (tokens, near, far, local, carry, params),
            [square],
            scalars=0,
        )[0]

    def rest_chain(values):
        values = yield from reduce_dp(values, (1,))
        parts = yield from gather_dp(values, (1, 2))
        out_grad, gates = call(
            unpack_rest,
            "unpack_rest",
            (info,) + parts,
            [shape(head_width, width, dtype=F32), shape(4 * head_width, width)],
        )
        other_gates = yield gates, "tensor", 1
        gate_grad, pass_grad = call(
            unpack_gates,
            "unpack_gates",
            (info, gates, other_gates),
            [shape(width, width, dtype=F32)] * 2,
        )
        return out_grad, gate_grad, pass_grad

    def down_chain(values):
        values = yield from reduce_dp(values, (2,))
        parts = yield from gather_dp(values)
        return call(
            unpack_down,
            "unpack_down",
            (info,) + parts,
            [shape(width, width, dtype=F32)],
            [pltpu.VMEM((width, width), F32)],
        )[0]

    def up_chain(values):
        values = yield from reduce_dp(values, (2,))
        parts = yield from gather_dp(values)
        return call(
            unpack_up,
            "unpack_up",
            (info,) + parts,
            [shape(width, width, dtype=F32)],
        )[0]

    (
        (out_grad, gate_grad, pass_grad),
        down_grad,
        up_grad,
        (heads_grad, vectors),
        tokens_grad,
    ) = run_chains(
        [
            rest_chain(fold(rest_kept, rest_got)),
            down_chain(fold(down_part[:half], down_got)),
            up_chain(fold(up_part[:half], up_got)),
            heads_chain(heads_sum, vec),
            rows_chain(),
        ]
    )
    (
        down_bias_grad,
        pass_bias_grad,
        second_shift_grad,
        second_gain_grad,
        output_bias_grad,
        gate_bias_grad,
        norm_gain_grad,
        norm_shift_grad,
        up_bias_grad,
    ) = vectors
    return (
        output,
        tokens_grad,
        norm_gain_grad,
        norm_shift_grad,
        heads_grad.transpose(1, 0, 2),
        out_grad,
        output_bias_grad,
        gate_grad,
        gate_bias_grad,
        second_gain_grad,
        second_shift_grad,
        up_grad,
        up_bias_grad,
        down_grad,
        down_bias_grad,
        pass_grad,
        pass_bias_grad,
    )


def solution(mesh):
    placed = (
        P(("dp", "tensor"), None),
        P(),
        P(),
        P(None, None, "tensor"),
        P("tensor", None),
        P(),
        P(),
        P(),
        P(),
        P(),
        P(None, "tensor"),
        P("tensor"),
        P("tensor", None),
        P(),
        P(),
        P(),
        P(),
        P(),
        P(("dp", "tensor"), None),
    )
    return jax.shard_map(
        body,
        mesh=mesh,
        in_specs=placed,
        out_specs=(
            P(("dp", "tensor"), None),
            P(("dp", "tensor"), None),
            P(),
            P(),
            P(None, None, "tensor"),
            P("tensor", None),
            P(),
            P(),
            P(),
            P(),
            P(),
            P(None, "tensor"),
            P("tensor"),
            P("tensor", None),
            P(),
            P(),
            P(),
        ),
        check_vma=False,
    )
```

```python
import functools

import jax
import jax.numpy as jnp
from jax import lax
from jax.experimental import pallas as pl
from jax.experimental.pallas import tpu as pltpu
from jax.sharding import PartitionSpec as P

HD = 64
EPS = 1e-05
NEGATIVE = -1e30
GELU_C = 0.7978845608028654
F32 = jnp.float32
BF16 = jnp.bfloat16
VMEM = pl.BlockSpec(memory_space=pltpu.VMEM)
HBM = pl.BlockSpec(memory_space=pltpu.HBM)
SMEM = pl.BlockSpec(memory_space=pltpu.SMEM)
PARTS = 8
WEIGHT_PARTS = 4


def dot(left, right, left_dim=1, right_dim=0):
    return lax.dot_general(
        left, right, (((left_dim,), (right_dim,)), ((), ())), preferred_element_type=F32
    )


def column_sum(values):
    return jnp.sum(values, axis=0, keepdims=True)


def row_mean(values):
    return jnp.mean(values, axis=-1, keepdims=True)


def normalized(values):
    centred = values - row_mean(values)
    scale = lax.rsqrt(row_mean(centred * centred) + EPS)
    return centred * scale, scale


def place(index, size):
    return pl.multiple_of(index * size, size)


def start_of(row, first, total):
    return jnp.where(row < first, 0, jnp.where(row < total, first, row))


def call(body, name, operands, outs, scratch=(), scalars=1, micros=2, mib=12, far=()):
    return pl.pallas_call(
        body,
        cost_estimate=pl.CostEstimate(flops=int(micros * 1.1e9), bytes_accessed=0, transcendentals=0),
        out_shape=[
            pltpu.HBM(item.shape, item.dtype) if n in far else item for n, item in enumerate(outs)
        ],
        in_specs=[SMEM] * scalars + [VMEM] * (len(operands) - scalars),
        out_specs=[
            HBM if n in far else SMEM if item.dtype == jnp.int32 else VMEM
            for n, item in enumerate(outs)
        ],
        scratch_shapes=list(scratch),
        compiler_params=pltpu.CompilerParams(vmem_limit_bytes=mib << 20),
        name=name,
    )(*operands)


def shape(*dims, dtype=BF16):
    return jax.ShapeDtypeStruct(dims, dtype)


def project(tok, params, weights):
    unit, _ = normalized(tok[...].astype(F32))
    normed = (unit * params[0:1, :] + params[1:2, :]).astype(BF16)
    q, key, v = [dot(normed, weights[c]).astype(BF16) for c in range(3)]
    return unit.astype(BF16), q * BF16(0.125), key, v


def attend(info, i, count, last, fresh, block, queries_t, keys, values_t, state):
    first, total = info[1], info[2]
    acc, sum_row, top_row = state
    width = acc.shape[0]
    base = i * block
    head = lax.broadcasted_iota(jnp.int32, (width, block), 0) // HD
    q_heads = [jnp.where(head == h, queries_t, BF16(0)) for h in range(width // HD)]
    row = base + lax.broadcasted_iota(jnp.int32, (1, block), 1)
    start = start_of(row, first, total)
    last_start = start_of(base + block - 1, first, total)

    @pl.when(fresh)
    def _():
        acc[...] = jnp.zeros_like(acc)
        sum_row[...] = jnp.zeros_like(sum_row)
        top_row[...] = jnp.full_like(top_row, NEGATIVE)

    def step(j, masked):
        at = place(j, block)
        key_rows = keys(j)
        for h in range(width // HD):
            part = slice(HD * h, HD * h + HD)
            scores = dot(key_rows, q_heads[h])
            if masked:
                col = at + lax.broadcasted_iota(jnp.int32, (block, block), 0)
                scores = jnp.where((col >= start) & (col <= row), scores, NEGATIVE)
            before = top_row[h : h + 1, :]
            top = jnp.maximum(before, jnp.max(scores, axis=0, keepdims=True))
            fade = jnp.exp(before - top)
            exponent = jnp.exp(scores - top)
            mixed = dot(values_t(part, j), exponent.astype(BF16))
            sum_row[h : h + 1, :] = sum_row[h : h + 1, :] * fade + column_sum(exponent)
            acc[part, :] = acc[part, :] * fade + mixed
            top_row[h : h + 1, :] = top

    def loop(n, carry):
        j = last - n
        masked = (j == i) | (j * block < last_start)

        @pl.when(masked)
        def _():
            step(j, True)

        @pl.when(jnp.logical_not(masked))
        def _():
            step(j, False)

        return carry

    lax.fori_loop(0, count, loop, 0)


def lowest_block(info, i, block):
    return start_of(i * block, info[1], info[2]) // block


def sequences(lengths, owners, info):
    here = lax.axis_index("dp")

    def entry(e, carry):
        first, seen, total = carry
        mine = owners[e] == here
        length = jnp.where(mine, lengths[e], 0)
        first = jnp.where(seen == 0, length, first)
        return first, seen + mine.astype(jnp.int32), total + length

    zero = jnp.int32(0)
    first, seen, total = lax.fori_loop(0, lengths.shape[0], entry, (zero, zero, zero))
    info[0] = lax.axis_index("tensor")
    info[1] = first
    info[2] = total
    info[3] = here % PARTS


def attend_near(
    lengths, owners, t0, t1, params, weights,
    info, unit_out, q_out, k_out, v_out, qt_out, kt_out, vt_out, acc, sum_row, top_row,
):
    sequences(lengths, owners, info)
    me = info[0]
    rows = t0.shape[0]
    for k, tok in enumerate((t0, t1)):
        at = place((me ^ k) % 2, rows)
        unit, q, key, v = project(tok, params, weights)
        unit_out[pl.ds(at, rows), :] = unit
        for out, turned, value in ((q_out, qt_out, q), (k_out, kt_out, key), (v_out, vt_out, v)):
            out[pl.ds(at, rows), :] = value
            turned[:, pl.ds(at, rows)] = value.T
    base = me // 2 * 2
    for n in range(2):
        i = base + n
        lanes = slice(n * rows, (n + 1) * rows)
        attend(
            info,
            i,
            i + 1 - jnp.maximum(lowest_block(info, i, rows), base),
            i,
            True,
            rows,
            qt_out[:, lanes],
            lambda j: k_out[pl.ds(place(j - base, rows), rows), :],
            lambda part, j: vt_out[part, pl.ds(place(j - base, rows), rows)],
            [ref.at[:, lanes] for ref in (acc, sum_row, top_row)],
        )


def attend_far(
    info, t2, t3, params, weights,
    unit_in, q_in, k_in, v_in, qt_in, kt_in, vt_in, acc_in, sum_in, top_in,
    unit_far, q_far, k_far, v_far, qt_far, kt_far, ot_far, lse_out, a0, a1, a2, a3,
    unit_new, q_new, k_new, v_new, qt_new, kt_new, keys, qt, vt, ot, acc, sum_row, top_row, done,
):
    me = info[0]
    rows = t2.shape[0]
    own = me // 2
    for k, tok in ((2, t2), (3, t3)):
        at = place((me ^ k) % 2, rows)
        unit, q, key, v = project(tok, params, weights)
        unit_new[pl.ds(at, rows), :] = unit
        q_new[pl.ds(at, rows), :] = q
        k_new[pl.ds(at, rows), :] = key
        v_new[pl.ds(at, rows), :] = v
        qt_new[:, pl.ds(at, rows)] = q.T
        kt_new[:, pl.ds(at, rows)] = key.T
        vt[:, pl.ds(place(me ^ k, rows), rows)] = v.T
    copies = []
    both = 2 * rows
    here, there = pl.ds(place(own, both), both), pl.ds(place(1 - own, both), both)
    for old, new, far in (
        (unit_in, unit_new, unit_far),
        (q_in, q_new, q_far),
        (k_in, k_new, k_far),
        (v_in, v_new, v_far),
    ):
        copies.append((old, far.at[here]))
        copies.append((new, far.at[there]))
    for old, new, far in ((qt_in, qt_new, qt_far), (kt_in, kt_new, kt_far)):
        copies.append((old, far.at[:, here]))
        copies.append((new, far.at[:, there]))
    copies.append((ot, ot_far))
    copies = [pltpu.make_async_copy(a, b, done.at[n]) for n, (a, b) in enumerate(copies)]
    for copy in copies[:-1]:
        copy.start()
    keys[here, :] = k_in[...]
    keys[there, :] = k_new[...]
    qt[:, here] = qt_in[...]
    qt[:, there] = qt_new[...]
    vt[:, here] = vt_in[...]

    def query_block(i, unused):
        other = i // 2 != own
        lanes = pl.ds(place(i, rows), rows)
        old = pl.ds(place(i % 2, rows), rows)
        lowest = lowest_block(info, i, rows)

        @pl.when(jnp.logical_not(other))
        def _():
            acc[...] = acc_in[:, old]
            sum_row[...] = sum_in[:, old]
            top_row[...] = top_in[:, old]

        attend(
            info,
            i,
            jnp.where(other, i + 1 - lowest, jnp.where(own == 1, jnp.maximum(2 - lowest, 0), 0)),
            jnp.where(other, i, 1),
            other,
            rows,
            qt[:, lanes],
            lambda j: keys[pl.ds(place(j, rows), rows), :],
            lambda part, j: vt[part, pl.ds(place(j, rows), rows)],
            (acc, sum_row, top_row),
        )
        for h in range(acc.shape[0] // HD):
            part = slice(HD * h, HD * h + HD)
            summed = sum_row[h : h + 1, :]
            ot[part, lanes] = acc[part, :] / summed
            lse_out[h : h + 1, lanes] = top_row[h : h + 1, :] + jnp.log(summed)
        return unused

    lax.fori_loop(0, 4, query_block, 0)
    copies[-1].start()
    for k, out in enumerate((a0, a1, a2, a3)):
        at = place(me ^ k, rows)
        out[...] = ot[:, pl.ds(at, rows)].T.astype(BF16)
    for copy in copies:
        copy.wait()


def live_rows(info, rows):
    row = info[0] * rows + lax.broadcasted_iota(jnp.int32, (rows, 1), 0)
    return (row < info[2]).astype(F32)


def put_parts(buf, base, grad, index, step, order, stride=None):
    for p in range(PARTS):
        at = base + order(p ^ index) * (step if stride is None else stride)
        buf[pl.ds(pl.multiple_of(at, 16), step), :] = grad[p * step : (p + 1) * step]


def hidden_block(pack, width, n2, gf_low):
    up, down = pack.at[0:width], pack.at[width + 16 : 2 * width + 16]
    pre = dot(n2, up[...]) + pack[width : width + 1, :].astype(F32)
    square = pre * pre
    th = jnp.tanh(GELU_C * pre * (1.0 + 0.044715 * square))
    half = 0.5 * (1.0 + th)
    hidden = (pre * half).astype(BF16)
    slope = half + 0.5 * GELU_C * pre * (1.0 - th * th) * (1.0 + 0.134145 * square)
    grad = dot(gf_low, down[...], 1, 1) * slope
    low = grad.astype(BF16)
    return hidden, low, column_sum(grad), dot(hidden, down[...]), dot(low, up[...], 1, 1)


def middle_first(
    info, p0, p1, p2, p3, o0, o1, o2, o3, tok, cot, w0, w1, params, gate_w, pass_w,
    n2_out, ffn_low, y_out, gate2_out, gate_out, mixed_out, ffn_out, gn2_out, vec, keep, send,
):
    me, index = info[0], info[3]
    gain, shift, out_b, gate_b, gain2, shift2, down_b, pass_b = [
        params[n : n + 1, :] for n in range(8)
    ]
    rows, width = tok.shape
    x = tok[...].astype(F32)
    unit, _ = normalized(x)
    n1 = (unit * gain + shift).astype(BF16)
    mixed = out_b
    for p, w in zip((p0, p1, p2, p3), (o0, o1, o2, o3)):
        mixed = mixed + dot(p[...], w[...])
    mixed_out[...] = mixed
    gate = jax.nn.sigmoid(dot(n1, gate_w[...]) + gate_b)
    gate_out[...] = gate
    y = gate * mixed + (1.0 - gate) * x
    y_out[...] = y
    unit2, _ = normalized(y)
    n2 = (unit2 * gain2 + shift2).astype(BF16)
    n2_out[...] = n2
    gate2 = jax.nn.sigmoid(dot(n2, pass_w[...]) + pass_b)
    gate2_out[...] = gate2
    gf = cot[...].astype(F32) * live_rows(info, rows) * gate2
    vec[...] = jnp.zeros_like(vec)
    vec[0:1, :] = column_sum(gf)
    gf_low = gf.astype(BF16)
    ffn_low[...] = gf_low
    n2_turned = n2.T
    ffn_turned = gf_low.T
    ffn, gn2 = down_b, 0.0
    for k, (pack, buf) in enumerate(((w0, keep), (w1, send))):
        hidden, low, columns, more_ffn, more_gn2 = hidden_block(pack, width, n2, gf_low)
        vec[pl.ds(8 + (me ^ k), 1), :] = columns
        ffn = ffn + more_ffn
        gn2 = gn2 + more_gn2
        step = width // PARTS
        put_parts(buf, 0, dot(ffn_turned, hidden).astype(BF16), index, step, reverse)
        put_parts(buf, width, dot(n2_turned, low).astype(BF16), index, step, reverse)
    ffn_out[...] = ffn
    gn2_out[...] = gn2


def middle_second(
    info, o0, o1, o2, o3, tok, cot, w2, w3, params, pass_w,
    n2_in, ffn_low, y_in, gate2_in, gate_in, mixed_in, ffn_in, gn2_in, vec_in,
    out, g0, g1, g2, g3, hid, pre_low, z2_low, z1_low, mixed_low, carry, vec,
    whole2, whole3,
):
    me = info[0]
    quarter = w2.shape[0] // WEIGHT_PARTS
    for part in range(WEIGHT_PARTS):
        at = place((info[3] ^ part) % WEIGHT_PARTS, quarter)
        for whole, parts in ((whole2, w2), (whole3, w3)):
            whole[pl.ds(at, quarter), :] = parts[part * quarter : (part + 1) * quarter]
    gain2 = params[4:5, :]
    rows, width = tok.shape
    n2, gf_low = n2_in[...], ffn_low[...]
    ffn, gn2 = ffn_in[...], gn2_in[...]
    vec[...] = vec_in[...]
    for n, pack in enumerate((whole2, whole3)):
        hidden, low, columns, more_ffn, more_gn2 = hidden_block(pack, width, n2, gf_low)
        hid[n] = hidden
        pre_low[n] = low
        vec[pl.ds(8 + (me ^ (2 + n)), 1), :] = columns
        ffn = ffn + more_ffn
        gn2 = gn2 + more_gn2
    live = live_rows(info, rows)
    gate2, y = gate2_in[...], y_in[...]
    out[...] = ((gate2 * ffn + (1.0 - gate2) * y) * live).astype(BF16)
    gy = cot[...].astype(F32) * live
    z2 = gy * gate2 * (ffn - y) * (1.0 - gate2)
    vec[1:2, :] = column_sum(z2)
    z2l = z2.astype(BF16)
    z2_low[...] = z2l
    gn2 = gn2 + dot(z2l, pass_w[...], 1, 1)
    unit2, scale2 = normalized(y)
    vec[2:3, :] = column_sum(gn2)
    vec[3:4, :] = column_sum(gn2 * unit2)
    g = gn2 * gain2
    gy1 = gy * (1.0 - gate2) + scale2 * (g - row_mean(g) - unit2 * row_mean(g * unit2))
    gate = gate_in[...]
    gm = gy1 * gate
    vec[4:5, :] = column_sum(gm)
    z1 = gm * (mixed_in[...] - tok[...].astype(F32)) * (1.0 - gate)
    vec[5:6, :] = column_sum(z1)
    z1_low[...] = z1.astype(BF16)
    gml = gm.astype(BF16)
    mixed_low[...] = gml
    carry[...] = gy1 * (1.0 - gate)
    for g_out, w in zip((g0, g1, g2, g3), (o0, o1, o2, o3)):
        g_out[...] = dot(gml, w[...], 1, 1).astype(BF16)


ORDER = [int(f"{p:03b}"[::-1], 2) for p in range(PARTS)]
UP_ORDER = [ORDER[p] for p in (0, 1, 4, 5, 2, 3, 6, 7)]
REST_ORDER = [((p >> 1) & 1) | ((p >> 2) << 1) | ((p & 1) << 2) for p in range(PARTS)]


def weight_grads(
    info, hid, pre_low, ffn_low, z2_low, n2, z1_low, mixed_low, tok, params, gate_w,
    p0, p1, p2, p3, vec_in,
    keep, send, vec,
    scratch_gate, scratch_pass,
):
    me, mine = info[0], info[3]
    gain, shift = params[0:1, :], params[1:2, :]
    width = tok.shape[1]
    heads = p0.shape[1]
    unit, _ = normalized(tok[...].astype(F32))
    n1 = (unit * gain + shift).astype(BF16)
    z1l = z1_low[...]
    step = width // PARTS
    small = heads // PARTS
    n2_turned = n2[...].T
    n1_turned = n1.T
    z2l = z2_low[...]
    gml = mixed_low[...]
    ffn_turned = ffn_low[...].T
    pieces = (p0, p1, p2, p3)
    scratch_gate[...] = dot(n1_turned, z1l)
    scratch_pass[...] = dot(n2_turned, z2l)
    for n, buf in enumerate((keep, send)):
        grad = dot(ffn_turned, hid[n]).astype(BF16)
        put_parts(buf, 0, grad, mine, step, reverse)
        grad = dot(n2_turned, pre_low[n]).astype(BF16)
        put_parts(buf, width, grad, mine, step, reverse)
    for k in range(4):
        buf = (keep, send)[k % 2]
        out_grad = dot(pieces[k][...], gml, 0, 0).astype(BF16)
        at = place(me ^ k, heads)
        rest = (out_grad,) + tuple(
            ref[pl.ds(at, heads), :].astype(BF16) for ref in (scratch_gate, scratch_pass)
        )
        for n, grad in enumerate(rest):
            base = 2 * width + (3 * (k // 2) + n) * small
            put_parts(buf, base, grad, mine, small, reverse_rest, 6 * small)
    dz = dot(z1l, gate_w[...], 1, 1)
    vec[...] = vec_in[...]
    vec[6:7, :] = column_sum(dz * unit)
    vec[7:8, :] = column_sum(dz)


def reverse_rest(part):
    return ((part & 2) << 1) | ((part & 1) << 1) | ((part >> 2) & 1)


def reverse(part):
    return ((part & 1) << 2) | (part & 2) | ((part >> 2) & 1)


def backward_blocks(lowest, info, q, k, v, qt, kt, lse, unit_low, weights, keep, send,
    up, upt, dqt, dk, dv, dots, moment, total_cols):
    me, first, total = info[0], info[1], info[2]
    rows = keep.shape[0]
    block = rows
    width = q.shape[1]
    heads = width // HD
    lane_head = lax.broadcasted_iota(jnp.int32, (block, width), 1) // HD
    row_head = lax.broadcasted_iota(jnp.int32, (width, block), 0) // HD

    def key_block(j, unused):
        at_k = place(j, block)
        keys = k[pl.ds(at_k, block), :]
        values = v[pl.ds(at_k, block), :]
        dk[...] = jnp.zeros_like(dk)
        dv[...] = jnp.zeros_like(dv)

        def step(at, masked):
            cols = pl.ds(at, block)
            scaled_t = qt[:, cols]
            scaled = q[pl.ds(at, block), :]
            ups = up[pl.ds(at, block), :]
            ups_t = upt[:, cols]
            for h in range(heads):
                part = slice(HD * h, HD * h + HD)
                scores = dot(keys, jnp.where(row_head == h, scaled_t, BF16(0)))
                if masked:
                    row = at + lax.broadcasted_iota(jnp.int32, (1, block), 1)
                    start = start_of(row, first, total)
                    col = at_k + lax.broadcasted_iota(jnp.int32, (block, block), 0)
                    scores = jnp.where((col >= start) & (col <= row), scores, NEGATIVE)
                probs = jnp.exp(scores - lse[h : h + 1, cols])
                grads = dot(values, jnp.where(row_head == h, ups_t, BF16(0)))
                score_grad = (probs * (grads - dots[h : h + 1, cols])).astype(BF16)
                dv[...] += dot(probs.astype(BF16), jnp.where(lane_head == h, ups, BF16(0)))
                dk[...] += dot(score_grad, jnp.where(lane_head == h, scaled, BF16(0)))
                dqt[part, cols] += dot(kt[part, pl.ds(at_k, block)], score_grad)

        def loop(i, carry):
            at = place(i, block)
            begin = start_of(at, first, total)
            last_start = start_of(at + block - 1, first, total)
            whole = (i > j) & (at_k >= last_start)

            @pl.when(whole)
            def _():
                step(at, False)

            @pl.when(jnp.logical_not(whole) & (at_k + block > begin))
            def _():
                step(at, True)

            return carry

        lax.fori_loop(j, 4, loop, 0)
        grads_t = (
            (dqt[:, pl.ds(at_k, block)] * 0.125).astype(BF16),
            dk[...].T.astype(BF16),
            dv[...].T.astype(BF16),
        )
        unit_rows = unit_low[pl.ds(at_k, block), :]
        spread = 0.0
        for c in range(3):
            spread = spread + dot(grads_t[c], weights[c], 0, 1)
            moment[c] += dot(grads_t[c], unit_rows)
            total_cols[c] += jnp.sum(grads_t[c].astype(F32), axis=1, keepdims=True)
        spread = spread.astype(BF16)
        even = (me ^ j) % 2 == 0

        @pl.when(even)
        def _():
            keep[...] = spread

        @pl.when(jnp.logical_not(even))
        def _():
            send[...] = spread

        return unused

    lax.fori_loop(lowest, lowest + 2, key_block, 0)


def attend_backward_first(
    info, q, k, v, qt, kt, ot, lse, gs, unit_low, weights,
    keep, send, up, upt, dots, dqt, moment, total_cols,
    dk, dv,
):
    me = info[0]
    rows = keep.shape[0]
    for n in range(4):
        at = place(me ^ n, rows)
        g = gs[n * rows : (n + 1) * rows, :]
        up[pl.ds(at, rows), :] = g
        upt[:, pl.ds(at, rows)] = g.T
    weighted = upt[...].astype(F32) * ot[...]
    for h in range(dots.shape[0]):
        dots[h : h + 1, :] = column_sum(weighted[HD * h : HD * h + HD])
    dqt[...] = jnp.zeros_like(dqt)
    moment[...] = jnp.zeros_like(moment)
    total_cols[...] = jnp.zeros_like(total_cols)
    backward_blocks(0, info, q, k, v, qt, kt, lse, unit_low, weights, keep, send,
        up, upt, dqt, dk, dv, dots, moment, total_cols)


def attend_backward_second(
    info, q, k, v, qt, kt, lse, unit_low, weights, up, upt, dots, dqt_in, moment_in, cols_in,
    params, vec_in,
    keep, send, heads_out, vec,
    dk, dv, dqt, moment, total_cols,
):
    mine = info[3]
    gain, shift = params[0:1, :], params[1:2, :]
    width = q.shape[1]
    half = dqt.shape[1] // 2
    dqt[:, half:] = dqt_in[:, half:]
    moment[...] = moment_in[...]
    total_cols[...] = cols_in[...]
    backward_blocks(2, info, q, k, v, qt, kt, lse, unit_low, weights, keep, send,
        up, upt, dqt, dk, dv, dots, moment, total_cols)
    step_rows = width // PARTS
    part_rows = 3 * step_rows
    gain_grad = 0.0
    shift_grad = 0.0
    for c in range(3):
        turned = weights[c].astype(F32).T
        gain_grad = gain_grad + column_sum(turned * moment[c])
        shift_grad = shift_grad + column_sum(turned * total_cols[c])
        grad = (moment[c] * gain + total_cols[c] * shift).astype(BF16)
        for p in range(PARTS):
            at = pl.multiple_of(reverse(p ^ mine) * part_rows + c * step_rows, 16)
            heads_out[pl.ds(at, step_rows), :] = grad[p * step_rows : (p + 1) * step_rows]
    pick = lax.broadcasted_iota(jnp.int32, vec_in.shape, 0)
    sums = vec_in[...] + jnp.where(pick == 6, gain_grad, 0.0) + jnp.where(pick == 7, shift_grad, 0.0)
    vec[...] = sums.astype(BF16)


def tokens_backward(tok, own, got, z1_low, gate_w, carry, params, out):
    unit, scale = normalized(tok[...].astype(F32))
    grad = own[...].astype(F32) + got[...].astype(F32) + dot(z1_low[...], gate_w[...], 1, 1)
    h = grad * params[0:1, :]
    out[...] = (
        carry[...] + scale * (h - row_mean(h) - unit * row_mean(h * unit))
    ).astype(BF16)


def each_part(info, refs, rows, order=ORDER):
    pos = 0
    for ref in refs:
        for n in range(ref.shape[0] // rows):
            yield order[pos] ^ info[3], ref, n * rows
            pos += 1


def unpack_ffn(info, d0, d1, d2, u0, u1, u2, down, up, turned):
    step = down.shape[0] // PARTS
    for p, ref, at in each_part(info, (d0, d1, d2), step):
        turned[pl.ds(place(p, step), step), :] = ref[at : at + step].astype(F32)
    for p, ref, at in each_part(info, (u0, u1, u2), step, UP_ORDER):
        up[pl.ds(place(p, step), step), :] = ref[at : at + step].astype(F32)
    down[...] = turned[...].T


def unpack_rest(info, s0, s1, s2, out, gates):
    rows = out.shape[0]
    step = rows // PARTS
    for p, ref, at in each_part(info, (s0, s1, s2), 3 * step, REST_ORDER):
        out[pl.ds(place(p, step), step), :] = ref[at : at + step].astype(F32)
        for n in range(2):
            first = at + (n + 1) * step
            gates[pl.ds(pl.multiple_of(n * rows + p * step, step), step), :] = ref[
                first : first + step
            ]


def unpack_heads(info, s0, s1, s2, heads, turned):
    step = heads.shape[2] // PARTS
    for p, ref, at in each_part(info, (s0, s1, s2), 3 * step):
        for c in range(3):
            turned[c, pl.ds(place(p, step), step), :] = ref[at + c * step : at + (c + 1) * step].astype(F32)
    for c in range(3):
        heads[c] = turned[c].T


def unpack_gates(info, s0, s1, s2, s3, gate, passed):
    rows = gate.shape[0] // 4
    for k, ref in enumerate((s0, s1, s2, s3)):
        at = place(info[0] ^ k, rows)
        gate[pl.ds(at, rows), :] = ref[0:rows].astype(F32)
        passed[pl.ds(at, rows), :] = ref[rows : 2 * rows].astype(F32)


def unpack_vectors(info, one, two, *outs):
    sums = one[...] + two[...]
    for n in range(8):
        outs[n][...] = sums[n : n + 1]
    pick = lax.broadcasted_iota(jnp.int32, sums.shape, 0) == 8 + info[0]
    outs[8][...] = column_sum(jnp.where(pick, sums, 0.0))


def swap_tensor(values, mask):
    return lax.ppermute(values, "tensor", [(i, i ^ mask) for i in range(4)])


def swap_dp(values, mask):
    return lax.ppermute(values, "dp", [(i, i ^ mask) for i in range(lax.axis_size("dp"))])


def fold(*terms):
    return sum(term.astype(F32) for term in terms).astype(BF16)


def scatter(values, axis, mask):
    half = values.shape[0] // 2
    got = yield values[half:], axis, mask
    return fold(values[:half], got)


def reduce_dp(values, masks, more=None):
    extra = 0 if more is None else more.shape[0]
    for mask in masks:
        half = values.shape[0] // 2
        sent = values[half:]
        if extra:
            sent = jnp.concatenate([sent, more])
        got = yield sent, "dp", mask
        values = fold(values[:half], got[:half])
        if extra:
            more = fold(more, got[half:])
    mask = 4
    while mask < lax.axis_size("dp"):
        size = values.shape[0]
        if mask == 4:
            sent = [values[size // 2 :], values[: size // 2]]
        else:
            sent = [values]
        if extra:
            sent = sent + [more]
        got = yield jnp.concatenate(sent), "dp", mask
        values = fold(values, got[:size])
        if extra:
            more = fold(more, got[size:])
        mask *= 2
    return (values, more) if extra else values


def gather_dp(values, masks=(2, 1)):
    s2 = yield values, "dp", masks[0]
    s3 = yield jnp.concatenate([values, s2]), "dp", masks[1]
    return values, s2, s3


def split_rest(values):
    step = values.shape[0] // PARTS
    shares = [values[n * step : (n + 1) * step] for n in range(PARTS)]
    return jnp.concatenate(shares[0::2]), jnp.concatenate(shares[1::2])


def run_chains(chains):
    results = [None] * len(chains)
    waiting = [None] * len(chains)
    alive = list(range(len(chains)))
    while alive:
        for n in list(alive):
            try:
                values, axis, mask = chains[n].send(waiting[n])
            except StopIteration as stop:
                results[n] = stop.value
                alive.remove(n)
                continue
            waiting[n] = (swap_dp if axis == "dp" else swap_tensor)(values, mask)
    return results


def body(
    tokens,
    norm_gain,
    norm_shift,
    heads_weight,
    output_weight,
    output_bias,
    gate_weight,
    gate_bias,
    second_gain,
    second_shift,
    up_weight,
    up_bias,
    down_weight,
    down_bias,
    pass_weight,
    pass_bias,
    lengths,
    owners,
    cotangent,
):
    rows, width = tokens.shape
    total_rows = 4 * rows
    head_width = heads_weight.shape[2]
    me = lax.axis_index("tensor")
    params = jnp.stack(
        [norm_gain, norm_shift, output_bias, gate_bias, second_gain, second_shift]
        + [down_bias, pass_bias]
    )
    split_heads = heads_weight.transpose(1, 0, 2)

    def kept(count):
        kinds = [shape(count, width)] + [shape(count, head_width)] * 3
        return kinds + [shape(head_width, count)] * 2

    tok2 = swap_tensor(tokens, 2)
    tok1 = swap_tensor(tokens, 1)
    state = [(head_width, 2 * rows), (8, 2 * rows), (8, 2 * rows)]
    info, *near = call(
        attend_near,
        "attend_near",
        (lengths, owners, tokens, tok1, params, split_heads),
        [shape(4, dtype=jnp.int32)]
        + kept(2 * rows)
        + [shape(head_width, 2 * rows)]
        + [shape(*dims, dtype=F32) for dims in state],
        scalars=2,
        micros=6,
        mib=12,
    )
    up_held, down_held, info = lax.optimization_barrier((up_weight, down_weight, info))
    bias_rows = jnp.broadcast_to(up_bias[None, :], (16, width))
    pack0 = jnp.concatenate([up_held, bias_rows, down_held, jnp.zeros((48, width), BF16)])
    quarter = pack0.shape[0] // WEIGHT_PARTS
    sent = lax.dynamic_slice_in_dim(
        pack0, lax.axis_index("dp") % WEIGHT_PARTS * quarter, quarter, 0
    )
    sent, out_held, tok2, *near = lax.optimization_barrier((sent, output_weight, tok2, *near))
    out2 = swap_tensor(out_held, 2)
    part0 = swap_tensor(sent, 2)
    tok3 = swap_tensor(tok2, 1)

    later = kept(total_rows) + [shape(head_width, total_rows, dtype=F32)]
    unit, q, key, v, qt, kt, ot, lse, a0, a1, a2, a3 = call(
        attend_far,
        "attend_far",
        (info, tok2, tok3, params, split_heads) + tuple(near),
        later
        + [shape(head_width // HD, total_rows, dtype=F32)]
        + [shape(rows, head_width)] * 4,
        [pltpu.VMEM(item.shape, item.dtype) for item in kept(2 * rows)]
        + [
            pltpu.VMEM((total_rows, head_width), BF16),
            pltpu.VMEM((head_width, total_rows), BF16),
            pltpu.VMEM((head_width, total_rows), BF16),
            pltpu.VMEM((head_width, total_rows), F32),
        ]
        + [pltpu.VMEM((dims[0], rows), F32) for dims in state]
        + [pltpu.SemaphoreType.DMA((13,))],
        micros=10,
        mib=20,
        far=range(len(later)),
    )
    a0, a1, a2, a3, out2, part0, pack0, out_held = lax.optimization_barrier(
        (a0, a1, a2, a3, out2, part0, pack0, output_weight)
    )
    pack1 = swap_tensor(pack0, 1)
    out1 = swap_tensor(out_held, 1)
    out3 = swap_tensor(out2, 1)
    p0, p1, p2, p3 = a0, swap_tensor(a1, 1), swap_tensor(a2, 2), swap_tensor(a3, 3)
    part1, part2 = swap_dp(part0, 1), swap_dp(part0, 2)
    p1, p2, p3, out3, part1, part2 = lax.optimization_barrier((p1, p2, p3, out3, part1, part2))
    part3 = swap_dp(part2, 1)
    outs = (output_weight, out1, out2, out3)
    square, square32 = shape(rows, width), shape(rows, width, dtype=F32)
    n2, ffn_low, y, gate2, gate, mixed, ffn, gn2, vec, keep0, send0 = call(
        middle_first,
        "middle_first",
        (info, p0, p1, p2, p3) + outs + (tokens, cotangent, pack0, pack1, params)
        + (gate_weight, pass_weight),
        [square] * 2
        + [square32] * 6
        + [shape(16, width, dtype=F32)]
        + [shape(2 * width, width)] * 2,
        micros=9,
        mib=20,
    )
    n2, part3, send0 = lax.optimization_barrier((n2, part3, send0))
    parts2 = jnp.concatenate([part0, part1, part2, part3])
    parts3 = swap_tensor(parts2, 1)
    got0 = swap_tensor(send0, 1)
    output, g0, g1, g2, g3, hid, pre_low, z2_low, z1_low, mixed_low, carry, vec = call(
        middle_second,
        "middle_second",
        (info,) + outs + (tokens, cotangent, parts2, parts3, params, pass_weight)
        + (n2, ffn_low, y, gate2, gate, mixed, ffn, gn2, vec),
        [square]
        + [shape(rows, head_width)] * 4
        + [shape(2, rows, width)] * 2
        + [square] * 3
        + [square32, shape(16, width, dtype=F32)],
        [pltpu.VMEM(pack0.shape, BF16)] * 2,
        micros=7,
        mib=20,
    )
    g1, g2, g3 = swap_tensor(g1, 1), swap_tensor(g2, 2), swap_tensor(g3, 3)
    keep, send, vec = call(
        weight_grads,
        "weight_grads",
        (info, hid, pre_low, ffn_low, z2_low, n2, z1_low, mixed_low, tokens, params)
        + (gate_weight, p0, p1, p2, p3, vec),
        [shape(2 * width + 6 * head_width, width)] * 2
        + [shape(16, width, dtype=F32)],
        [pltpu.VMEM((width, width), F32)] * 2,
        micros=4,
        mib=14,
    )
    g1, g2, g3, got0, keep, send, vec = lax.optimization_barrier(
        (g1, g2, g3, got0, keep, send, vec)
    )
    got = swap_tensor(send, 1)
    near = fold(keep0, got0)
    total = fold(keep, got)
    half = width // 2
    down0, up_keep = near[:width], near[width:]
    down2, up_send = total[:width], total[width : 2 * width]
    rest = total[2 * width :]
    down_send = jnp.concatenate([down0[half:], down2[half:]])
    down_keep = jnp.concatenate([down0[:half], down2[:half]])
    half = rest.shape[0] // 2
    down_send, up_send, rest_send, vec = lax.optimization_barrier(
        (down_send, up_send, rest[half:], vec)
    )
    down_got = swap_dp(down_send, 1)
    up_got = swap_tensor(up_send, 2)
    rest_got = swap_dp(rest_send, 2)
    blocks = [pltpu.VMEM((rows, head_width), F32)] * 2
    totals = [(head_width, total_rows), (3, head_width, width), (3, head_width, 1)]
    rows_keep0, rows_send0, up, upt, dots, dqt, moment, total_cols = call(
        attend_backward_first,
        "attend_backward_first",
        (info, q, key, v, qt, kt, ot, lse, jnp.concatenate([g0, g1, g2, g3]), unit, split_heads),
        [square] * 2
        + [shape(total_rows, head_width), shape(head_width, total_rows)]
        + [shape(head_width // HD, total_rows, dtype=F32)]
        + [shape(*dims, dtype=F32) for dims in totals],
        blocks,
        micros=12,
        mib=12,
    )
    rows_keep0, rows_send0, dqt, down_got, up_got, rest_got = lax.optimization_barrier(
        (rows_keep0, rows_send0, dqt, down_got, up_got, rest_got)
    )
    down_part = fold(down_keep, down_got)
    up_part = fold(up_keep, up_got)
    rest = fold(rest[:half], rest_got)
    half = down_part.shape[0] // 2
    down_send, up_send, dqt = lax.optimization_barrier((down_part[half:], up_part[half:], dqt))
    down_got = swap_tensor(down_send, 2)
    up_got = swap_dp(up_send, 1)
    rest_kept, rest_sent = split_rest(rest)
    rest_got = swap_tensor(rest_sent, 2)
    rows_got0 = swap_tensor(rows_send0, 1)
    keep1, send1, heads_sum, vec = call(
        attend_backward_second,
        "attend_backward_second",
        (info, q, key, v, qt, kt, lse, unit, split_heads, up, upt, dots, dqt, moment)
        + (total_cols, params, vec),
        [square] * 2 + [shape(3 * head_width, width), shape(16, width)],
        blocks + [pltpu.VMEM(dims, F32) for dims in totals],
        micros=7,
        mib=12,
    )
    down_got, up_got, rest_got, rows_got0, heads_sum, vec, keep1, send1 = lax.optimization_barrier(
        (down_got, up_got, rest_got, rows_got0, heads_sum, vec, keep1, send1)
    )

    down_part, up_part = fold(down_part[:half], down_got), fold(up_part[:half], up_got)
    step = width // PARTS
    both = jnp.concatenate(
        [
            piece[n * step : (n + 1) * step]
            for n in range(PARTS // 2)
            for piece in (down_part, up_part)
        ]
    )

    def heads_chain(values, vec):
        values, vec = yield from reduce_dp(values, (1, 2), vec)
        vec = vec.astype(F32)
        s2 = yield values, "dp", 2
        got = yield vec, "tensor", 1
        vec = vec + got
        got = yield vec, "tensor", 2
        vectors = call(
            unpack_vectors,
            "unpack_vectors",
            (info, vec, got),
            [shape(1, width, dtype=F32)] * 9,
        )
        s3 = yield jnp.concatenate([values, s2]), "dp", 1
        (heads_grad,) = call(
            unpack_heads,
            "unpack_heads",
            (info, values, s2, s3),
            [shape(3, width, head_width, dtype=F32)],
            [pltpu.VMEM((3, head_width, width), F32)],
        )
        return heads_grad, [v.reshape(width) for v in vectors]

    def rows_chain():
        got = yield send1, "tensor", 1
        lower, upper = fold(rows_keep0, rows_got0), fold(keep1, got)
        is_lower = me < 2
        near = jnp.where(is_lower, lower, upper)
        far = yield jnp.where(is_lower, upper, lower), "tensor", 2
        return call(
            tokens_backward,
            "tokens_backward",
            (tokens, near, far, z1_low, gate_weight, carry, params),
            [square],
            scalars=0,
        )[0]

    def rest_chain(values):
        values = yield from reduce_dp(values, (1,))
        parts = yield from gather_dp(values, (1, 2))
        out_grad, gates = call(
            unpack_rest,
            "unpack_rest",
            (info,) + parts,
            [shape(head_width, width, dtype=F32), shape(2 * head_width, width)],
        )
        gates2 = yield gates, "tensor", 2
        other = yield jnp.concatenate([gates, gates2]), "tensor", 1
        gate_grad, pass_grad = call(
            unpack_gates,
            "unpack_gates",
            (info, gates, other[: 2 * head_width], gates2, other[2 * head_width :]),
            [shape(width, width, dtype=F32)] * 2,
        )
        return out_grad, gate_grad, pass_grad

    def ffn_chain(values):
        values = yield from reduce_dp(values, (2,))
        d0 = jnp.concatenate([values[:step], values[2 * step : 3 * step]])
        u0 = jnp.concatenate([values[step : 2 * step], values[3 * step :]])
        d1 = yield d0, "dp", 2
        u1 = yield u0, "dp", 1
        d2 = yield jnp.concatenate([d0, d1]), "dp", 1
        u2 = yield jnp.concatenate([u0, u1]), "dp", 2
        return d0, d1, d2, u0, u1, u2

    (tokens_grad,) = run_chains([rows_chain()])
    (
        (out_grad, gate_grad, pass_grad),
        ffn_parts,
        (heads_grad, vectors),
    ) = run_chains(
        [
            rest_chain(fold(rest_kept, rest_got)),
            ffn_chain(both),
            heads_chain(heads_sum, vec),
        ]
    )
    down_grad, up_grad = call(
        unpack_ffn,
        "unpack_ffn",
        (info,) + ffn_parts,
        [shape(width, width, dtype=F32)] * 2,
        [pltpu.VMEM((width, width), F32)],
    )
    (
        down_bias_grad,
        pass_bias_grad,
        second_shift_grad,
        second_gain_grad,
        output_bias_grad,
        gate_bias_grad,
        norm_gain_grad,
        norm_shift_grad,
        up_bias_grad,
    ) = vectors
    return (
        output,
        tokens_grad,
        norm_gain_grad,
        norm_shift_grad,
        heads_grad.transpose(1, 0, 2),
        out_grad,
        output_bias_grad,
        gate_grad,
        gate_bias_grad,
        second_gain_grad,
        second_shift_grad,
        up_grad,
        up_bias_grad,
        down_grad,
        down_bias_grad,
        pass_grad,
        pass_bias_grad,
    )


def solution(mesh):
    placed = (
        P(("dp", "tensor"), None),
        P(),
        P(),
        P(None, None, "tensor"),
        P("tensor", None),
        P(),
        P(),
        P(),
        P(),
        P(),
        P(None, "tensor"),
        P("tensor"),
        P("tensor", None),
        P(),
        P(),
        P(),
        P(),
        P(),
        P(("dp", "tensor"), None),
    )
    return jax.shard_map(
        body,
        mesh=mesh,
        in_specs=placed,
        out_specs=(
            P(("dp", "tensor"), None),
            P(("dp", "tensor"), None),
            P(),
            P(),
            P(None, None, "tensor"),
            P("tensor", None),
            P(),
            P(),
            P(),
            P(),
            P(),
            P(None, "tensor"),
            P("tensor"),
            P("tensor", None),
            P(),
            P(),
            P(),
        ),
        check_vma=False,
    )
```

```python
import functools

import jax
import jax.numpy as jnp
from jax import lax
from jax.experimental import pallas as pl
from jax.experimental.pallas import tpu as pltpu
from jax.sharding import PartitionSpec as P

HD = 64
EPS = 1e-05
NEGATIVE = -1e30
GELU_C = 0.7978845608028654
F32 = jnp.float32
BF16 = jnp.bfloat16
VMEM = pl.BlockSpec(memory_space=pltpu.VMEM)
HBM = pl.BlockSpec(memory_space=pltpu.HBM)
SMEM = pl.BlockSpec(memory_space=pltpu.SMEM)
PARTS = 8
WEIGHT_PARTS = 4


def dot(left, right, left_dim=1, right_dim=0):
    return lax.dot_general(
        left, right, (((left_dim,), (right_dim,)), ((), ())), preferred_element_type=F32
    )


def column_sum(values):
    return jnp.sum(values, axis=0, keepdims=True)


def row_mean(values):
    return jnp.mean(values, axis=-1, keepdims=True)


def normalized(values):
    centred = values - row_mean(values)
    scale = lax.rsqrt(row_mean(centred * centred) + EPS)
    return centred * scale, scale


def place(index, size):
    return pl.multiple_of(index * size, size)


def start_of(row, first, total):
    return jnp.where(row < first, 0, jnp.where(row < total, first, row))


def call(body, name, operands, outs, scratch=(), scalars=1, micros=2, mib=12, far=()):
    return pl.pallas_call(
        body,
        cost_estimate=pl.CostEstimate(flops=int(micros * 1.1e9), bytes_accessed=0, transcendentals=0),
        out_shape=[
            pltpu.HBM(item.shape, item.dtype) if n in far else item for n, item in enumerate(outs)
        ],
        in_specs=[SMEM] * scalars + [VMEM] * (len(operands) - scalars),
        out_specs=[
            HBM if n in far else SMEM if item.dtype == jnp.int32 else VMEM
            for n, item in enumerate(outs)
        ],
        scratch_shapes=list(scratch),
        compiler_params=pltpu.CompilerParams(vmem_limit_bytes=mib << 20),
        name=name,
    )(*operands)


def shape(*dims, dtype=BF16):
    return jax.ShapeDtypeStruct(dims, dtype)


def project(tok, params, weights):
    unit, _ = normalized(tok[...].astype(F32))
    normed = (unit * params[0:1, :] + params[1:2, :]).astype(BF16)
    q, key, v = [dot(normed, weights[c]).astype(BF16) for c in range(3)]
    return unit.astype(BF16), q * BF16(0.125), key, v


def attend(info, i, count, last, fresh, block, queries_t, keys, values_t, state):
    first, total = info[1], info[2]
    acc, sum_row, top_row = state
    width = acc.shape[0]
    base = i * block
    head = lax.broadcasted_iota(jnp.int32, (width, block), 0) // HD
    q_heads = [jnp.where(head == h, queries_t, BF16(0)) for h in range(width // HD)]
    row = base + lax.broadcasted_iota(jnp.int32, (1, block), 1)
    start = start_of(row, first, total)
    last_start = start_of(base + block - 1, first, total)

    @pl.when(fresh)
    def _():
        acc[...] = jnp.zeros_like(acc)
        sum_row[...] = jnp.zeros_like(sum_row)
        top_row[...] = jnp.full_like(top_row, NEGATIVE)

    def step(j, masked):
        at = place(j, block)
        key_rows = keys(j)
        for h in range(width // HD):
            part = slice(HD * h, HD * h + HD)
            scores = dot(key_rows, q_heads[h])
            if masked:
                col = at + lax.broadcasted_iota(jnp.int32, (block, block), 0)
                scores = jnp.where((col >= start) & (col <= row), scores, NEGATIVE)
            before = top_row[h : h + 1, :]
            top = jnp.maximum(before, jnp.max(scores, axis=0, keepdims=True))
            fade = jnp.exp(before - top)
            exponent = jnp.exp(scores - top)
            mixed = dot(values_t(part, j), exponent.astype(BF16))
            sum_row[h : h + 1, :] = sum_row[h : h + 1, :] * fade + column_sum(exponent)
            acc[part, :] = acc[part, :] * fade + mixed
            top_row[h : h + 1, :] = top

    def loop(n, carry):
        j = last - n
        masked = (j == i) | (j * block < last_start)

        @pl.when(masked)
        def _():
            step(j, True)

        @pl.when(jnp.logical_not(masked))
        def _():
            step(j, False)

        return carry

    lax.fori_loop(0, count, loop, 0)


def lowest_block(info, i, block):
    return start_of(i * block, info[1], info[2]) // block


def sequences(lengths, owners, info):
    here = lax.axis_index("dp")

    def entry(e, carry):
        first, seen, total = carry
        mine = owners[e] == here
        length = jnp.where(mine, lengths[e], 0)
        first = jnp.where(seen == 0, length, first)
        return first, seen + mine.astype(jnp.int32), total + length

    zero = jnp.int32(0)
    first, seen, total = lax.fori_loop(0, lengths.shape[0], entry, (zero, zero, zero))
    info[0] = lax.axis_index("tensor")
    info[1] = first
    info[2] = total
    info[3] = here % PARTS


def attend_near(
    lengths, owners, t0, t1, params, weights,
    info, unit_out, q_out, k_out, v_out, qt_out, kt_out, vt_out, acc, sum_row, top_row,
):
    sequences(lengths, owners, info)
    me = info[0]
    rows = t0.shape[0]
    for k, tok in enumerate((t0, t1)):
        at = place((me ^ k) % 2, rows)
        unit, q, key, v = project(tok, params, weights)
        unit_out[pl.ds(at, rows), :] = unit
        for out, turned, value in ((q_out, qt_out, q), (k_out, kt_out, key), (v_out, vt_out, v)):
            out[pl.ds(at, rows), :] = value
            turned[:, pl.ds(at, rows)] = value.T
    base = me // 2 * 2
    for n in range(2):
        i = base + n
        lanes = slice(n * rows, (n + 1) * rows)
        attend(
            info,
            i,
            i + 1 - jnp.maximum(lowest_block(info, i, rows), base),
            i,
            True,
            rows,
            qt_out[:, lanes],
            lambda j: k_out[pl.ds(place(j - base, rows), rows), :],
            lambda part, j: vt_out[part, pl.ds(place(j - base, rows), rows)],
            [ref.at[:, lanes] for ref in (acc, sum_row, top_row)],
        )


def attend_far(
    info, t2, t3, params, weights,
    unit_in, q_in, k_in, v_in, qt_in, kt_in, vt_in, acc_in, sum_in, top_in,
    unit_far, q_far, k_far, v_far, qt_far, kt_far, ot_far, lse_out, a0, a1, a2, a3,
    unit_new, q_new, k_new, v_new, qt_new, kt_new, keys, qt, vt, ot, acc, sum_row, top_row, done,
):
    me = info[0]
    rows = t2.shape[0]
    own = me // 2
    for k, tok in ((2, t2), (3, t3)):
        at = place((me ^ k) % 2, rows)
        unit, q, key, v = project(tok, params, weights)
        unit_new[pl.ds(at, rows), :] = unit
        q_new[pl.ds(at, rows), :] = q
        k_new[pl.ds(at, rows), :] = key
        v_new[pl.ds(at, rows), :] = v
        qt_new[:, pl.ds(at, rows)] = q.T
        kt_new[:, pl.ds(at, rows)] = key.T
        vt[:, pl.ds(place(me ^ k, rows), rows)] = v.T
    copies = []
    both = 2 * rows
    here, there = pl.ds(place(own, both), both), pl.ds(place(1 - own, both), both)
    for old, new, far in (
        (unit_in, unit_new, unit_far),
        (q_in, q_new, q_far),
        (k_in, k_new, k_far),
        (v_in, v_new, v_far),
    ):
        copies.append((old, far.at[here]))
        copies.append((new, far.at[there]))
    for old, new, far in ((qt_in, qt_new, qt_far), (kt_in, kt_new, kt_far)):
        copies.append((old, far.at[:, here]))
        copies.append((new, far.at[:, there]))
    copies.append((ot, ot_far))
    copies = [pltpu.make_async_copy(a, b, done.at[n]) for n, (a, b) in enumerate(copies)]
    for copy in copies[:-1]:
        copy.start()
    keys[here, :] = k_in[...]
    keys[there, :] = k_new[...]
    qt[:, here] = qt_in[...]
    qt[:, there] = qt_new[...]
    vt[:, here] = vt_in[...]

    def query_block(i, unused):
        other = i // 2 != own
        lanes = pl.ds(place(i, rows), rows)
        old = pl.ds(place(i % 2, rows), rows)
        lowest = lowest_block(info, i, rows)

        @pl.when(jnp.logical_not(other))
        def _():
            acc[...] = acc_in[:, old]
            sum_row[...] = sum_in[:, old]
            top_row[...] = top_in[:, old]

        attend(
            info,
            i,
            jnp.where(other, i + 1 - lowest, jnp.where(own == 1, jnp.maximum(2 - lowest, 0), 0)),
            jnp.where(other, i, 1),
            other,
            rows,
            qt[:, lanes],
            lambda j: keys[pl.ds(place(j, rows), rows), :],
            lambda part, j: vt[part, pl.ds(place(j, rows), rows)],
            (acc, sum_row, top_row),
        )
        for h in range(acc.shape[0] // HD):
            part = slice(HD * h, HD * h + HD)
            summed = sum_row[h : h + 1, :]
            ot[part, lanes] = acc[part, :] / summed
            lse_out[h : h + 1, lanes] = top_row[h : h + 1, :] + jnp.log(summed)
        return unused

    lax.fori_loop(0, 4, query_block, 0)
    copies[-1].start()
    for k, out in enumerate((a0, a1, a2, a3)):
        at = place(me ^ k, rows)
        out[...] = ot[:, pl.ds(at, rows)].T.astype(BF16)
    for copy in copies:
        copy.wait()


def live_rows(info, rows):
    row = info[0] * rows + lax.broadcasted_iota(jnp.int32, (rows, 1), 0)
    return (row < info[2]).astype(F32)


def put_parts(buf, base, grad, index, step, order, stride=None):
    for p in range(PARTS):
        at = base + order(p ^ index) * (step if stride is None else stride)
        buf[pl.ds(pl.multiple_of(at, 16), step), :] = grad[p * step : (p + 1) * step]


def hidden_block(pack, width, n2, gf_low):
    up, down = pack.at[0:width], pack.at[width + 16 : 2 * width + 16]
    pre = dot(n2, up[...]) + pack[width : width + 1, :].astype(F32)
    square = pre * pre
    th = jnp.tanh(GELU_C * pre * (1.0 + 0.044715 * square))
    half = 0.5 * (1.0 + th)
    hidden = (pre * half).astype(BF16)
    slope = half + 0.5 * GELU_C * pre * (1.0 - th * th) * (1.0 + 0.134145 * square)
    grad = dot(gf_low, down[...], 1, 1) * slope
    low = grad.astype(BF16)
    return hidden, low, column_sum(grad), dot(hidden, down[...]), dot(low, up[...], 1, 1)


def middle_first(
    info, p0, p1, p2, p3, o0, o1, o2, o3, tok, cot, w0, w1, params, gate_w, pass_w,
    n2_out, ffn_low, y_out, gate2_out, gate_out, mixed_out, ffn_out, gn2_out, vec, keep, send,
):
    me, index = info[0], info[3]
    gain, shift, out_b, gate_b, gain2, shift2, down_b, pass_b = [
        params[n : n + 1, :] for n in range(8)
    ]
    rows, width = tok.shape
    x = tok[...].astype(F32)
    unit, _ = normalized(x)
    n1 = (unit * gain + shift).astype(BF16)
    mixed = out_b
    for p, w in zip((p0, p1, p2, p3), (o0, o1, o2, o3)):
        mixed = mixed + dot(p[...], w[...])
    mixed_out[...] = mixed
    gate = jax.nn.sigmoid(dot(n1, gate_w[...]) + gate_b)
    gate_out[...] = gate
    y = gate * mixed + (1.0 - gate) * x
    y_out[...] = y
    unit2, _ = normalized(y)
    n2 = (unit2 * gain2 + shift2).astype(BF16)
    n2_out[...] = n2
    gate2 = jax.nn.sigmoid(dot(n2, pass_w[...]) + pass_b)
    gate2_out[...] = gate2
    gf = cot[...].astype(F32) * live_rows(info, rows) * gate2
    vec[...] = jnp.zeros_like(vec)
    vec[0:1, :] = column_sum(gf)
    gf_low = gf.astype(BF16)
    ffn_low[...] = gf_low
    n2_turned = n2.T
    ffn_turned = gf_low.T
    ffn, gn2 = down_b, 0.0
    for k, (pack, buf) in enumerate(((w0, keep), (w1, send))):
        hidden, low, columns, more_ffn, more_gn2 = hidden_block(pack, width, n2, gf_low)
        vec[pl.ds(8 + (me ^ k), 1), :] = columns
        ffn = ffn + more_ffn
        gn2 = gn2 + more_gn2
        step = width // PARTS
        put_parts(buf, 0, dot(ffn_turned, hidden).astype(BF16), index, step, reverse)
        put_parts(buf, width, dot(n2_turned, low).astype(BF16), index, step, reverse)
    ffn_out[...] = ffn
    gn2_out[...] = gn2


def middle_second(
    info, o0, o1, o2, o3, tok, cot, w2, w3, params, pass_w,
    n2_in, ffn_low, y_in, gate2_in, gate_in, mixed_in, ffn_in, gn2_in, vec_in,
    out, g0, g1, g2, g3, hid, pre_low, z2_low, z1_low, mixed_low, carry, vec,
    whole2, whole3,
):
    me = info[0]
    quarter = w2.shape[0] // WEIGHT_PARTS
    for part in range(WEIGHT_PARTS):
        at = place((info[3] ^ part) % WEIGHT_PARTS, quarter)
        for whole, parts in ((whole2, w2), (whole3, w3)):
            whole[pl.ds(at, quarter), :] = parts[part * quarter : (part + 1) * quarter]
    gain2 = params[4:5, :]
    rows, width = tok.shape
    n2, gf_low = n2_in[...], ffn_low[...]
    ffn, gn2 = ffn_in[...], gn2_in[...]
    vec[...] = vec_in[...]
    for n, pack in enumerate((whole2, whole3)):
        hidden, low, columns, more_ffn, more_gn2 = hidden_block(pack, width, n2, gf_low)
        hid[n] = hidden
        pre_low[n] = low
        vec[pl.ds(8 + (me ^ (2 + n)), 1), :] = columns
        ffn = ffn + more_ffn
        gn2 = gn2 + more_gn2
    live = live_rows(info, rows)
    gate2, y = gate2_in[...], y_in[...]
    out[...] = ((gate2 * ffn + (1.0 - gate2) * y) * live).astype(BF16)
    gy = cot[...].astype(F32) * live
    z2 = gy * gate2 * (ffn - y) * (1.0 - gate2)
    vec[1:2, :] = column_sum(z2)
    z2l = z2.astype(BF16)
    z2_low[...] = z2l
    gn2 = gn2 + dot(z2l, pass_w[...], 1, 1)
    unit2, scale2 = normalized(y)
    vec[2:3, :] = column_sum(gn2)
    vec[3:4, :] = column_sum(gn2 * unit2)
    g = gn2 * gain2
    gy1 = gy * (1.0 - gate2) + scale2 * (g - row_mean(g) - unit2 * row_mean(g * unit2))
    gate = gate_in[...]
    gm = gy1 * gate
    vec[4:5, :] = column_sum(gm)
    z1 = gm * (mixed_in[...] - tok[...].astype(F32)) * (1.0 - gate)
    vec[5:6, :] = column_sum(z1)
    z1_low[...] = z1.astype(BF16)
    gml = gm.astype(BF16)
    mixed_low[...] = gml
    carry[...] = gy1 * (1.0 - gate)
    for g_out, w in zip((g0, g1, g2, g3), (o0, o1, o2, o3)):
        g_out[...] = dot(gml, w[...], 1, 1).astype(BF16)


ORDER = [int(f"{p:03b}"[::-1], 2) for p in range(PARTS)]
UP_ORDER = [ORDER[p] for p in (0, 1, 4, 5, 2, 3, 6, 7)]
REST_ORDER = [((p >> 1) & 1) | ((p >> 2) << 1) | ((p & 1) << 2) for p in range(PARTS)]


def weight_grads(
    info, hid, pre_low, ffn_low, z2_low, n2, z1_low, mixed_low, tok, params, gate_w,
    p0, p1, p2, p3, vec_in,
    keep, send, vec,
    scratch_gate, scratch_pass,
):
    me, mine = info[0], info[3]
    gain, shift = params[0:1, :], params[1:2, :]
    width = tok.shape[1]
    heads = p0.shape[1]
    unit, _ = normalized(tok[...].astype(F32))
    n1 = (unit * gain + shift).astype(BF16)
    z1l = z1_low[...]
    step = width // PARTS
    small = heads // PARTS
    n2_turned = n2[...].T
    n1_turned = n1.T
    z2l = z2_low[...]
    gml = mixed_low[...]
    ffn_turned = ffn_low[...].T
    pieces = (p0, p1, p2, p3)
    scratch_gate[...] = dot(n1_turned, z1l)
    scratch_pass[...] = dot(n2_turned, z2l)
    for n, buf in enumerate((keep, send)):
        grad = dot(ffn_turned, hid[n]).astype(BF16)
        put_parts(buf, 0, grad, mine, step, reverse)
        grad = dot(n2_turned, pre_low[n]).astype(BF16)
        put_parts(buf, width, grad, mine, step, reverse)
    for k in range(4):
        buf = (keep, send)[k % 2]
        out_grad = dot(pieces[k][...], gml, 0, 0).astype(BF16)
        at = place(me ^ k, heads)
        rest = (out_grad,) + tuple(
            ref[pl.ds(at, heads), :].astype(BF16) for ref in (scratch_gate, scratch_pass)
        )
        for n, grad in enumerate(rest):
            base = 2 * width + (3 * (k // 2) + n) * small
            put_parts(buf, base, grad, mine, small, reverse_rest, 6 * small)
    dz = dot(z1l, gate_w[...], 1, 1)
    vec[...] = vec_in[...]
    vec[6:7, :] = column_sum(dz * unit)
    vec[7:8, :] = column_sum(dz)


def reverse_rest(part):
    return ((part & 2) << 1) | ((part & 1) << 1) | ((part >> 2) & 1)


def reverse(part):
    return ((part & 1) << 2) | (part & 2) | ((part >> 2) & 1)


def backward_blocks(lowest, info, q, k, v, qt, kt, lse, unit_low, weights, keep, send,
    up, upt, dqt, dk, dv, dots, moment, total_cols):
    me, first, total = info[0], info[1], info[2]
    rows = keep.shape[0]
    block = rows
    width = q.shape[1]
    heads = width // HD
    lane_head = lax.broadcasted_iota(jnp.int32, (block, width), 1) // HD
    row_head = lax.broadcasted_iota(jnp.int32, (width, block), 0) // HD

    def key_block(j, unused):
        at_k = place(j, block)
        keys = k[pl.ds(at_k, block), :]
        values = v[pl.ds(at_k, block), :]
        dk[...] = jnp.zeros_like(dk)
        dv[...] = jnp.zeros_like(dv)

        def step(at, masked):
            cols = pl.ds(at, block)
            scaled_t = qt[:, cols]
            scaled = q[pl.ds(at, block), :]
            ups = up[pl.ds(at, block), :]
            ups_t = upt[:, cols]
            for h in range(heads):
                part = slice(HD * h, HD * h + HD)
                scores = dot(keys, jnp.where(row_head == h, scaled_t, BF16(0)))
                if masked:
                    row = at + lax.broadcasted_iota(jnp.int32, (1, block), 1)
                    start = start_of(row, first, total)
                    col = at_k + lax.broadcasted_iota(jnp.int32, (block, block), 0)
                    scores = jnp.where((col >= start) & (col <= row), scores, NEGATIVE)
                probs = jnp.exp(scores - lse[h : h + 1, cols])
                grads = dot(values, jnp.where(row_head == h, ups_t, BF16(0)))
                score_grad = (probs * (grads - dots[h : h + 1, cols])).astype(BF16)
                dv[...] += dot(probs.astype(BF16), jnp.where(lane_head == h, ups, BF16(0)))
                dk[...] += dot(score_grad, jnp.where(lane_head == h, scaled, BF16(0)))
                dqt[part, cols] += dot(kt[part, pl.ds(at_k, block)], score_grad)

        def loop(i, carry):
            at = place(i, block)
            begin = start_of(at, first, total)
            last_start = start_of(at + block - 1, first, total)
            whole = (i > j) & (at_k >= last_start)

            @pl.when(whole)
            def _():
                step(at, False)

            @pl.when(jnp.logical_not(whole) & (at_k + block > begin))
            def _():
                step(at, True)

            return carry

        lax.fori_loop(j, 4, loop, 0)
        grads_t = (
            (dqt[:, pl.ds(at_k, block)] * 0.125).astype(BF16),
            dk[...].T.astype(BF16),
            dv[...].T.astype(BF16),
        )
        unit_rows = unit_low[pl.ds(at_k, block), :]
        spread = 0.0
        for c in range(3):
            spread = spread + dot(grads_t[c], weights[c], 0, 1)
            moment[c] += dot(grads_t[c], unit_rows)
            total_cols[c] += jnp.sum(grads_t[c].astype(F32), axis=1, keepdims=True)
        spread = spread.astype(BF16)
        even = (me ^ j) % 2 == 0

        @pl.when(even)
        def _():
            keep[...] = spread

        @pl.when(jnp.logical_not(even))
        def _():
            send[...] = spread

        return unused

    lax.fori_loop(lowest, lowest + 2, key_block, 0)


def attend_backward_first(
    info, q, k, v, qt, kt, ot, lse, gs, unit_low, weights,
    keep, send, up, upt, dots, dqt, moment, total_cols,
    dk, dv,
):
    me = info[0]
    rows = keep.shape[0]
    for n in range(4):
        at = place(me ^ n, rows)
        g = gs[n * rows : (n + 1) * rows, :]
        up[pl.ds(at, rows), :] = g
        upt[:, pl.ds(at, rows)] = g.T
    weighted = upt[...].astype(F32) * ot[...]
    for h in range(dots.shape[0]):
        dots[h : h + 1, :] = column_sum(weighted[HD * h : HD * h + HD])
    dqt[...] = jnp.zeros_like(dqt)
    moment[...] = jnp.zeros_like(moment)
    total_cols[...] = jnp.zeros_like(total_cols)
    backward_blocks(0, info, q, k, v, qt, kt, lse, unit_low, weights, keep, send,
        up, upt, dqt, dk, dv, dots, moment, total_cols)


def attend_backward_second(
    info, q, k, v, qt, kt, lse, unit_low, weights, up, upt, dots, dqt_in, moment_in, cols_in,
    params, vec_in,
    keep, send, heads_out, vec,
    dk, dv, dqt, moment, total_cols,
):
    mine = info[3]
    gain, shift = params[0:1, :], params[1:2, :]
    width = q.shape[1]
    half = dqt.shape[1] // 2
    dqt[:, half:] = dqt_in[:, half:]
    moment[...] = moment_in[...]
    total_cols[...] = cols_in[...]
    backward_blocks(2, info, q, k, v, qt, kt, lse, unit_low, weights, keep, send,
        up, upt, dqt, dk, dv, dots, moment, total_cols)
    step_rows = width // PARTS
    part_rows = 3 * step_rows
    gain_grad = 0.0
    shift_grad = 0.0
    for c in range(3):
        turned = weights[c].astype(F32).T
        gain_grad = gain_grad + column_sum(turned * moment[c])
        shift_grad = shift_grad + column_sum(turned * total_cols[c])
        grad = (moment[c] * gain + total_cols[c] * shift).astype(BF16)
        for p in range(PARTS):
            at = pl.multiple_of(reverse(p ^ mine) * part_rows + c * step_rows, 16)
            heads_out[pl.ds(at, step_rows), :] = grad[p * step_rows : (p + 1) * step_rows]
    pick = lax.broadcasted_iota(jnp.int32, vec_in.shape, 0)
    sums = vec_in[...] + jnp.where(pick == 6, gain_grad, 0.0) + jnp.where(pick == 7, shift_grad, 0.0)
    vec[...] = sums.astype(BF16)


def tokens_backward(tok, own, got, z1_low, gate_w, carry, params, out):
    unit, scale = normalized(tok[...].astype(F32))
    grad = own[...].astype(F32) + got[...].astype(F32) + dot(z1_low[...], gate_w[...], 1, 1)
    h = grad * params[0:1, :]
    out[...] = (
        carry[...] + scale * (h - row_mean(h) - unit * row_mean(h * unit))
    ).astype(BF16)


def each_part(info, refs, rows, order=ORDER):
    pos = 0
    for ref in refs:
        for n in range(ref.shape[0] // rows):
            yield order[pos] ^ info[3], ref, n * rows
            pos += 1


def unpack_ffn(info, d0, d1, d2, u0, u1, u2, down, up, turned):
    step = down.shape[0] // PARTS
    for p, ref, at in each_part(info, (d0, d1, d2), step):
        turned[pl.ds(place(p, step), step), :] = ref[at : at + step].astype(F32)
    for p, ref, at in each_part(info, (u0, u1, u2), step, UP_ORDER):
        up[pl.ds(place(p, step), step), :] = ref[at : at + step].astype(F32)
    down[...] = turned[...].T


def unpack_rest(info, s0, s1, s2, out, gates):
    rows = out.shape[0]
    step = rows // PARTS
    for p, ref, at in each_part(info, (s0, s1, s2), 3 * step, REST_ORDER):
        out[pl.ds(place(p, step), step), :] = ref[at : at + step].astype(F32)
        for n in range(2):
            first = at + (n + 1) * step
            gates[pl.ds(pl.multiple_of(n * rows + p * step, step), step), :] = ref[
                first : first + step
            ]


def unpack_heads(info, s0, s1, s2, heads, turned):
    step = heads.shape[2] // PARTS
    for p, ref, at in each_part(info, (s0, s1, s2), 3 * step):
        for c in range(3):
            turned[c, pl.ds(place(p, step), step), :] = ref[at + c * step : at + (c + 1) * step].astype(F32)
    for c in range(3):
        heads[c] = turned[c].T


def unpack_gates(info, s0, s1, s2, s3, gate, passed):
    rows = gate.shape[0] // 4
    for k, ref in enumerate((s0, s1, s2, s3)):
        at = place(info[0] ^ k, rows)
        gate[pl.ds(at, rows), :] = ref[0:rows].astype(F32)
        passed[pl.ds(at, rows), :] = ref[rows : 2 * rows].astype(F32)


def unpack_vectors(info, one, two, *outs):
    sums = one[...] + two[...]
    for n in range(8):
        outs[n][...] = sums[n : n + 1]
    pick = lax.broadcasted_iota(jnp.int32, sums.shape, 0) == 8 + info[0]
    outs[8][...] = column_sum(jnp.where(pick, sums, 0.0))


def swap_tensor(values, mask):
    return lax.ppermute(values, "tensor", [(i, i ^ mask) for i in range(4)])


def swap_dp(values, mask):
    return lax.ppermute(values, "dp", [(i, i ^ mask) for i in range(lax.axis_size("dp"))])


def fold(*terms):
    return sum(term.astype(F32) for term in terms).astype(BF16)


def scatter(values, axis, mask):
    half = values.shape[0] // 2
    got = yield values[half:], axis, mask
    return fold(values[:half], got)


def reduce_dp(values, masks, more=None):
    extra = 0 if more is None else more.shape[0]
    for mask in masks:
        half = values.shape[0] // 2
        sent = values[half:]
        if extra:
            sent = jnp.concatenate([sent, more])
        got = yield sent, "dp", mask
        values = fold(values[:half], got[:half])
        if extra:
            more = fold(more, got[half:])
    mask = 4
    while mask < lax.axis_size("dp"):
        size = values.shape[0]
        if mask == 4:
            sent = [values[size // 2 :], values[: size // 2]]
        else:
            sent = [values]
        if extra:
            sent = sent + [more]
        got = yield jnp.concatenate(sent), "dp", mask
        values = fold(values, got[:size])
        if extra:
            more = fold(more, got[size:])
        mask *= 2
    return (values, more) if extra else values


def gather_dp(values, masks=(2, 1)):
    s2 = yield values, "dp", masks[0]
    s3 = yield jnp.concatenate([values, s2]), "dp", masks[1]
    return values, s2, s3


def split_rest(values):
    step = values.shape[0] // PARTS
    shares = [values[n * step : (n + 1) * step] for n in range(PARTS)]
    return jnp.concatenate(shares[0::2]), jnp.concatenate(shares[1::2])


def run_chains(chains):
    results = [None] * len(chains)
    waiting = [None] * len(chains)
    alive = list(range(len(chains)))
    while alive:
        for n in list(alive):
            try:
                values, axis, mask = chains[n].send(waiting[n])
            except StopIteration as stop:
                results[n] = stop.value
                alive.remove(n)
                continue
            waiting[n] = (swap_dp if axis == "dp" else swap_tensor)(values, mask)
    return results


def body(
    tokens,
    norm_gain,
    norm_shift,
    heads_weight,
    output_weight,
    output_bias,
    gate_weight,
    gate_bias,
    second_gain,
    second_shift,
    up_weight,
    up_bias,
    down_weight,
    down_bias,
    pass_weight,
    pass_bias,
    lengths,
    owners,
    cotangent,
):
    rows, width = tokens.shape
    total_rows = 4 * rows
    head_width = heads_weight.shape[2]
    me = lax.axis_index("tensor")
    params = jnp.stack(
        [norm_gain, norm_shift, output_bias, gate_bias, second_gain, second_shift]
        + [down_bias, pass_bias]
    )
    split_heads = heads_weight.transpose(1, 0, 2)

    def kept(count):
        kinds = [shape(count, width)] + [shape(count, head_width)] * 3
        return kinds + [shape(head_width, count)] * 2

    tok2 = swap_tensor(tokens, 2)
    tok1 = swap_tensor(tokens, 1)
    state = [(head_width, 2 * rows), (8, 2 * rows), (8, 2 * rows)]
    info, *near = call(
        attend_near,
        "attend_near",
        (lengths, owners, tokens, tok1, params, split_heads),
        [shape(4, dtype=jnp.int32)]
        + kept(2 * rows)
        + [shape(head_width, 2 * rows)]
        + [shape(*dims, dtype=F32) for dims in state],
        scalars=2,
        micros=6,
        mib=12,
    )
    up_held, down_held, info = lax.optimization_barrier((up_weight, down_weight, info))
    bias_rows = jnp.broadcast_to(up_bias[None, :], (16, width))
    pack0 = jnp.concatenate([up_held, bias_rows, down_held, jnp.zeros((48, width), BF16)])
    quarter = pack0.shape[0] // WEIGHT_PARTS
    sent = lax.dynamic_slice_in_dim(
        pack0, lax.axis_index("dp") % WEIGHT_PARTS * quarter, quarter, 0
    )
    sent, out_held, tok2, *near = lax.optimization_barrier((sent, output_weight, tok2, *near))
    out2 = swap_tensor(out_held, 2)
    part0 = swap_tensor(sent, 2)
    tok3 = swap_tensor(tok2, 1)

    later = kept(total_rows) + [shape(head_width, total_rows, dtype=F32)]
    unit, q, key, v, qt, kt, ot, lse, a0, a1, a2, a3 = call(
        attend_far,
        "attend_far",
        (info, tok2, tok3, params, split_heads) + tuple(near),
        later
        + [shape(head_width // HD, total_rows, dtype=F32)]
        + [shape(rows, head_width)] * 4,
        [pltpu.VMEM(item.shape, item.dtype) for item in kept(2 * rows)]
        + [
            pltpu.VMEM((total_rows, head_width), BF16),
            pltpu.VMEM((head_width, total_rows), BF16),
            pltpu.VMEM((head_width, total_rows), BF16),
            pltpu.VMEM((head_width, total_rows), F32),
        ]
        + [pltpu.VMEM((dims[0], rows), F32) for dims in state]
        + [pltpu.SemaphoreType.DMA((13,))],
        micros=10,
        mib=20,
        far=range(len(later)),
    )
    a0, a1, a2, a3, out2, part0, pack0, out_held = lax.optimization_barrier(
        (a0, a1, a2, a3, out2, part0, pack0, output_weight)
    )
    pack1 = swap_tensor(pack0, 1)
    out1 = swap_tensor(out_held, 1)
    out3 = swap_tensor(out2, 1)
    p0, p1, p2, p3 = a0, swap_tensor(a1, 1), swap_tensor(a2, 2), swap_tensor(a3, 3)
    part1, part2 = swap_dp(part0, 1), swap_dp(part0, 2)
    p1, p2, p3, out3, part1, part2 = lax.optimization_barrier((p1, p2, p3, out3, part1, part2))
    part3 = swap_dp(part2, 1)
    outs = (output_weight, out1, out2, out3)
    square, square32 = shape(rows, width), shape(rows, width, dtype=F32)
    n2, ffn_low, y, gate2, gate, mixed, ffn, gn2, vec, keep0, send0 = call(
        middle_first,
        "middle_first",
        (info, p0, p1, p2, p3) + outs + (tokens, cotangent, pack0, pack1, params)
        + (gate_weight, pass_weight),
        [square] * 2
        + [square32] * 6
        + [shape(16, width, dtype=F32)]
        + [shape(2 * width, width)] * 2,
        micros=9,
        mib=20,
    )
    n2, part3, send0 = lax.optimization_barrier((n2, part3, send0))
    parts2 = jnp.concatenate([part0, part1, part2, part3])
    parts3 = swap_tensor(parts2, 1)
    got0 = swap_tensor(send0, 1)
    output, g0, g1, g2, g3, hid, pre_low, z2_low, z1_low, mixed_low, carry, vec = call(
        middle_second,
        "middle_second",
        (info,) + outs + (tokens, cotangent, parts2, parts3, params, pass_weight)
        + (n2, ffn_low, y, gate2, gate, mixed, ffn, gn2, vec),
        [square]
        + [shape(rows, head_width)] * 4
        + [shape(2, rows, width)] * 2
        + [square] * 3
        + [square32, shape(16, width, dtype=F32)],
        [pltpu.VMEM(pack0.shape, BF16)] * 2,
        micros=7,
        mib=20,
    )
    g1, g2, g3 = swap_tensor(g1, 1), swap_tensor(g2, 2), swap_tensor(g3, 3)
    keep, send, vec = call(
        weight_grads,
        "weight_grads",
        (info, hid, pre_low, ffn_low, z2_low, n2, z1_low, mixed_low, tokens, params)
        + (gate_weight, p0, p1, p2, p3, vec),
        [shape(2 * width + 6 * head_width, width)] * 2
        + [shape(16, width, dtype=F32)],
        [pltpu.VMEM((width, width), F32)] * 2,
        micros=4,
        mib=14,
    )
    g1, g2, g3, got0, keep, send, vec = lax.optimization_barrier(
        (g1, g2, g3, got0, keep, send, vec)
    )
    got = swap_tensor(send, 1)
    near = fold(keep0, got0)
    total = fold(keep, got)
    half = width // 2
    down0, up_keep = near[:width], near[width:]
    down2, up_send = total[:width], total[width : 2 * width]
    rest = total[2 * width :]
    down_send = jnp.concatenate([down0[half:], down2[half:]])
    down_keep = jnp.concatenate([down0[:half], down2[:half]])
    half = rest.shape[0] // 2
    down_send, up_send, rest_send, vec = lax.optimization_barrier(
        (down_send, up_send, rest[half:], vec)
    )
    down_got = swap_dp(down_send, 1)
    up_got = swap_tensor(up_send, 2)
    rest_got = swap_dp(rest_send, 2)
    blocks = [pltpu.VMEM((rows, head_width), F32)] * 2
    totals = [(head_width, total_rows), (3, head_width, width), (3, head_width, 1)]
    rows_keep0, rows_send0, up, upt, dots, dqt, moment, total_cols = call(
        attend_backward_first,
        "attend_backward_first",
        (info, q, key, v, qt, kt, ot, lse, jnp.concatenate([g0, g1, g2, g3]), unit, split_heads),
        [square] * 2
        + [shape(total_rows, head_width), shape(head_width, total_rows)]
        + [shape(head_width // HD, total_rows, dtype=F32)]
        + [shape(*dims, dtype=F32) for dims in totals],
        blocks,
        micros=12,
        mib=12,
    )
    rows_keep0, rows_send0, dqt, down_got, up_got, rest_got = lax.optimization_barrier(
        (rows_keep0, rows_send0, dqt, down_got, up_got, rest_got)
    )
    down_part = fold(down_keep, down_got)
    up_part = fold(up_keep, up_got)
    rest = fold(rest[:half], rest_got)
    half = down_part.shape[0] // 2
    down_send, up_send, dqt = lax.optimization_barrier((down_part[half:], up_part[half:], dqt))
    down_got = swap_tensor(down_send, 2)
    up_got = swap_dp(up_send, 1)
    rest_kept, rest_sent = split_rest(rest)
    rest_got = swap_tensor(rest_sent, 2)
    rows_got0 = swap_tensor(rows_send0, 1)
    keep1, send1, heads_sum, vec = call(
        attend_backward_second,
        "attend_backward_second",
        (info, q, key, v, qt, kt, lse, unit, split_heads, up, upt, dots, dqt, moment)
        + (total_cols, params, vec),
        [square] * 2 + [shape(3 * head_width, width), shape(16, width)],
        blocks + [pltpu.VMEM(dims, F32) for dims in totals],
        micros=7,
        mib=12,
    )
    down_got, up_got, rest_got, rows_got0, heads_sum, vec, keep1, send1 = lax.optimization_barrier(
        (down_got, up_got, rest_got, rows_got0, heads_sum, vec, keep1, send1)
    )

    down_part, up_part = fold(down_part[:half], down_got), fold(up_part[:half], up_got)
    step = width // PARTS
    both = jnp.concatenate(
        [
            piece[n * step : (n + 1) * step]
            for n in range(PARTS // 2)
            for piece in (down_part, up_part)
        ]
    )

    size = both.shape[0] // 2
    first_ffn = fold(both[:size], swap_dp(both[size:], 2))

    def heads_chain(values, vec):
        size = values.shape[0] // 2
        got = yield jnp.concatenate([values[size:], vec]), "dp", 1
        values, vec = fold(values[:size], got[:size]), fold(vec, got[size:])
        values, _ = lax.optimization_barrier((values, first_ffn))
        values, vec = yield from reduce_dp(values, (2,), vec)
        vec = vec.astype(F32)
        s2 = yield values, "dp", 2
        got = yield vec, "tensor", 1
        vec = vec + got
        got = yield vec, "tensor", 2
        vectors = call(
            unpack_vectors,
            "unpack_vectors",
            (info, vec, got),
            [shape(1, width, dtype=F32)] * 9,
        )
        s3 = yield jnp.concatenate([values, s2]), "dp", 1
        (heads_grad,) = call(
            unpack_heads,
            "unpack_heads",
            (info, values, s2, s3),
            [shape(3, width, head_width, dtype=F32)],
            [pltpu.VMEM((3, head_width, width), F32)],
        )
        return heads_grad, [v.reshape(width) for v in vectors]

    def rows_chain():
        got = yield send1, "tensor", 1
        lower, upper = fold(rows_keep0, rows_got0), fold(keep1, got)
        is_lower = me < 2
        near = jnp.where(is_lower, lower, upper)
        far = yield jnp.where(is_lower, upper, lower), "tensor", 2
        return call(
            tokens_backward,
            "tokens_backward",
            (tokens, near, far, z1_low, gate_weight, carry, params),
            [square],
            scalars=0,
        )[0]

    def rest_chain(values):
        values = yield from reduce_dp(values, (1,))
        parts = yield from gather_dp(values, (1, 2))
        out_grad, gates = call(
            unpack_rest,
            "unpack_rest",
            (info,) + parts,
            [shape(head_width, width, dtype=F32), shape(2 * head_width, width)],
        )
        gates2 = yield gates, "tensor", 2
        other = yield jnp.concatenate([gates, gates2]), "tensor", 1
        gate_grad, pass_grad = call(
            unpack_gates,
            "unpack_gates",
            (info, gates, other[: 2 * head_width], gates2, other[2 * head_width :]),
            [shape(width, width, dtype=F32)] * 2,
        )
        return out_grad, gate_grad, pass_grad

    def ffn_chain(values):
        values = yield from reduce_dp(values, ())
        d0 = jnp.concatenate([values[:step], values[2 * step : 3 * step]])
        u0 = jnp.concatenate([values[step : 2 * step], values[3 * step :]])
        d1 = yield d0, "dp", 2
        u1 = yield u0, "dp", 1
        d2 = yield jnp.concatenate([d0, d1]), "dp", 1
        u2 = yield jnp.concatenate([u0, u1]), "dp", 2
        return d0, d1, d2, u0, u1, u2

    (tokens_grad,) = run_chains([rows_chain()])
    (
        (out_grad, gate_grad, pass_grad),
        ffn_parts,
        (heads_grad, vectors),
    ) = run_chains(
        [
            rest_chain(fold(rest_kept, rest_got)),
            ffn_chain(first_ffn),
            heads_chain(heads_sum, vec),
        ]
    )
    down_grad, up_grad = call(
        unpack_ffn,
        "unpack_ffn",
        (info,) + ffn_parts,
        [shape(width, width, dtype=F32)] * 2,
        [pltpu.VMEM((width, width), F32)],
    )
    (
        down_bias_grad,
        pass_bias_grad,
        second_shift_grad,
        second_gain_grad,
        output_bias_grad,
        gate_bias_grad,
        norm_gain_grad,
        norm_shift_grad,
        up_bias_grad,
    ) = vectors
    return (
        output,
        tokens_grad,
        norm_gain_grad,
        norm_shift_grad,
        heads_grad.transpose(1, 0, 2),
        out_grad,
        output_bias_grad,
        gate_grad,
        gate_bias_grad,
        second_gain_grad,
        second_shift_grad,
        up_grad,
        up_bias_grad,
        down_grad,
        down_bias_grad,
        pass_grad,
        pass_bias_grad,
    )


def solution(mesh):
    placed = (
        P(("dp", "tensor"), None),
        P(),
        P(),
        P(None, None, "tensor"),
        P("tensor", None),
        P(),
        P(),
        P(),
        P(),
        P(),
        P(None, "tensor"),
        P("tensor"),
        P("tensor", None),
        P(),
        P(),
        P(),
        P(),
        P(),
        P(("dp", "tensor"), None),
    )
    return jax.shard_map(
        body,
        mesh=mesh,
        in_specs=placed,
        out_specs=(
            P(("dp", "tensor"), None),
            P(("dp", "tensor"), None),
            P(),
            P(),
            P(None, None, "tensor"),
            P("tensor", None),
            P(),
            P(),
            P(),
            P(),
            P(),
            P(None, "tensor"),
            P("tensor"),
            P("tensor", None),
            P(),
            P(),
            P(),
        ),
        check_vma=False,
    )
```

```python
import functools

import jax
import jax.numpy as jnp
from jax import lax
from jax.experimental import pallas as pl
from jax.experimental.pallas import tpu as pltpu
from jax.sharding import PartitionSpec as P

HD = 64
EPS = 1e-05
NEGATIVE = -1e30
GELU_C = 0.7978845608028654
F32 = jnp.float32
BF16 = jnp.bfloat16
VMEM = pl.BlockSpec(memory_space=pltpu.VMEM)
HBM = pl.BlockSpec(memory_space=pltpu.HBM)
SMEM = pl.BlockSpec(memory_space=pltpu.SMEM)
PARTS = 8
WEIGHT_PARTS = 4


def dot(left, right, left_dim=1, right_dim=0):
    return lax.dot_general(
        left, right, (((left_dim,), (right_dim,)), ((), ())), preferred_element_type=F32
    )


def column_sum(values):
    return jnp.sum(values, axis=0, keepdims=True)


def row_mean(values):
    return jnp.mean(values, axis=-1, keepdims=True)


def normalized(values):
    centred = values - row_mean(values)
    scale = lax.rsqrt(row_mean(centred * centred) + EPS)
    return centred * scale, scale


def place(index, size):
    return pl.multiple_of(index * size, size)


def start_of(row, first, total):
    return jnp.where(row < first, 0, jnp.where(row < total, first, row))


def call(body, name, operands, outs, scratch=(), scalars=1, micros=2, mib=12, far=()):
    return pl.pallas_call(
        body,
        cost_estimate=pl.CostEstimate(flops=int(micros * 1.1e9), bytes_accessed=0, transcendentals=0),
        out_shape=[
            pltpu.HBM(item.shape, item.dtype) if n in far else item for n, item in enumerate(outs)
        ],
        in_specs=[SMEM] * scalars + [VMEM] * (len(operands) - scalars),
        out_specs=[
            HBM if n in far else SMEM if item.dtype == jnp.int32 else VMEM
            for n, item in enumerate(outs)
        ],
        scratch_shapes=list(scratch),
        compiler_params=pltpu.CompilerParams(vmem_limit_bytes=mib << 20),
        name=name,
    )(*operands)


def shape(*dims, dtype=BF16):
    return jax.ShapeDtypeStruct(dims, dtype)


def project(tok, params, weights):
    unit, _ = normalized(tok[...].astype(F32))
    normed = (unit * params[0:1, :] + params[1:2, :]).astype(BF16)
    q, key, v = [dot(normed, weights[c]).astype(BF16) for c in range(3)]
    return unit.astype(BF16), q * BF16(0.125), key, v


def attend(info, i, count, last, fresh, block, queries_t, keys, values_t, state):
    first, total = info[1], info[2]
    acc, sum_row, top_row = state
    width = acc.shape[0]
    base = i * block
    head = lax.broadcasted_iota(jnp.int32, (width, block), 0) // HD
    q_heads = [jnp.where(head == h, queries_t, BF16(0)) for h in range(width // HD)]
    row = base + lax.broadcasted_iota(jnp.int32, (1, block), 1)
    start = start_of(row, first, total)
    last_start = start_of(base + block - 1, first, total)

    @pl.when(fresh)
    def _():
        acc[...] = jnp.zeros_like(acc)
        sum_row[...] = jnp.zeros_like(sum_row)
        top_row[...] = jnp.full_like(top_row, NEGATIVE)

    def step(j, masked):
        at = place(j, block)
        key_rows = keys(j)
        for h in range(width // HD):
            part = slice(HD * h, HD * h + HD)
            scores = dot(key_rows, q_heads[h])
            if masked:
                col = at + lax.broadcasted_iota(jnp.int32, (block, block), 0)
                scores = jnp.where((col >= start) & (col <= row), scores, NEGATIVE)
            before = top_row[h : h + 1, :]
            top = jnp.maximum(before, jnp.max(scores, axis=0, keepdims=True))
            fade = jnp.exp(before - top)
            exponent = jnp.exp(scores - top)
            mixed = dot(values_t(part, j), exponent.astype(BF16))
            sum_row[h : h + 1, :] = sum_row[h : h + 1, :] * fade + column_sum(exponent)
            acc[part, :] = acc[part, :] * fade + mixed
            top_row[h : h + 1, :] = top

    def loop(n, carry):
        j = last - n
        masked = (j == i) | (j * block < last_start)

        step(j, True)

        return carry

    lax.fori_loop(0, count, loop, 0)


def lowest_block(info, i, block):
    return start_of(i * block, info[1], info[2]) // block


def sequences(lengths, owners, info):
    here = lax.axis_index("dp")

    def entry(e, carry):
        first, seen, total = carry
        mine = owners[e] == here
        length = jnp.where(mine, lengths[e], 0)
        first = jnp.where(seen == 0, length, first)
        return first, seen + mine.astype(jnp.int32), total + length

    zero = jnp.int32(0)
    first, seen, total = lax.fori_loop(0, lengths.shape[0], entry, (zero, zero, zero))
    info[0] = lax.axis_index("tensor")
    info[1] = first
    info[2] = total
    info[3] = here % PARTS


def attend_near(
    lengths, owners, t0, t1, params, weights,
    info, unit_out, q_out, k_out, v_out, qt_out, kt_out, vt_out, acc, sum_row, top_row,
):
    sequences(lengths, owners, info)
    me = info[0]
    rows = t0.shape[0]
    for k, tok in enumerate((t0, t1)):
        at = place((me ^ k) % 2, rows)
        unit, q, key, v = project(tok, params, weights)
        unit_out[pl.ds(at, rows), :] = unit
        for out, turned, value in ((q_out, qt_out, q), (k_out, kt_out, key), (v_out, vt_out, v)):
            out[pl.ds(at, rows), :] = value
            turned[:, pl.ds(at, rows)] = value.T
    base = me // 2 * 2
    for n in range(2):
        i = base + n
        lanes = slice(n * rows, (n + 1) * rows)
        attend(
            info,
            i,
            i + 1 - jnp.maximum(lowest_block(info, i, rows), base),
            i,
            True,
            rows,
            qt_out[:, lanes],
            lambda j: k_out[pl.ds(place(j - base, rows), rows), :],
            lambda part, j: vt_out[part, pl.ds(place(j - base, rows), rows)],
            [ref.at[:, lanes] for ref in (acc, sum_row, top_row)],
        )


def attend_far(
    info, t2, t3, params, weights,
    unit_in, q_in, k_in, v_in, qt_in, kt_in, vt_in, acc_in, sum_in, top_in,
    unit_far, q_far, k_far, v_far, qt_far, kt_far, ot_far, lse_out, a0, a1, a2, a3,
    unit_new, q_new, k_new, v_new, qt_new, kt_new, keys, qt, vt, ot, acc, sum_row, top_row, done,
):
    me = info[0]
    rows = t2.shape[0]
    own = me // 2
    for k, tok in ((2, t2), (3, t3)):
        at = place((me ^ k) % 2, rows)
        unit, q, key, v = project(tok, params, weights)
        unit_new[pl.ds(at, rows), :] = unit
        q_new[pl.ds(at, rows), :] = q
        k_new[pl.ds(at, rows), :] = key
        v_new[pl.ds(at, rows), :] = v
        qt_new[:, pl.ds(at, rows)] = q.T
        kt_new[:, pl.ds(at, rows)] = key.T
        vt[:, pl.ds(place(me ^ k, rows), rows)] = v.T
    copies = []
    both = 2 * rows
    here, there = pl.ds(place(own, both), both), pl.ds(place(1 - own, both), both)
    for old, new, far in (
        (unit_in, unit_new, unit_far),
        (q_in, q_new, q_far),
        (k_in, k_new, k_far),
        (v_in, v_new, v_far),
    ):
        copies.append((old, far.at[here]))
        copies.append((new, far.at[there]))
    for old, new, far in ((qt_in, qt_new, qt_far), (kt_in, kt_new, kt_far)):
        copies.append((old, far.at[:, here]))
        copies.append((new, far.at[:, there]))
    copies.append((ot, ot_far))
    copies = [pltpu.make_async_copy(a, b, done.at[n]) for n, (a, b) in enumerate(copies)]
    for copy in copies[:-1]:
        copy.start()
    keys[here, :] = k_in[...]
    keys[there, :] = k_new[...]
    qt[:, here] = qt_in[...]
    qt[:, there] = qt_new[...]
    vt[:, here] = vt_in[...]

    def query_block(i, unused):
        other = i // 2 != own
        lanes = pl.ds(place(i, rows), rows)
        old = pl.ds(place(i % 2, rows), rows)
        lowest = lowest_block(info, i, rows)

        @pl.when(jnp.logical_not(other))
        def _():
            acc[...] = acc_in[:, old]
            sum_row[...] = sum_in[:, old]
            top_row[...] = top_in[:, old]

        attend(
            info,
            i,
            jnp.where(other, i + 1 - lowest, jnp.where(own == 1, jnp.maximum(2 - lowest, 0), 0)),
            jnp.where(other, i, 1),
            other,
            rows,
            qt[:, lanes],
            lambda j: keys[pl.ds(place(j, rows), rows), :],
            lambda part, j: vt[part, pl.ds(place(j, rows), rows)],
            (acc, sum_row, top_row),
        )
        for h in range(acc.shape[0] // HD):
            part = slice(HD * h, HD * h + HD)
            summed = sum_row[h : h + 1, :]
            ot[part, lanes] = acc[part, :] / summed
            lse_out[h : h + 1, lanes] = top_row[h : h + 1, :] + jnp.log(summed)
        return unused

    lax.fori_loop(0, 4, query_block, 0)
    copies[-1].start()
    for k, out in enumerate((a0, a1, a2, a3)):
        at = place(me ^ k, rows)
        out[...] = ot[:, pl.ds(at, rows)].T.astype(BF16)
    for copy in copies:
        copy.wait()


def live_rows(info, rows):
    row = info[0] * rows + lax.broadcasted_iota(jnp.int32, (rows, 1), 0)
    return (row < info[2]).astype(F32)


def put_parts(buf, base, grad, index, step, order, stride=None):
    for p in range(PARTS):
        at = base + order(p ^ index) * (step if stride is None else stride)
        buf[pl.ds(pl.multiple_of(at, 16), step), :] = grad[p * step : (p + 1) * step]


def hidden_block(pack, width, n2, gf_low):
    up, down = pack.at[0:width], pack.at[width + 16 : 2 * width + 16]
    pre = dot(n2, up[...]) + pack[width : width + 1, :].astype(F32)
    square = pre * pre
    th = jnp.tanh(GELU_C * pre * (1.0 + 0.044715 * square))
    half = 0.5 * (1.0 + th)
    hidden = (pre * half).astype(BF16)
    slope = half + 0.5 * GELU_C * pre * (1.0 - th * th) * (1.0 + 0.134145 * square)
    grad = dot(gf_low, down[...], 1, 1) * slope
    low = grad.astype(BF16)
    return hidden, low, column_sum(grad), dot(hidden, down[...]), dot(low, up[...], 1, 1)


def middle_first(
    info, p0, p1, p2, p3, o0, o1, o2, o3, tok, cot, w0, w1, params, gate_w, pass_w,
    n2_out, ffn_low, y_out, gate2_out, gate_out, mixed_out, ffn_out, gn2_out, vec, keep, send,
):
    me, index = info[0], info[3]
    gain, shift, out_b, gate_b, gain2, shift2, down_b, pass_b = [
        params[n : n + 1, :] for n in range(8)
    ]
    rows, width = tok.shape
    x = tok[...].astype(F32)
    unit, _ = normalized(x)
    n1 = (unit * gain + shift).astype(BF16)
    mixed = out_b
    for p, w in zip((p0, p1, p2, p3), (o0, o1, o2, o3)):
        mixed = mixed + dot(p[...], w[...])
    mixed_out[...] = mixed
    gate = jax.nn.sigmoid(dot(n1, gate_w[...]) + gate_b)
    gate_out[...] = gate
    y = gate * mixed + (1.0 - gate) * x
    y_out[...] = y
    unit2, _ = normalized(y)
    n2 = (unit2 * gain2 + shift2).astype(BF16)
    n2_out[...] = n2
    gate2 = jax.nn.sigmoid(dot(n2, pass_w[...]) + pass_b)
    gate2_out[...] = gate2
    gf = cot[...].astype(F32) * live_rows(info, rows) * gate2
    vec[...] = jnp.zeros_like(vec)
    vec[0:1, :] = column_sum(gf)
    gf_low = gf.astype(BF16)
    ffn_low[...] = gf_low
    n2_turned = n2.T
    ffn_turned = gf_low.T
    ffn, gn2 = down_b, 0.0
    for k, (pack, buf) in enumerate(((w0, keep), (w1, send))):
        hidden, low, columns, more_ffn, more_gn2 = hidden_block(pack, width, n2, gf_low)
        vec[pl.ds(8 + (me ^ k), 1), :] = columns
        ffn = ffn + more_ffn
        gn2 = gn2 + more_gn2
        step = width // PARTS
        put_parts(buf, 0, dot(ffn_turned, hidden).astype(BF16), index, step, reverse)
        put_parts(buf, width, dot(n2_turned, low).astype(BF16), index, step, reverse)
    ffn_out[...] = ffn
    gn2_out[...] = gn2


def middle_second(
    info, o0, o1, o2, o3, tok, cot, w2, w3, params, pass_w,
    n2_in, ffn_low, y_in, gate2_in, gate_in, mixed_in, ffn_in, gn2_in, vec_in,
    out, g0, g1, g2, g3, hid, pre_low, z2_low, z1_low, mixed_low, carry, vec,
    whole2, whole3,
):
    me = info[0]
    quarter = w2.shape[0] // WEIGHT_PARTS
    for part in range(WEIGHT_PARTS):
        at = place((info[3] ^ part) % WEIGHT_PARTS, quarter)
        for whole, parts in ((whole2, w2), (whole3, w3)):
            whole[pl.ds(at, quarter), :] = parts[part * quarter : (part + 1) * quarter]
    gain2 = params[4:5, :]
    rows, width = tok.shape
    n2, gf_low = n2_in[...], ffn_low[...]
    ffn, gn2 = ffn_in[...], gn2_in[...]
    vec[...] = vec_in[...]
    for n, pack in enumerate((whole2, whole3)):
        hidden, low, columns, more_ffn, more_gn2 = hidden_block(pack, width, n2, gf_low)
        hid[n] = hidden
        pre_low[n] = low
        vec[pl.ds(8 + (me ^ (2 + n)), 1), :] = columns
        ffn = ffn + more_ffn
        gn2 = gn2 + more_gn2
    live = live_rows(info, rows)
    gate2, y = gate2_in[...], y_in[...]
    out[...] = ((gate2 * ffn + (1.0 - gate2) * y) * live).astype(BF16)
    gy = cot[...].astype(F32) * live
    z2 = gy * gate2 * (ffn - y) * (1.0 - gate2)
    vec[1:2, :] = column_sum(z2)
    z2l = z2.astype(BF16)
    z2_low[...] = z2l
    gn2 = gn2 + dot(z2l, pass_w[...], 1, 1)
    unit2, scale2 = normalized(y)
    vec[2:3, :] = column_sum(gn2)
    vec[3:4, :] = column_sum(gn2 * unit2)
    g = gn2 * gain2
    gy1 = gy * (1.0 - gate2) + scale2 * (g - row_mean(g) - unit2 * row_mean(g * unit2))
    gate = gate_in[...]
    gm = gy1 * gate
    vec[4:5, :] = column_sum(gm)
    z1 = gm * (mixed_in[...] - tok[...].astype(F32)) * (1.0 - gate)
    vec[5:6, :] = column_sum(z1)
    z1_low[...] = z1.astype(BF16)
    gml = gm.astype(BF16)
    mixed_low[...] = gml
    carry[...] = gy1 * (1.0 - gate)
    for g_out, w in zip((g0, g1, g2, g3), (o0, o1, o2, o3)):
        g_out[...] = dot(gml, w[...], 1, 1).astype(BF16)


ORDER = [int(f"{p:03b}"[::-1], 2) for p in range(PARTS)]
UP_ORDER = [ORDER[p] for p in (0, 1, 4, 5, 2, 3, 6, 7)]
REST_ORDER = [((p >> 1) & 1) | ((p >> 2) << 1) | ((p & 1) << 2) for p in range(PARTS)]


def weight_grads(
    info, hid, pre_low, ffn_low, z2_low, n2, z1_low, mixed_low, tok, params, gate_w,
    p0, p1, p2, p3, vec_in,
    keep, send, vec,
    scratch_gate, scratch_pass,
):
    me, mine = info[0], info[3]
    gain, shift = params[0:1, :], params[1:2, :]
    width = tok.shape[1]
    heads = p0.shape[1]
    unit, _ = normalized(tok[...].astype(F32))
    n1 = (unit * gain + shift).astype(BF16)
    z1l = z1_low[...]
    step = width // PARTS
    small = heads // PARTS
    n2_turned = n2[...].T
    n1_turned = n1.T
    z2l = z2_low[...]
    gml = mixed_low[...]
    ffn_turned = ffn_low[...].T
    pieces = (p0, p1, p2, p3)
    scratch_gate[...] = dot(n1_turned, z1l)
    scratch_pass[...] = dot(n2_turned, z2l)
    for n, buf in enumerate((keep, send)):
        grad = dot(ffn_turned, hid[n]).astype(BF16)
        put_parts(buf, 0, grad, mine, step, reverse)
        grad = dot(n2_turned, pre_low[n]).astype(BF16)
        put_parts(buf, width, grad, mine, step, reverse)
    for k in range(4):
        buf = (keep, send)[k % 2]
        out_grad = dot(pieces[k][...], gml, 0, 0).astype(BF16)
        at = place(me ^ k, heads)
        rest = (out_grad,) + tuple(
            ref[pl.ds(at, heads), :].astype(BF16) for ref in (scratch_gate, scratch_pass)
        )
        for n, grad in enumerate(rest):
            base = 2 * width + (3 * (k // 2) + n) * small
            put_parts(buf, base, grad, mine, small, reverse_rest, 6 * small)
    dz = dot(z1l, gate_w[...], 1, 1)
    vec[...] = vec_in[...]
    vec[6:7, :] = column_sum(dz * unit)
    vec[7:8, :] = column_sum(dz)


def reverse_rest(part):
    return ((part & 2) << 1) | ((part & 1) << 1) | ((part >> 2) & 1)


def reverse(part):
    return ((part & 1) << 2) | (part & 2) | ((part >> 2) & 1)


def backward_blocks(lowest, info, q, k, v, qt, kt, lse, unit_low, weights, keep, send,
    up, upt, dqt, dk, dv, dots, moment, total_cols):
    me, first, total = info[0], info[1], info[2]
    rows = keep.shape[0]
    block = rows
    width = q.shape[1]
    heads = width // HD
    lane_head = lax.broadcasted_iota(jnp.int32, (block, width), 1) // HD
    row_head = lax.broadcasted_iota(jnp.int32, (width, block), 0) // HD

    def key_block(j, unused):
        at_k = place(j, block)
        keys = k[pl.ds(at_k, block), :]
        values = v[pl.ds(at_k, block), :]
        dk[...] = jnp.zeros_like(dk)
        dv[...] = jnp.zeros_like(dv)

        def step(at, masked):
            cols = pl.ds(at, block)
            scaled_t = qt[:, cols]
            scaled = q[pl.ds(at, block), :]
            ups = up[pl.ds(at, block), :]
            ups_t = upt[:, cols]
            for h in range(heads):
                part = slice(HD * h, HD * h + HD)
                scores = dot(keys, jnp.where(row_head == h, scaled_t, BF16(0)))
                if masked:
                    row = at + lax.broadcasted_iota(jnp.int32, (1, block), 1)
                    start = start_of(row, first, total)
                    col = at_k + lax.broadcasted_iota(jnp.int32, (block, block), 0)
                    scores = jnp.where((col >= start) & (col <= row), scores, NEGATIVE)
                probs = jnp.exp(scores - lse[h : h + 1, cols])
                grads = dot(values, jnp.where(row_head == h, ups_t, BF16(0)))
                score_grad = (probs * (grads - dots[h : h + 1, cols])).astype(BF16)
                dv[...] += dot(probs.astype(BF16), jnp.where(lane_head == h, ups, BF16(0)))
                dk[...] += dot(score_grad, jnp.where(lane_head == h, scaled, BF16(0)))
                dqt[part, cols] += dot(kt[part, pl.ds(at_k, block)], score_grad)

        def loop(i, carry):
            at = place(i, block)
            begin = start_of(at, first, total)
            last_start = start_of(at + block - 1, first, total)
            whole = (i > j) & (at_k >= last_start)

            @pl.when(at_k + block > begin)
            def _():
                step(at, True)

            return carry

        lax.fori_loop(j, 4, loop, 0)
        grads_t = (
            (dqt[:, pl.ds(at_k, block)] * 0.125).astype(BF16),
            dk[...].T.astype(BF16),
            dv[...].T.astype(BF16),
        )
        unit_rows = unit_low[pl.ds(at_k, block), :]
        spread = 0.0
        for c in range(3):
            spread = spread + dot(grads_t[c], weights[c], 0, 1)
            moment[c] += dot(grads_t[c], unit_rows)
            total_cols[c] += jnp.sum(grads_t[c].astype(F32), axis=1, keepdims=True)
        spread = spread.astype(BF16)
        even = (me ^ j) % 2 == 0

        @pl.when(even)
        def _():
            keep[...] = spread

        @pl.when(jnp.logical_not(even))
        def _():
            send[...] = spread

        return unused

    lax.fori_loop(lowest, lowest + 2, key_block, 0)


def attend_backward_first(
    info, q, k, v, qt, kt, ot, lse, gs, unit_low, weights,
    keep, send, up, upt, dots, dqt, moment, total_cols,
    dk, dv,
):
    me = info[0]
    rows = keep.shape[0]
    for n in range(4):
        at = place(me ^ n, rows)
        g = gs[n * rows : (n + 1) * rows, :]
        up[pl.ds(at, rows), :] = g
        upt[:, pl.ds(at, rows)] = g.T
    weighted = upt[...].astype(F32) * ot[...]
    for h in range(dots.shape[0]):
        dots[h : h + 1, :] = column_sum(weighted[HD * h : HD * h + HD])
    dqt[...] = jnp.zeros_like(dqt)
    moment[...] = jnp.zeros_like(moment)
    total_cols[...] = jnp.zeros_like(total_cols)
    backward_blocks(0, info, q, k, v, qt, kt, lse, unit_low, weights, keep, send,
        up, upt, dqt, dk, dv, dots, moment, total_cols)


def attend_backward_second(
    info, q, k, v, qt, kt, lse, unit_low, weights, up, upt, dots, dqt_in, moment_in, cols_in,
    params, vec_in,
    keep, send, heads_out, vec,
    dk, dv, dqt, moment, total_cols,
):
    mine = info[3]
    gain, shift = params[0:1, :], params[1:2, :]
    width = q.shape[1]
    half = dqt.shape[1] // 2
    dqt[:, half:] = dqt_in[:, half:]
    moment[...] = moment_in[...]
    total_cols[...] = cols_in[...]
    backward_blocks(2, info, q, k, v, qt, kt, lse, unit_low, weights, keep, send,
        up, upt, dqt, dk, dv, dots, moment, total_cols)
    step_rows = width // PARTS
    part_rows = 3 * step_rows
    gain_grad = 0.0
    shift_grad = 0.0
    for c in range(3):
        turned = weights[c].astype(F32).T
        gain_grad = gain_grad + column_sum(turned * moment[c])
        shift_grad = shift_grad + column_sum(turned * total_cols[c])
        grad = (moment[c] * gain + total_cols[c] * shift).astype(BF16)
        for p in range(PARTS):
            at = pl.multiple_of(reverse(p ^ mine) * part_rows + c * step_rows, 16)
            heads_out[pl.ds(at, step_rows), :] = grad[p * step_rows : (p + 1) * step_rows]
    pick = lax.broadcasted_iota(jnp.int32, vec_in.shape, 0)
    sums = vec_in[...] + jnp.where(pick == 6, gain_grad, 0.0) + jnp.where(pick == 7, shift_grad, 0.0)
    vec[...] = sums.astype(BF16)


def tokens_backward(tok, own, got, z1_low, gate_w, carry, params, out):
    unit, scale = normalized(tok[...].astype(F32))
    grad = own[...].astype(F32) + got[...].astype(F32) + dot(z1_low[...], gate_w[...], 1, 1)
    h = grad * params[0:1, :]
    out[...] = (
        carry[...] + scale * (h - row_mean(h) - unit * row_mean(h * unit))
    ).astype(BF16)


def each_part(info, refs, rows, order=ORDER):
    pos = 0
    for ref in refs:
        for n in range(ref.shape[0] // rows):
            yield order[pos] ^ info[3], ref, n * rows
            pos += 1


def unpack_ffn(info, d0, d1, d2, u0, u1, u2, down, up, turned):
    step = down.shape[0] // PARTS
    for p, ref, at in each_part(info, (d0, d1, d2), step):
        turned[pl.ds(place(p, step), step), :] = ref[at : at + step].astype(F32)
    for p, ref, at in each_part(info, (u0, u1, u2), step, UP_ORDER):
        up[pl.ds(place(p, step), step), :] = ref[at : at + step].astype(F32)
    down[...] = turned[...].T


def unpack_rest(info, s0, s1, s2, out, gates):
    rows = out.shape[0]
    step = rows // PARTS
    for p, ref, at in each_part(info, (s0, s1, s2), 3 * step, REST_ORDER):
        out[pl.ds(place(p, step), step), :] = ref[at : at + step].astype(F32)
        for n in range(2):
            first = at + (n + 1) * step
            gates[pl.ds(pl.multiple_of(n * rows + p * step, step), step), :] = ref[
                first : first + step
            ]


def unpack_heads(info, s0, s1, s2, heads, turned):
    step = heads.shape[2] // PARTS
    for p, ref, at in each_part(info, (s0, s1, s2), 3 * step):
        for c in range(3):
            turned[c, pl.ds(place(p, step), step), :] = ref[at + c * step : at + (c + 1) * step].astype(F32)
    for c in range(3):
        heads[c] = turned[c].T


def unpack_gates(info, s0, s1, s2, s3, gate, passed):
    rows = gate.shape[0] // 4
    for k, ref in enumerate((s0, s1, s2, s3)):
        at = place(info[0] ^ k, rows)
        gate[pl.ds(at, rows), :] = ref[0:rows].astype(F32)
        passed[pl.ds(at, rows), :] = ref[rows : 2 * rows].astype(F32)


def unpack_vectors(info, one, two, *outs):
    sums = one[...] + two[...]
    for n in range(8):
        outs[n][...] = sums[n : n + 1]
    pick = lax.broadcasted_iota(jnp.int32, sums.shape, 0) == 8 + info[0]
    outs[8][...] = column_sum(jnp.where(pick, sums, 0.0))


def swap_tensor(values, mask):
    return lax.ppermute(values, "tensor", [(i, i ^ mask) for i in range(4)])


def swap_dp(values, mask):
    return lax.ppermute(values, "dp", [(i, i ^ mask) for i in range(lax.axis_size("dp"))])


def fold(*terms):
    return sum(term.astype(F32) for term in terms).astype(BF16)


def scatter(values, axis, mask):
    half = values.shape[0] // 2
    got = yield values[half:], axis, mask
    return fold(values[:half], got)


def reduce_dp(values, masks, more=None):
    extra = 0 if more is None else more.shape[0]
    for mask in masks:
        half = values.shape[0] // 2
        sent = values[half:]
        if extra:
            sent = jnp.concatenate([sent, more])
        got = yield sent, "dp", mask
        values = fold(values[:half], got[:half])
        if extra:
            more = fold(more, got[half:])
    mask = 4
    while mask < lax.axis_size("dp"):
        size = values.shape[0]
        if mask == 4:
            sent = [values[size // 2 :], values[: size // 2]]
        else:
            sent = [values]
        if extra:
            sent = sent + [more]
        got = yield jnp.concatenate(sent), "dp", mask
        values = fold(values, got[:size])
        if extra:
            more = fold(more, got[size:])
        mask *= 2
    return (values, more) if extra else values


def gather_dp(values, masks=(2, 1)):
    s2 = yield values, "dp", masks[0]
    s3 = yield jnp.concatenate([values, s2]), "dp", masks[1]
    return values, s2, s3


def split_rest(values):
    step = values.shape[0] // PARTS
    shares = [values[n * step : (n + 1) * step] for n in range(PARTS)]
    return jnp.concatenate(shares[0::2]), jnp.concatenate(shares[1::2])


def run_chains(chains):
    results = [None] * len(chains)
    waiting = [None] * len(chains)
    alive = list(range(len(chains)))
    while alive:
        for n in list(alive):
            try:
                values, axis, mask = chains[n].send(waiting[n])
            except StopIteration as stop:
                results[n] = stop.value
                alive.remove(n)
                continue
            waiting[n] = (swap_dp if axis == "dp" else swap_tensor)(values, mask)
    return results


def body(
    tokens,
    norm_gain,
    norm_shift,
    heads_weight,
    output_weight,
    output_bias,
    gate_weight,
    gate_bias,
    second_gain,
    second_shift,
    up_weight,
    up_bias,
    down_weight,
    down_bias,
    pass_weight,
    pass_bias,
    lengths,
    owners,
    cotangent,
):
    rows, width = tokens.shape
    total_rows = 4 * rows
    head_width = heads_weight.shape[2]
    me = lax.axis_index("tensor")
    params = jnp.stack(
        [norm_gain, norm_shift, output_bias, gate_bias, second_gain, second_shift]
        + [down_bias, pass_bias]
    )
    split_heads = heads_weight.transpose(1, 0, 2)

    def kept(count):
        kinds = [shape(count, width)] + [shape(count, head_width)] * 3
        return kinds + [shape(head_width, count)] * 2

    tok2 = swap_tensor(tokens, 2)
    tok1 = swap_tensor(tokens, 1)
    state = [(head_width, 2 * rows), (8, 2 * rows), (8, 2 * rows)]
    info, *near = call(
        attend_near,
        "attend_near",
        (lengths, owners, tokens, tok1, params, split_heads),
        [shape(4, dtype=jnp.int32)]
        + kept(2 * rows)
        + [shape(head_width, 2 * rows)]
        + [shape(*dims, dtype=F32) for dims in state],
        scalars=2,
        micros=6,
        mib=12,
    )
    up_held, down_held, info = lax.optimization_barrier((up_weight, down_weight, info))
    bias_rows = jnp.broadcast_to(up_bias[None, :], (16, width))
    pack0 = jnp.concatenate([up_held, bias_rows, down_held, jnp.zeros((48, width), BF16)])
    quarter = pack0.shape[0] // WEIGHT_PARTS
    sent = lax.dynamic_slice_in_dim(
        pack0, lax.axis_index("dp") % WEIGHT_PARTS * quarter, quarter, 0
    )
    sent, out_held, tok2, *near = lax.optimization_barrier((sent, output_weight, tok2, *near))
    out2 = swap_tensor(out_held, 2)
    part0 = swap_tensor(sent, 2)
    tok3 = swap_tensor(tok2, 1)

    later = kept(total_rows) + [shape(head_width, total_rows, dtype=F32)]
    unit, q, key, v, qt, kt, ot, lse, a0, a1, a2, a3 = call(
        attend_far,
        "attend_far",
        (info, tok2, tok3, params, split_heads) + tuple(near),
        later
        + [shape(head_width // HD, total_rows, dtype=F32)]
        + [shape(rows, head_width)] * 4,
        [pltpu.VMEM(item.shape, item.dtype) for item in kept(2 * rows)]
        + [
            pltpu.VMEM((total_rows, head_width), BF16),
            pltpu.VMEM((head_width, total_rows), BF16),
            pltpu.VMEM((head_width, total_rows), BF16),
            pltpu.VMEM((head_width, total_rows), F32),
        ]
        + [pltpu.VMEM((dims[0], rows), F32) for dims in state]
        + [pltpu.SemaphoreType.DMA((13,))],
        micros=10,
        mib=20,
        far=range(len(later)),
    )
    a0, a1, a2, a3, out2, part0, pack0, out_held = lax.optimization_barrier(
        (a0, a1, a2, a3, out2, part0, pack0, output_weight)
    )
    pack1 = swap_tensor(pack0, 1)
    out1 = swap_tensor(out_held, 1)
    out3 = swap_tensor(out2, 1)
    p0, p1, p2, p3 = a0, swap_tensor(a1, 1), swap_tensor(a2, 2), swap_tensor(a3, 3)
    part1, part2 = swap_dp(part0, 1), swap_dp(part0, 2)
    p1, p2, p3, out3, part1, part2 = lax.optimization_barrier((p1, p2, p3, out3, part1, part2))
    part3 = swap_dp(part2, 1)
    outs = (output_weight, out1, out2, out3)
    square, square32 = shape(rows, width), shape(rows, width, dtype=F32)
    n2, ffn_low, y, gate2, gate, mixed, ffn, gn2, vec, keep0, send0 = call(
        middle_first,
        "middle_first",
        (info, p0, p1, p2, p3) + outs + (tokens, cotangent, pack0, pack1, params)
        + (gate_weight, pass_weight),
        [square] * 2
        + [square32] * 6
        + [shape(16, width, dtype=F32)]
        + [shape(2 * width, width)] * 2,
        micros=9,
        mib=20,
    )
    n2, part3, send0 = lax.optimization_barrier((n2, part3, send0))
    parts2 = jnp.concatenate([part0, part1, part2, part3])
    parts3 = swap_tensor(parts2, 1)
    got0 = swap_tensor(send0, 1)
    output, g0, g1, g2, g3, hid, pre_low, z2_low, z1_low, mixed_low, carry, vec = call(
        middle_second,
        "middle_second",
        (info,) + outs + (tokens, cotangent, parts2, parts3, params, pass_weight)
        + (n2, ffn_low, y, gate2, gate, mixed, ffn, gn2, vec),
        [square]
        + [shape(rows, head_width)] * 4
        + [shape(2, rows, width)] * 2
        + [square] * 3
        + [square32, shape(16, width, dtype=F32)],
        [pltpu.VMEM(pack0.shape, BF16)] * 2,
        micros=7,
        mib=20,
    )
    g1, g2, g3 = swap_tensor(g1, 1), swap_tensor(g2, 2), swap_tensor(g3, 3)
    keep, send, vec = call(
        weight_grads,
        "weight_grads",
        (info, hid, pre_low, ffn_low, z2_low, n2, z1_low, mixed_low, tokens, params)
        + (gate_weight, p0, p1, p2, p3, vec),
        [shape(2 * width + 6 * head_width, width)] * 2
        + [shape(16, width, dtype=F32)],
        [pltpu.VMEM((width, width), F32)] * 2,
        micros=4,
        mib=14,
    )
    g1, g2, g3, got0, keep, send, vec = lax.optimization_barrier(
        (g1, g2, g3, got0, keep, send, vec)
    )
    got = swap_tensor(send, 1)
    near = fold(keep0, got0)
    total = fold(keep, got)
    half = width // 2
    down0, up_keep = near[:width], near[width:]
    down2, up_send = total[:width], total[width : 2 * width]
    rest = total[2 * width :]
    down_send = jnp.concatenate([down0[half:], down2[half:]])
    down_keep = jnp.concatenate([down0[:half], down2[:half]])
    half = rest.shape[0] // 2
    down_send, up_send, rest_send, vec = lax.optimization_barrier(
        (down_send, up_send, rest[half:], vec)
    )
    down_got = swap_dp(down_send, 1)
    up_got = swap_tensor(up_send, 2)
    rest_got = swap_dp(rest_send, 2)
    blocks = [pltpu.VMEM((rows, head_width), F32)] * 2
    totals = [(head_width, total_rows), (3, head_width, width), (3, head_width, 1)]
    rows_keep0, rows_send0, up, upt, dots, dqt, moment, total_cols = call(
        attend_backward_first,
        "attend_backward_first",
        (info, q, key, v, qt, kt, ot, lse, jnp.concatenate([g0, g1, g2, g3]), unit, split_heads),
        [square] * 2
        + [shape(total_rows, head_width), shape(head_width, total_rows)]
        + [shape(head_width // HD, total_rows, dtype=F32)]
        + [shape(*dims, dtype=F32) for dims in totals],
        blocks,
        micros=12,
        mib=12,
    )
    rows_keep0, rows_send0, dqt, down_got, up_got, rest_got = lax.optimization_barrier(
        (rows_keep0, rows_send0, dqt, down_got, up_got, rest_got)
    )
    down_part = fold(down_keep, down_got)
    up_part = fold(up_keep, up_got)
    rest = fold(rest[:half], rest_got)
    half = down_part.shape[0] // 2
    down_send, up_send, dqt = lax.optimization_barrier((down_part[half:], up_part[half:], dqt))
    down_got = swap_tensor(down_send, 2)
    up_got = swap_dp(up_send, 1)
    rest_kept, rest_sent = split_rest(rest)
    rest_got = swap_tensor(rest_sent, 2)
    rows_got0 = swap_tensor(rows_send0, 1)
    keep1, send1, heads_sum, vec = call(
        attend_backward_second,
        "attend_backward_second",
        (info, q, key, v, qt, kt, lse, unit, split_heads, up, upt, dots, dqt, moment)
        + (total_cols, params, vec),
        [square] * 2 + [shape(3 * head_width, width), shape(16, width)],
        blocks + [pltpu.VMEM(dims, F32) for dims in totals],
        micros=7,
        mib=12,
    )
    down_got, up_got, rest_got, rows_got0, heads_sum, vec, keep1, send1 = lax.optimization_barrier(
        (down_got, up_got, rest_got, rows_got0, heads_sum, vec, keep1, send1)
    )

    down_part, up_part = fold(down_part[:half], down_got), fold(up_part[:half], up_got)
    step = width // PARTS
    both = jnp.concatenate(
        [
            piece[n * step : (n + 1) * step]
            for n in range(PARTS // 2)
            for piece in (down_part, up_part)
        ]
    )

    size = both.shape[0] // 2
    first_ffn = fold(both[:size], swap_dp(both[size:], 2))

    def heads_chain(values, vec):
        size = values.shape[0] // 2
        got = yield jnp.concatenate([values[size:], vec]), "dp", 1
        values, vec = fold(values[:size], got[:size]), fold(vec, got[size:])
        values, _ = lax.optimization_barrier((values, first_ffn))
        values, vec = yield from reduce_dp(values, (2,), vec)
        vec = vec.astype(F32)
        s2 = yield values, "dp", 2
        got = yield vec, "tensor", 1
        vec = vec + got
        got = yield vec, "tensor", 2
        vectors = call(
            unpack_vectors,
            "unpack_vectors",
            (info, vec, got),
            [shape(1, width, dtype=F32)] * 9,
        )
        s3 = yield jnp.concatenate([values, s2]), "dp", 1
        (heads_grad,) = call(
            unpack_heads,
            "unpack_heads",
            (info, values, s2, s3),
            [shape(3, width, head_width, dtype=F32)],
            [pltpu.VMEM((3, head_width, width), F32)],
        )
        return heads_grad, [v.reshape(width) for v in vectors]

    def rows_chain():
        got = yield send1, "tensor", 1
        lower, upper = fold(rows_keep0, rows_got0), fold(keep1, got)
        is_lower = me < 2
        near = jnp.where(is_lower, lower, upper)
        far = yield jnp.where(is_lower, upper, lower), "tensor", 2
        return call(
            tokens_backward,
            "tokens_backward",
            (tokens, near, far, z1_low, gate_weight, carry, params),
            [square],
            scalars=0,
        )[0]

    def rest_chain(values):
        values = yield from reduce_dp(values, (1,))
        parts = yield from gather_dp(values, (1, 2))
        out_grad, gates = call(
            unpack_rest,
            "unpack_rest",
            (info,) + parts,
            [shape(head_width, width, dtype=F32), shape(2 * head_width, width)],
        )
        gates2 = yield gates, "tensor", 2
        other = yield jnp.concatenate([gates, gates2]), "tensor", 1
        gate_grad, pass_grad = call(
            unpack_gates,
            "unpack_gates",
            (info, gates, other[: 2 * head_width], gates2, other[2 * head_width :]),
            [shape(width, width, dtype=F32)] * 2,
        )
        return out_grad, gate_grad, pass_grad

    def ffn_chain(values):
        values = yield from reduce_dp(values, ())
        d0 = jnp.concatenate([values[:step], values[2 * step : 3 * step]])
        u0 = jnp.concatenate([values[step : 2 * step], values[3 * step :]])
        d1 = yield d0, "dp", 2
        u1 = yield u0, "dp", 1
        d2 = yield jnp.concatenate([d0, d1]), "dp", 1
        u2 = yield jnp.concatenate([u0, u1]), "dp", 2
        return d0, d1, d2, u0, u1, u2

    (tokens_grad,) = run_chains([rows_chain()])
    (
        (out_grad, gate_grad, pass_grad),
        ffn_parts,
        (heads_grad, vectors),
    ) = run_chains(
        [
            rest_chain(fold(rest_kept, rest_got)),
            ffn_chain(first_ffn),
            heads_chain(heads_sum, vec),
        ]
    )
    down_grad, up_grad = call(
        unpack_ffn,
        "unpack_ffn",
        (info,) + ffn_parts,
        [shape(width, width, dtype=F32)] * 2,
        [pltpu.VMEM((width, width), F32)],
    )
    (
        down_bias_grad,
        pass_bias_grad,
        second_shift_grad,
        second_gain_grad,
        output_bias_grad,
        gate_bias_grad,
        norm_gain_grad,
        norm_shift_grad,
        up_bias_grad,
    ) = vectors
    return (
        output,
        tokens_grad,
        norm_gain_grad,
        norm_shift_grad,
        heads_grad.transpose(1, 0, 2),
        out_grad,
        output_bias_grad,
        gate_grad,
        gate_bias_grad,
        second_gain_grad,
        second_shift_grad,
        up_grad,
        up_bias_grad,
        down_grad,
        down_bias_grad,
        pass_grad,
        pass_bias_grad,
    )


def solution(mesh):
    placed = (
        P(("dp", "tensor"), None),
        P(),
        P(),
        P(None, None, "tensor"),
        P("tensor", None),
        P(),
        P(),
        P(),
        P(),
        P(),
        P(None, "tensor"),
        P("tensor"),
        P("tensor", None),
        P(),
        P(),
        P(),
        P(),
        P(),
        P(("dp", "tensor"), None),
    )
    return jax.shard_map(
        body,
        mesh=mesh,
        in_specs=placed,
        out_specs=(
            P(("dp", "tensor"), None),
            P(("dp", "tensor"), None),
            P(),
            P(),
            P(None, None, "tensor"),
            P("tensor", None),
            P(),
            P(),
            P(),
            P(),
            P(),
            P(None, "tensor"),
            P("tensor"),
            P("tensor", None),
            P(),
            P(),
            P(),
        ),
        check_vma=False,
    )
```

```python
import functools

import jax
import jax.numpy as jnp
from jax import lax
from jax.experimental import pallas as pl
from jax.experimental.pallas import tpu as pltpu
from jax.sharding import PartitionSpec as P

HD = 64
EPS = 1e-05
NEGATIVE = -1e30
GELU_C = 0.7978845608028654
F32 = jnp.float32
BF16 = jnp.bfloat16
VMEM = pl.BlockSpec(memory_space=pltpu.VMEM)
HBM = pl.BlockSpec(memory_space=pltpu.HBM)
SMEM = pl.BlockSpec(memory_space=pltpu.SMEM)
PARTS = 8
WEIGHT_PARTS = 4


def dot(left, right, left_dim=1, right_dim=0):
    return lax.dot_general(
        left, right, (((left_dim,), (right_dim,)), ((), ())), preferred_element_type=F32
    )


def column_sum(values):
    return jnp.sum(values, axis=0, keepdims=True)


def row_mean(values):
    return jnp.mean(values, axis=-1, keepdims=True)


def normalized(values):
    centred = values - row_mean(values)
    scale = lax.rsqrt(row_mean(centred * centred) + EPS)
    return centred * scale, scale


def place(index, size):
    return pl.multiple_of(index * size, size)


def start_of(row, first, total):
    return jnp.where(row < first, 0, jnp.where(row < total, first, row))


def call(body, name, operands, outs, scratch=(), scalars=1, micros=2, mib=12, far=()):
    return pl.pallas_call(
        body,
        cost_estimate=pl.CostEstimate(flops=int(micros * 1.1e9), bytes_accessed=0, transcendentals=0),
        out_shape=[
            pltpu.HBM(item.shape, item.dtype) if n in far else item for n, item in enumerate(outs)
        ],
        in_specs=[SMEM] * scalars + [VMEM] * (len(operands) - scalars),
        out_specs=[
            HBM if n in far else SMEM if item.dtype == jnp.int32 else VMEM
            for n, item in enumerate(outs)
        ],
        scratch_shapes=list(scratch),
        compiler_params=pltpu.CompilerParams(vmem_limit_bytes=mib << 20),
        name=name,
    )(*operands)


def shape(*dims, dtype=BF16):
    return jax.ShapeDtypeStruct(dims, dtype)


def project(tok, params, weights):
    unit, _ = normalized(tok[...].astype(F32))
    normed = (unit * params[0:1, :] + params[1:2, :]).astype(BF16)
    q, key, v = [dot(normed, weights[c]).astype(BF16) for c in range(3)]
    return unit.astype(BF16), q * BF16(0.125), key, v


def attend(info, i, count, last, fresh, block, queries_t, keys, values_t, state):
    first, total = info[1], info[2]
    acc, sum_row, top_row = state
    width = acc.shape[0]
    base = i * block
    head = lax.broadcasted_iota(jnp.int32, (width, block), 0) // HD
    q_heads = [jnp.where(head == h, queries_t, BF16(0)) for h in range(width // HD)]
    row = base + lax.broadcasted_iota(jnp.int32, (1, block), 1)
    start = start_of(row, first, total)
    last_start = start_of(base + block - 1, first, total)

    @pl.when(fresh)
    def _():
        acc[...] = jnp.zeros_like(acc)
        sum_row[...] = jnp.zeros_like(sum_row)
        top_row[...] = jnp.full_like(top_row, NEGATIVE)

    def step(j, masked):
        at = place(j, block)
        key_rows = keys(j)
        for h in range(width // HD):
            part = slice(HD * h, HD * h + HD)
            scores = dot(key_rows, q_heads[h])
            if masked:
                col = at + lax.broadcasted_iota(jnp.int32, (block, block), 0)
                scores = jnp.where((col >= start) & (col <= row), scores, NEGATIVE)
            before = top_row[h : h + 1, :]
            top = jnp.maximum(before, jnp.max(scores, axis=0, keepdims=True))
            fade = jnp.exp(before - top)
            exponent = jnp.exp(scores - top)
            mixed = dot(values_t(part, j), exponent.astype(BF16))
            sum_row[h : h + 1, :] = sum_row[h : h + 1, :] * fade + column_sum(exponent)
            acc[part, :] = acc[part, :] * fade + mixed
            top_row[h : h + 1, :] = top

    def loop(n, carry):
        j = last - n
        masked = (j == i) | (j * block < last_start)

        step(j, True)

        return carry

    lax.fori_loop(0, count, loop, 0)


def lowest_block(info, i, block):
    return start_of(i * block, info[1], info[2]) // block


def sequences(lengths, owners, info):
    here = lax.axis_index("dp")

    def entry(e, carry):
        first, seen, total = carry
        mine = owners[e] == here
        length = jnp.where(mine, lengths[e], 0)
        first = jnp.where(seen == 0, length, first)
        return first, seen + mine.astype(jnp.int32), total + length

    zero = jnp.int32(0)
    first, seen, total = lax.fori_loop(0, lengths.shape[0], entry, (zero, zero, zero))
    info[0] = lax.axis_index("tensor")
    info[1] = first
    info[2] = total
    info[3] = here % PARTS


def attend_near(
    lengths, owners, t0, t1, params, weights,
    info, unit_out, q_out, k_out, v_out, qt_out, kt_out, vt_out, acc, sum_row, top_row,
):
    sequences(lengths, owners, info)
    me = info[0]
    rows = t0.shape[0]
    for k, tok in enumerate((t0, t1)):
        at = place((me ^ k) % 2, rows)
        unit, q, key, v = project(tok, params, weights)
        unit_out[pl.ds(at, rows), :] = unit
        for out, turned, value in ((q_out, qt_out, q), (k_out, kt_out, key), (v_out, vt_out, v)):
            out[pl.ds(at, rows), :] = value
            turned[:, pl.ds(at, rows)] = value.T
    base = me // 2 * 2
    for n in range(2):
        i = base + n
        lanes = slice(n * rows, (n + 1) * rows)
        attend(
            info,
            i,
            i + 1 - jnp.maximum(lowest_block(info, i, rows), base),
            i,
            True,
            rows,
            qt_out[:, lanes],
            lambda j: k_out[pl.ds(place(j - base, rows), rows), :],
            lambda part, j: vt_out[part, pl.ds(place(j - base, rows), rows)],
            [ref.at[:, lanes] for ref in (acc, sum_row, top_row)],
        )


def attend_far(
    info, t2, t3, params, weights,
    unit_in, q_in, k_in, v_in, qt_in, kt_in, vt_in, acc_in, sum_in, top_in,
    unit_far, q_far, k_far, v_far, qt_far, kt_far, ot_far, lse_out, a0, a1, a2, a3,
    unit_new, q_new, k_new, v_new, qt_new, kt_new, keys, qt, vt, ot, acc, sum_row, top_row, done,
):
    me = info[0]
    rows = t2.shape[0]
    own = me // 2
    for k, tok in ((2, t2), (3, t3)):
        at = place((me ^ k) % 2, rows)
        unit, q, key, v = project(tok, params, weights)
        unit_new[pl.ds(at, rows), :] = unit
        q_new[pl.ds(at, rows), :] = q
        k_new[pl.ds(at, rows), :] = key
        v_new[pl.ds(at, rows), :] = v
        qt_new[:, pl.ds(at, rows)] = q.T
        kt_new[:, pl.ds(at, rows)] = key.T
        vt[:, pl.ds(place(me ^ k, rows), rows)] = v.T
    copies = []
    both = 2 * rows
    here, there = pl.ds(place(own, both), both), pl.ds(place(1 - own, both), both)
    for old, new, far in (
        (unit_in, unit_new, unit_far),
        (q_in, q_new, q_far),
        (k_in, k_new, k_far),
        (v_in, v_new, v_far),
    ):
        copies.append((old, far.at[here]))
        copies.append((new, far.at[there]))
    for old, new, far in ((qt_in, qt_new, qt_far), (kt_in, kt_new, kt_far)):
        copies.append((old, far.at[:, here]))
        copies.append((new, far.at[:, there]))
    copies.append((ot, ot_far))
    copies = [pltpu.make_async_copy(a, b, done.at[n]) for n, (a, b) in enumerate(copies)]
    for copy in copies[:-1]:
        copy.start()
    keys[here, :] = k_in[...]
    keys[there, :] = k_new[...]
    qt[:, here] = qt_in[...]
    qt[:, there] = qt_new[...]
    vt[:, here] = vt_in[...]

    def query_block(i, unused):
        other = i // 2 != own
        lanes = pl.ds(place(i, rows), rows)
        old = pl.ds(place(i % 2, rows), rows)
        lowest = lowest_block(info, i, rows)

        @pl.when(jnp.logical_not(other))
        def _():
            acc[...] = acc_in[:, old]
            sum_row[...] = sum_in[:, old]
            top_row[...] = top_in[:, old]

        attend(
            info,
            i,
            jnp.where(other, i + 1 - lowest, jnp.where(own == 1, jnp.maximum(2 - lowest, 0), 0)),
            jnp.where(other, i, 1),
            other,
            rows,
            qt[:, lanes],
            lambda j: keys[pl.ds(place(j, rows), rows), :],
            lambda part, j: vt[part, pl.ds(place(j, rows), rows)],
            (acc, sum_row, top_row),
        )
        for h in range(acc.shape[0] // HD):
            part = slice(HD * h, HD * h + HD)
            summed = sum_row[h : h + 1, :]
            ot[part, lanes] = acc[part, :] / summed
            lse_out[h : h + 1, lanes] = top_row[h : h + 1, :] + jnp.log(summed)
        return unused

    lax.fori_loop(0, 4, query_block, 0)
    copies[-1].start()
    for k, out in enumerate((a0, a1, a2, a3)):
        at = place(me ^ k, rows)
        out[...] = ot[:, pl.ds(at, rows)].T.astype(BF16)
    for copy in copies:
        copy.wait()


def live_rows(info, rows):
    row = info[0] * rows + lax.broadcasted_iota(jnp.int32, (rows, 1), 0)
    return (row < info[2]).astype(F32)


def put_parts(buf, base, grad, index, step, order, stride=None):
    for p in range(PARTS):
        at = base + order(p ^ index) * (step if stride is None else stride)
        buf[pl.ds(pl.multiple_of(at, 16), step), :] = grad[p * step : (p + 1) * step]


def hidden_block(pack, width, n2, gf_low):
    up, down = pack.at[0:width], pack.at[width + 16 : 2 * width + 16]
    pre = dot(n2, up[...]) + pack[width : width + 1, :].astype(F32)
    square = pre * pre
    th = jnp.tanh(GELU_C * pre * (1.0 + 0.044715 * square))
    half = 0.5 * (1.0 + th)
    hidden = (pre * half).astype(BF16)
    slope = half + 0.5 * GELU_C * pre * (1.0 - th * th) * (1.0 + 0.134145 * square)
    grad = dot(gf_low, down[...], 1, 1) * slope
    low = grad.astype(BF16)
    return hidden, low, column_sum(grad), dot(hidden, down[...]), dot(low, up[...], 1, 1)


def middle_first(
    info, p0, p1, p2, p3, o0, o1, o2, o3, tok, cot, w0, w1, params, gate_w, pass_w,
    n2_out, ffn_low, y_out, gate2_out, gate_out, mixed_out, ffn_out, gn2_out, vec, keep, send,
):
    me, index = info[0], info[3]
    gain, shift, out_b, gate_b, gain2, shift2, down_b, pass_b = [
        params[n : n + 1, :] for n in range(8)
    ]
    rows, width = tok.shape
    x = tok[...].astype(F32)
    unit, _ = normalized(x)
    n1 = (unit * gain + shift).astype(BF16)
    mixed = out_b
    for p, w in zip((p0, p1, p2, p3), (o0, o1, o2, o3)):
        mixed = mixed + dot(p[...], w[...])
    mixed_out[...] = mixed
    gate = jax.nn.sigmoid(dot(n1, gate_w[...]) + gate_b)
    gate_out[...] = gate
    y = gate * mixed + (1.0 - gate) * x
    y_out[...] = y
    unit2, _ = normalized(y)
    n2 = (unit2 * gain2 + shift2).astype(BF16)
    n2_out[...] = n2
    gate2 = jax.nn.sigmoid(dot(n2, pass_w[...]) + pass_b)
    gate2_out[...] = gate2
    gf = cot[...].astype(F32) * live_rows(info, rows) * gate2
    vec[...] = jnp.zeros_like(vec)
    vec[0:1, :] = column_sum(gf)
    gf_low = gf.astype(BF16)
    ffn_low[...] = gf_low
    n2_turned = n2.T
    ffn_turned = gf_low.T
    ffn, gn2 = down_b, 0.0
    for k, (pack, buf) in enumerate(((w0, keep), (w1, send))):
        hidden, low, columns, more_ffn, more_gn2 = hidden_block(pack, width, n2, gf_low)
        vec[pl.ds(8 + (me ^ k), 1), :] = columns
        ffn = ffn + more_ffn
        gn2 = gn2 + more_gn2
        step = width // PARTS
        put_parts(buf, 0, dot(ffn_turned, hidden).astype(BF16), index, step, reverse)
        put_parts(buf, width, dot(n2_turned, low).astype(BF16), index, step, reverse)
    ffn_out[...] = ffn
    gn2_out[...] = gn2


def middle_second(
    info, o0, o1, o2, o3, tok, cot, w2, w3, params, pass_w,
    n2_in, ffn_low, y_in, gate2_in, gate_in, mixed_in, ffn_in, gn2_in, vec_in,
    out, g0, g1, g2, g3, hid, pre_low, z2_low, z1_low, mixed_low, carry, vec,
    whole2, whole3,
):
    me = info[0]
    quarter = w2.shape[0] // WEIGHT_PARTS
    for part in range(WEIGHT_PARTS):
        at = place((info[3] ^ part) % WEIGHT_PARTS, quarter)
        for whole, parts in ((whole2, w2), (whole3, w3)):
            whole[pl.ds(at, quarter), :] = parts[part * quarter : (part + 1) * quarter]
    gain2 = params[4:5, :]
    rows, width = tok.shape
    n2, gf_low = n2_in[...], ffn_low[...]
    ffn, gn2 = ffn_in[...], gn2_in[...]
    vec[...] = vec_in[...]
    for n, pack in enumerate((whole2, whole3)):
        hidden, low, columns, more_ffn, more_gn2 = hidden_block(pack, width, n2, gf_low)
        hid[n] = hidden
        pre_low[n] = low
        vec[pl.ds(8 + (me ^ (2 + n)), 1), :] = columns
        ffn = ffn + more_ffn
        gn2 = gn2 + more_gn2
    live = live_rows(info, rows)
    gate2, y = gate2_in[...], y_in[...]
    out[...] = ((gate2 * ffn + (1.0 - gate2) * y) * live).astype(BF16)
    gy = cot[...].astype(F32) * live
    z2 = gy * gate2 * (ffn - y) * (1.0 - gate2)
    vec[1:2, :] = column_sum(z2)
    z2l = z2.astype(BF16)
    z2_low[...] = z2l
    gn2 = gn2 + dot(z2l, pass_w[...], 1, 1)
    unit2, scale2 = normalized(y)
    vec[2:3, :] = column_sum(gn2)
    vec[3:4, :] = column_sum(gn2 * unit2)
    g = gn2 * gain2
    gy1 = gy * (1.0 - gate2) + scale2 * (g - row_mean(g) - unit2 * row_mean(g * unit2))
    gate = gate_in[...]
    gm = gy1 * gate
    vec[4:5, :] = column_sum(gm)
    z1 = gm * (mixed_in[...] - tok[...].astype(F32)) * (1.0 - gate)
    vec[5:6, :] = column_sum(z1)
    z1_low[...] = z1.astype(BF16)
    gml = gm.astype(BF16)
    mixed_low[...] = gml
    carry[...] = gy1 * (1.0 - gate)
    for g_out, w in zip((g0, g1, g2, g3), (o0, o1, o2, o3)):
        g_out[...] = dot(gml, w[...], 1, 1).astype(BF16)


ORDER = [int(f"{p:03b}"[::-1], 2) for p in range(PARTS)]
UP_ORDER = [ORDER[p] for p in (0, 1, 4, 5, 2, 3, 6, 7)]
REST_ORDER = [((p >> 1) & 1) | ((p >> 2) << 1) | ((p & 1) << 2) for p in range(PARTS)]


def weight_grads(
    info, hid, pre_low, ffn_low, z2_low, n2, z1_low, mixed_low, tok, params, gate_w,
    p0, p1, p2, p3, vec_in,
    keep, send, vec,
    scratch_gate, scratch_pass,
):
    me, mine = info[0], info[3]
    gain, shift = params[0:1, :], params[1:2, :]
    width = tok.shape[1]
    heads = p0.shape[1]
    unit, _ = normalized(tok[...].astype(F32))
    n1 = (unit * gain + shift).astype(BF16)
    z1l = z1_low[...]
    step = width // PARTS
    small = heads // PARTS
    n2_turned = n2[...].T
    n1_turned = n1.T
    z2l = z2_low[...]
    gml = mixed_low[...]
    ffn_turned = ffn_low[...].T
    pieces = (p0, p1, p2, p3)
    scratch_gate[...] = dot(n1_turned, z1l)
    scratch_pass[...] = dot(n2_turned, z2l)
    for n, buf in enumerate((keep, send)):
        grad = dot(ffn_turned, hid[n]).astype(BF16)
        put_parts(buf, 0, grad, mine, step, reverse)
        grad = dot(n2_turned, pre_low[n]).astype(BF16)
        put_parts(buf, width, grad, mine, step, reverse)
    for k in range(4):
        buf = (keep, send)[k % 2]
        out_grad = dot(pieces[k][...], gml, 0, 0).astype(BF16)
        at = place(me ^ k, heads)
        rest = (out_grad,) + tuple(
            ref[pl.ds(at, heads), :].astype(BF16) for ref in (scratch_gate, scratch_pass)
        )
        for n, grad in enumerate(rest):
            base = 2 * width + (3 * (k // 2) + n) * small
            put_parts(buf, base, grad, mine, small, reverse_rest, 6 * small)
    dz = dot(z1l, gate_w[...], 1, 1)
    vec[...] = vec_in[...]
    vec[6:7, :] = column_sum(dz * unit)
    vec[7:8, :] = column_sum(dz)


def reverse_rest(part):
    return ((part & 2) << 1) | ((part & 1) << 1) | ((part >> 2) & 1)


def reverse(part):
    return ((part & 1) << 2) | (part & 2) | ((part >> 2) & 1)


def backward_blocks(lowest, info, q, k, v, qt, kt, lse, unit_low, weights, keep, send,
    up, upt, dqt, dk, dv, dots, moment, total_cols):
    me, first, total = info[0], info[1], info[2]
    rows = keep.shape[0]
    block = rows
    width = q.shape[1]
    heads = width // HD
    lane_head = lax.broadcasted_iota(jnp.int32, (block, width), 1) // HD
    row_head = lax.broadcasted_iota(jnp.int32, (width, block), 0) // HD

    def key_block(j, unused):
        at_k = place(j, block)
        keys = k[pl.ds(at_k, block), :]
        values = v[pl.ds(at_k, block), :]
        dk[...] = jnp.zeros_like(dk)
        dv[...] = jnp.zeros_like(dv)

        def step(at, masked):
            cols = pl.ds(at, block)
            scaled_t = qt[:, cols]
            scaled = q[pl.ds(at, block), :]
            ups = up[pl.ds(at, block), :]
            ups_t = upt[:, cols]
            for h in range(heads):
                part = slice(HD * h, HD * h + HD)
                scores = dot(keys, jnp.where(row_head == h, scaled_t, BF16(0)))
                if masked:
                    row = at + lax.broadcasted_iota(jnp.int32, (1, block), 1)
                    start = start_of(row, first, total)
                    col = at_k + lax.broadcasted_iota(jnp.int32, (block, block), 0)
                    scores = jnp.where((col >= start) & (col <= row), scores, NEGATIVE)
                probs = jnp.exp(scores - lse[h : h + 1, cols])
                grads = dot(values, jnp.where(row_head == h, ups_t, BF16(0)))
                score_grad = (probs * (grads - dots[h : h + 1, cols])).astype(BF16)
                dv[...] += dot(probs.astype(BF16), jnp.where(lane_head == h, ups, BF16(0)))
                dk[...] += dot(score_grad, jnp.where(lane_head == h, scaled, BF16(0)))
                dqt[part, cols] += dot(kt[part, pl.ds(at_k, block)], score_grad)

        def loop(i, carry):
            at = place(i, block)
            begin = start_of(at, first, total)
            last_start = start_of(at + block - 1, first, total)
            whole = (i > j) & (at_k >= last_start)

            @pl.when(whole)
            def _():
                step(at, False)

            @pl.when(jnp.logical_not(whole) & (at_k + block > begin))
            def _():
                step(at, True)

            return carry

        lax.fori_loop(j, 4, loop, 0)
        grads_t = (
            (dqt[:, pl.ds(at_k, block)] * 0.125).astype(BF16),
            dk[...].T.astype(BF16),
            dv[...].T.astype(BF16),
        )
        unit_rows = unit_low[pl.ds(at_k, block), :]
        spread = 0.0
        for c in range(3):
            spread = spread + dot(grads_t[c], weights[c], 0, 1)
            moment[c] += dot(grads_t[c], unit_rows)
            total_cols[c] += jnp.sum(grads_t[c].astype(F32), axis=1, keepdims=True)
        spread = spread.astype(BF16)
        even = (me ^ j) % 2 == 0

        @pl.when(even)
        def _():
            keep[...] = spread

        @pl.when(jnp.logical_not(even))
        def _():
            send[...] = spread

        return unused

    lax.fori_loop(lowest, lowest + 2, key_block, 0)


def attend_backward_first(
    info, q, k, v, qt, kt, ot, lse, gs, unit_low, weights,
    keep, send, up, upt, dots, dqt, moment, total_cols,
    dk, dv,
):
    me = info[0]
    rows = keep.shape[0]
    for n in range(4):
        at = place(me ^ n, rows)
        g = gs[n * rows : (n + 1) * rows, :]
        up[pl.ds(at, rows), :] = g
        upt[:, pl.ds(at, rows)] = g.T
    weighted = upt[...].astype(F32) * ot[...]
    for h in range(dots.shape[0]):
        dots[h : h + 1, :] = column_sum(weighted[HD * h : HD * h + HD])
    dqt[...] = jnp.zeros_like(dqt)
    moment[...] = jnp.zeros_like(moment)
    total_cols[...] = jnp.zeros_like(total_cols)
    backward_blocks(0, info, q, k, v, qt, kt, lse, unit_low, weights, keep, send,
        up, upt, dqt, dk, dv, dots, moment, total_cols)


def attend_backward_second(
    info, q, k, v, qt, kt, lse, unit_low, weights, up, upt, dots, dqt_in, moment_in, cols_in,
    params, vec_in,
    keep, send, heads_out, vec,
    dk, dv, dqt, moment, total_cols,
):
    mine = info[3]
    gain, shift = params[0:1, :], params[1:2, :]
    width = q.shape[1]
    half = dqt.shape[1] // 2
    dqt[:, half:] = dqt_in[:, half:]
    moment[...] = moment_in[...]
    total_cols[...] = cols_in[...]
    backward_blocks(2, info, q, k, v, qt, kt, lse, unit_low, weights, keep, send,
        up, upt, dqt, dk, dv, dots, moment, total_cols)
    step_rows = width // PARTS
    part_rows = 3 * step_rows
    gain_grad = 0.0
    shift_grad = 0.0
    for c in range(3):
        turned = weights[c].astype(F32).T
        gain_grad = gain_grad + column_sum(turned * moment[c])
        shift_grad = shift_grad + column_sum(turned * total_cols[c])
        grad = (moment[c] * gain + total_cols[c] * shift).astype(BF16)
        for p in range(PARTS):
            at = pl.multiple_of(reverse(p ^ mine) * part_rows + c * step_rows, 16)
            heads_out[pl.ds(at, step_rows), :] = grad[p * step_rows : (p + 1) * step_rows]
    pick = lax.broadcasted_iota(jnp.int32, vec_in.shape, 0)
    sums = vec_in[...] + jnp.where(pick == 6, gain_grad, 0.0) + jnp.where(pick == 7, shift_grad, 0.0)
    vec[...] = sums.astype(BF16)


def tokens_backward(tok, own, got, z1_low, gate_w, carry, params, out):
    unit, scale = normalized(tok[...].astype(F32))
    grad = own[...].astype(F32) + got[...].astype(F32) + dot(z1_low[...], gate_w[...], 1, 1)
    h = grad * params[0:1, :]
    out[...] = (
        carry[...] + scale * (h - row_mean(h) - unit * row_mean(h * unit))
    ).astype(BF16)


def each_part(info, refs, rows, order=ORDER):
    pos = 0
    for ref in refs:
        for n in range(ref.shape[0] // rows):
            yield order[pos] ^ info[3], ref, n * rows
            pos += 1


def unpack_ffn(info, d0, d1, d2, u0, u1, u2, down, up, turned):
    step = down.shape[0] // PARTS
    for p, ref, at in each_part(info, (d0, d1, d2), step):
        turned[pl.ds(place(p, step), step), :] = ref[at : at + step].astype(F32)
    for p, ref, at in each_part(info, (u0, u1, u2), step, UP_ORDER):
        up[pl.ds(place(p, step), step), :] = ref[at : at + step].astype(F32)
    down[...] = turned[...].T


def unpack_rest(info, s0, s1, s2, out, gates):
    rows = out.shape[0]
    step = rows // PARTS
    for p, ref, at in each_part(info, (s0, s1, s2), 3 * step, REST_ORDER):
        out[pl.ds(place(p, step), step), :] = ref[at : at + step].astype(F32)
        for n in range(2):
            first = at + (n + 1) * step
            gates[pl.ds(pl.multiple_of(n * rows + p * step, step), step), :] = ref[
                first : first + step
            ]


def unpack_heads(info, s0, s1, s2, heads, turned):
    step = heads.shape[2] // PARTS
    for p, ref, at in each_part(info, (s0, s1, s2), 3 * step):
        for c in range(3):
            turned[c, pl.ds(place(p, step), step), :] = ref[at + c * step : at + (c + 1) * step].astype(F32)
    for c in range(3):
        heads[c] = turned[c].T


def unpack_gates(info, s0, s1, s2, s3, gate, passed):
    rows = gate.shape[0] // 4
    for k, ref in enumerate((s0, s1, s2, s3)):
        at = place(info[0] ^ k, rows)
        gate[pl.ds(at, rows), :] = ref[0:rows].astype(F32)
        passed[pl.ds(at, rows), :] = ref[rows : 2 * rows].astype(F32)


def unpack_vectors(info, one, two, *outs):
    sums = one[...] + two[...]
    for n in range(8):
        outs[n][...] = sums[n : n + 1]
    pick = lax.broadcasted_iota(jnp.int32, sums.shape, 0) == 8 + info[0]
    outs[8][...] = column_sum(jnp.where(pick, sums, 0.0))


def swap_tensor(values, mask):
    return lax.ppermute(values, "tensor", [(i, i ^ mask) for i in range(4)])


def swap_dp(values, mask):
    return lax.ppermute(values, "dp", [(i, i ^ mask) for i in range(lax.axis_size("dp"))])


def fold(*terms):
    return sum(term.astype(F32) for term in terms).astype(BF16)


def scatter(values, axis, mask):
    half = values.shape[0] // 2
    got = yield values[half:], axis, mask
    return fold(values[:half], got)


def reduce_dp(values, masks, more=None):
    extra = 0 if more is None else more.shape[0]
    for mask in masks:
        half = values.shape[0] // 2
        sent = values[half:]
        if extra:
            sent = jnp.concatenate([sent, more])
        got = yield sent, "dp", mask
        values = fold(values[:half], got[:half])
        if extra:
            more = fold(more, got[half:])
    mask = 4
    while mask < lax.axis_size("dp"):
        size = values.shape[0]
        if mask == 4:
            sent = [values[size // 2 :], values[: size // 2]]
        else:
            sent = [values]
        if extra:
            sent = sent + [more]
        got = yield jnp.concatenate(sent), "dp", mask
        values = fold(values, got[:size])
        if extra:
            more = fold(more, got[size:])
        mask *= 2
    return (values, more) if extra else values


def gather_dp(values, masks=(2, 1)):
    s2 = yield values, "dp", masks[0]
    s3 = yield jnp.concatenate([values, s2]), "dp", masks[1]
    return values, s2, s3


def split_rest(values):
    step = values.shape[0] // PARTS
    shares = [values[n * step : (n + 1) * step] for n in range(PARTS)]
    return jnp.concatenate(shares[0::2]), jnp.concatenate(shares[1::2])


def run_chains(chains):
    results = [None] * len(chains)
    waiting = [None] * len(chains)
    alive = list(range(len(chains)))
    while alive:
        for n in list(alive):
            try:
                values, axis, mask = chains[n].send(waiting[n])
            except StopIteration as stop:
                results[n] = stop.value
                alive.remove(n)
                continue
            waiting[n] = (swap_dp if axis == "dp" else swap_tensor)(values, mask)
    return results


def body(
    tokens,
    norm_gain,
    norm_shift,
    heads_weight,
    output_weight,
    output_bias,
    gate_weight,
    gate_bias,
    second_gain,
    second_shift,
    up_weight,
    up_bias,
    down_weight,
    down_bias,
    pass_weight,
    pass_bias,
    lengths,
    owners,
    cotangent,
):
    rows, width = tokens.shape
    total_rows = 4 * rows
    head_width = heads_weight.shape[2]
    me = lax.axis_index("tensor")
    params = jnp.stack(
        [norm_gain, norm_shift, output_bias, gate_bias, second_gain, second_shift]
        + [down_bias, pass_bias]
    )
    split_heads = heads_weight.transpose(1, 0, 2)

    def kept(count):
        kinds = [shape(count, width)] + [shape(count, head_width)] * 3
        return kinds + [shape(head_width, count)] * 2

    tok2 = swap_tensor(tokens, 2)
    tok1 = swap_tensor(tokens, 1)
    state = [(head_width, 2 * rows), (8, 2 * rows), (8, 2 * rows)]
    info, *near = call(
        attend_near,
        "attend_near",
        (lengths, owners, tokens, tok1, params, split_heads),
        [shape(4, dtype=jnp.int32)]
        + kept(2 * rows)
        + [shape(head_width, 2 * rows)]
        + [shape(*dims, dtype=F32) for dims in state],
        scalars=2,
        micros=6,
        mib=12,
    )
    up_held, down_held, info = lax.optimization_barrier((up_weight, down_weight, info))
    bias_rows = jnp.broadcast_to(up_bias[None, :], (16, width))
    pack0 = jnp.concatenate([up_held, bias_rows, down_held, jnp.zeros((48, width), BF16)])
    quarter = pack0.shape[0] // WEIGHT_PARTS
    sent = lax.dynamic_slice_in_dim(
        pack0, lax.axis_index("dp") % WEIGHT_PARTS * quarter, quarter, 0
    )
    sent, out_held, tok2, *near = lax.optimization_barrier((sent, output_weight, tok2, *near))
    out2 = swap_tensor(out_held, 2)
    part0 = swap_tensor(sent, 2)
    tok3 = swap_tensor(tok2, 1)

    later = kept(total_rows) + [shape(head_width, total_rows, dtype=F32)]
    unit, q, key, v, qt, kt, ot, lse, a0, a1, a2, a3 = call(
        attend_far,
        "attend_far",
        (info, tok2, tok3, params, split_heads) + tuple(near),
        later
        + [shape(head_width // HD, total_rows, dtype=F32)]
        + [shape(rows, head_width)] * 4,
        [pltpu.VMEM(item.shape, item.dtype) for item in kept(2 * rows)]
        + [
            pltpu.VMEM((total_rows, head_width), BF16),
            pltpu.VMEM((head_width, total_rows), BF16),
            pltpu.VMEM((head_width, total_rows), BF16),
            pltpu.VMEM((head_width, total_rows), F32),
        ]
        + [pltpu.VMEM((dims[0], rows), F32) for dims in state]
        + [pltpu.SemaphoreType.DMA((13,))],
        micros=10,
        mib=20,
        far=range(len(later)),
    )
    a0, a1, a2, a3, out2, part0, pack0, out_held = lax.optimization_barrier(
        (a0, a1, a2, a3, out2, part0, pack0, output_weight)
    )
    pack1 = swap_tensor(pack0, 1)
    out1 = swap_tensor(out_held, 1)
    out3 = swap_tensor(out2, 1)
    p0, p1, p2, p3 = a0, swap_tensor(a1, 1), swap_tensor(a2, 2), swap_tensor(a3, 3)
    part1, part2 = swap_dp(part0, 1), swap_dp(part0, 2)
    p1, p2, p3, out3, part1, part2 = lax.optimization_barrier((p1, p2, p3, out3, part1, part2))
    part3 = swap_dp(part2, 1)
    outs = (output_weight, out1, out2, out3)
    square, square32 = shape(rows, width), shape(rows, width, dtype=F32)
    n2, ffn_low, y, gate2, gate, mixed, ffn, gn2, vec, keep0, send0 = call(
        middle_first,
        "middle_first",
        (info, p0, p1, p2, p3) + outs + (tokens, cotangent, pack0, pack1, params)
        + (gate_weight, pass_weight),
        [square] * 2
        + [square32] * 6
        + [shape(16, width, dtype=F32)]
        + [shape(2 * width, width)] * 2,
        micros=9,
        mib=20,
    )
    n2, part3, send0 = lax.optimization_barrier((n2, part3, send0))
    parts2 = jnp.concatenate([part0, part1, part2, part3])
    parts3 = swap_tensor(parts2, 1)
    got0 = swap_tensor(send0, 1)
    output, g0, g1, g2, g3, hid, pre_low, z2_low, z1_low, mixed_low, carry, vec = call(
        middle_second,
        "middle_second",
        (info,) + outs + (tokens, cotangent, parts2, parts3, params, pass_weight)
        + (n2, ffn_low, y, gate2, gate, mixed, ffn, gn2, vec),
        [square]
        + [shape(rows, head_width)] * 4
        + [shape(2, rows, width)] * 2
        + [square] * 3
        + [square32, shape(16, width, dtype=F32)],
        [pltpu.VMEM(pack0.shape, BF16)] * 2,
        micros=7,
        mib=20,
    )
    g1, g2, g3 = swap_tensor(g1, 1), swap_tensor(g2, 2), swap_tensor(g3, 3)
    keep, send, vec = call(
        weight_grads,
        "weight_grads",
        (info, hid, pre_low, ffn_low, z2_low, n2, z1_low, mixed_low, tokens, params)
        + (gate_weight, p0, p1, p2, p3, vec),
        [shape(2 * width + 6 * head_width, width)] * 2
        + [shape(16, width, dtype=F32)],
        [pltpu.VMEM((width, width), F32)] * 2,
        micros=4,
        mib=14,
    )
    g1, g2, g3, got0, keep, send, vec = lax.optimization_barrier(
        (g1, g2, g3, got0, keep, send, vec)
    )
    got = swap_tensor(send, 1)
    near = fold(keep0, got0)
    total = fold(keep, got)
    half = width // 2
    down0, up_keep = near[:width], near[width:]
    down2, up_send = total[:width], total[width : 2 * width]
    rest = total[2 * width :]
    down_send = jnp.concatenate([down0[half:], down2[half:]])
    down_keep = jnp.concatenate([down0[:half], down2[:half]])
    half = rest.shape[0] // 2
    down_send, up_send, rest_send, vec = lax.optimization_barrier(
        (down_send, up_send, rest[half:], vec)
    )
    down_got = swap_dp(down_send, 1)
    up_got = swap_tensor(up_send, 2)
    rest_got = swap_dp(rest_send, 2)
    blocks = [pltpu.VMEM((rows, head_width), F32)] * 2
    totals = [(head_width, total_rows), (3, head_width, width), (3, head_width, 1)]
    rows_keep0, rows_send0, up, upt, dots, dqt, moment, total_cols = call(
        attend_backward_first,
        "attend_backward_first",
        (info, q, key, v, qt, kt, ot, lse, jnp.concatenate([g0, g1, g2, g3]), unit, split_heads),
        [square] * 2
        + [shape(total_rows, head_width), shape(head_width, total_rows)]
        + [shape(head_width // HD, total_rows, dtype=F32)]
        + [shape(*dims, dtype=F32) for dims in totals],
        blocks,
        micros=12,
        mib=12,
    )
    rows_keep0, rows_send0, dqt, down_got, up_got, rest_got = lax.optimization_barrier(
        (rows_keep0, rows_send0, dqt, down_got, up_got, rest_got)
    )
    down_part = fold(down_keep, down_got)
    up_part = fold(up_keep, up_got)
    rest = fold(rest[:half], rest_got)
    half = down_part.shape[0] // 2
    down_send, up_send, dqt = lax.optimization_barrier((down_part[half:], up_part[half:], dqt))
    down_got = swap_tensor(down_send, 2)
    up_got = swap_dp(up_send, 1)
    rest_kept, rest_sent = split_rest(rest)
    rest_got = swap_tensor(rest_sent, 2)
    rows_got0 = swap_tensor(rows_send0, 1)
    keep1, send1, heads_sum, vec = call(
        attend_backward_second,
        "attend_backward_second",
        (info, q, key, v, qt, kt, lse, unit, split_heads, up, upt, dots, dqt, moment)
        + (total_cols, params, vec),
        [square] * 2 + [shape(3 * head_width, width), shape(16, width)],
        blocks + [pltpu.VMEM(dims, F32) for dims in totals],
        micros=7,
        mib=12,
    )
    down_got, up_got, rest_got, rows_got0, heads_sum, vec, keep1, send1 = lax.optimization_barrier(
        (down_got, up_got, rest_got, rows_got0, heads_sum, vec, keep1, send1)
    )

    down_part, up_part = fold(down_part[:half], down_got), fold(up_part[:half], up_got)
    step = width // PARTS
    both = jnp.concatenate(
        [
            piece[n * step : (n + 1) * step]
            for n in range(PARTS // 2)
            for piece in (down_part, up_part)
        ]
    )

    size = both.shape[0] // 2
    first_ffn = fold(both[:size], swap_dp(both[size:], 2))

    def heads_chain(values, vec):
        size = values.shape[0] // 2
        got = yield jnp.concatenate([values[size:], vec]), "dp", 1
        values, vec = fold(values[:size], got[:size]), fold(vec, got[size:])
        values, _ = lax.optimization_barrier((values, first_ffn))
        values, vec = yield from reduce_dp(values, (2,), vec)
        vec = vec.astype(F32)
        s2 = yield values, "dp", 2
        got = yield vec, "tensor", 1
        vec = vec + got
        got = yield vec, "tensor", 2
        vectors = call(
            unpack_vectors,
            "unpack_vectors",
            (info, vec, got),
            [shape(1, width, dtype=F32)] * 9,
        )
        s3 = yield jnp.concatenate([values, s2]), "dp", 1
        (heads_grad,) = call(
            unpack_heads,
            "unpack_heads",
            (info, values, s2, s3),
            [shape(3, width, head_width, dtype=F32)],
            [pltpu.VMEM((3, head_width, width), F32)],
        )
        return heads_grad, [v.reshape(width) for v in vectors]

    def rows_chain():
        got = yield send1, "tensor", 1
        lower, upper = fold(rows_keep0, rows_got0), fold(keep1, got)
        is_lower = me < 2
        near = jnp.where(is_lower, lower, upper)
        far = yield jnp.where(is_lower, upper, lower), "tensor", 2
        return call(
            tokens_backward,
            "tokens_backward",
            (tokens, near, far, z1_low, gate_weight, carry, params),
            [square],
            scalars=0,
        )[0]

    def rest_chain(values):
        values = yield from reduce_dp(values, (1,))
        parts = yield from gather_dp(values, (1, 2))
        out_grad, gates = call(
            unpack_rest,
            "unpack_rest",
            (info,) + parts,
            [shape(head_width, width, dtype=F32), shape(2 * head_width, width)],
        )
        gates2 = yield gates, "tensor", 2
        other = yield jnp.concatenate([gates, gates2]), "tensor", 1
        gate_grad, pass_grad = call(
            unpack_gates,
            "unpack_gates",
            (info, gates, other[: 2 * head_width], gates2, other[2 * head_width :]),
            [shape(width, width, dtype=F32)] * 2,
        )
        return out_grad, gate_grad, pass_grad

    def ffn_chain(values):
        values = yield from reduce_dp(values, ())
        d0 = jnp.concatenate([values[:step], values[2 * step : 3 * step]])
        u0 = jnp.concatenate([values[step : 2 * step], values[3 * step :]])
        d1 = yield d0, "dp", 2
        u1 = yield u0, "dp", 1
        d2 = yield jnp.concatenate([d0, d1]), "dp", 1
        u2 = yield jnp.concatenate([u0, u1]), "dp", 2
        return d0, d1, d2, u0, u1, u2

    (tokens_grad,) = run_chains([rows_chain()])
    (
        (out_grad, gate_grad, pass_grad),
        ffn_parts,
        (heads_grad, vectors),
    ) = run_chains(
        [
            rest_chain(fold(rest_kept, rest_got)),
            ffn_chain(first_ffn),
            heads_chain(heads_sum, vec),
        ]
    )
    down_grad, up_grad = call(
        unpack_ffn,
        "unpack_ffn",
        (info,) + ffn_parts,
        [shape(width, width, dtype=F32)] * 2,
        [pltpu.VMEM((width, width), F32)],
    )
    (
        down_bias_grad,
        pass_bias_grad,
        second_shift_grad,
        second_gain_grad,
        output_bias_grad,
        gate_bias_grad,
        norm_gain_grad,
        norm_shift_grad,
        up_bias_grad,
    ) = vectors
    return (
        output,
        tokens_grad,
        norm_gain_grad,
        norm_shift_grad,
        heads_grad.transpose(1, 0, 2),
        out_grad,
        output_bias_grad,
        gate_grad,
        gate_bias_grad,
        second_gain_grad,
        second_shift_grad,
        up_grad,
        up_bias_grad,
        down_grad,
        down_bias_grad,
        pass_grad,
        pass_bias_grad,
    )


def solution(mesh):
    placed = (
        P(("dp", "tensor"), None),
        P(),
        P(),
        P(None, None, "tensor"),
        P("tensor", None),
        P(),
        P(),
        P(),
        P(),
        P(),
        P(None, "tensor"),
        P("tensor"),
        P("tensor", None),
        P(),
        P(),
        P(),
        P(),
        P(),
        P(("dp", "tensor"), None),
    )
    return jax.shard_map(
        body,
        mesh=mesh,
        in_specs=placed,
        out_specs=(
            P(("dp", "tensor"), None),
            P(("dp", "tensor"), None),
            P(),
            P(),
            P(None, None, "tensor"),
            P("tensor", None),
            P(),
            P(),
            P(),
            P(),
            P(),
            P(None, "tensor"),
            P("tensor"),
            P("tensor", None),
            P(),
            P(),
            P(),
        ),
        check_vma=False,
    )
```

```python
import functools

import jax
import jax.numpy as jnp
from jax import lax
from jax.experimental import pallas as pl
from jax.experimental.pallas import tpu as pltpu
from jax.sharding import PartitionSpec as P

HD = 64
EPS = 1e-05
NEGATIVE = -1e30
GELU_C = 0.7978845608028654
F32 = jnp.float32
BF16 = jnp.bfloat16
VMEM = pl.BlockSpec(memory_space=pltpu.VMEM)
HBM = pl.BlockSpec(memory_space=pltpu.HBM)
SMEM = pl.BlockSpec(memory_space=pltpu.SMEM)
PARTS = 8
WEIGHT_PARTS = 4


def dot(left, right, left_dim=1, right_dim=0):
    return lax.dot_general(
        left, right, (((left_dim,), (right_dim,)), ((), ())), preferred_element_type=F32
    )


def column_sum(values):
    return jnp.sum(values, axis=0, keepdims=True)


def row_mean(values):
    return jnp.mean(values, axis=-1, keepdims=True)


def normalized(values):
    centred = values - row_mean(values)
    scale = lax.rsqrt(row_mean(centred * centred) + EPS)
    return centred * scale, scale


def place(index, size):
    return pl.multiple_of(index * size, size)


def start_of(row, first, total):
    return jnp.where(row < first, 0, jnp.where(row < total, first, row))


def call(body, name, operands, outs, scratch=(), scalars=1, micros=2, mib=12, far=()):
    return pl.pallas_call(
        body,
        cost_estimate=pl.CostEstimate(flops=int(micros * 1.1e9), bytes_accessed=0, transcendentals=0),
        out_shape=[
            pltpu.HBM(item.shape, item.dtype) if n in far else item for n, item in enumerate(outs)
        ],
        in_specs=[SMEM] * scalars + [VMEM] * (len(operands) - scalars),
        out_specs=[
            HBM if n in far else SMEM if item.dtype == jnp.int32 else VMEM
            for n, item in enumerate(outs)
        ],
        scratch_shapes=list(scratch),
        compiler_params=pltpu.CompilerParams(vmem_limit_bytes=mib << 20),
        name=name,
    )(*operands)


def shape(*dims, dtype=BF16):
    return jax.ShapeDtypeStruct(dims, dtype)


def project(tok, params, weights):
    unit, _ = normalized(tok[...].astype(F32))
    normed = (unit * params[0:1, :] + params[1:2, :]).astype(BF16)
    q, key, v = [dot(normed, weights[c]).astype(BF16) for c in range(3)]
    return unit.astype(BF16), q * BF16(0.125), key, v


def attend(info, i, count, last, fresh, block, queries_t, keys, values_t, state):
    first, total = info[1], info[2]
    acc, sum_row, top_row = state
    width = acc.shape[0]
    base = i * block
    head = lax.broadcasted_iota(jnp.int32, (width, block), 0) // HD
    q_heads = [jnp.where(head == h, queries_t, BF16(0)) for h in range(width // HD)]
    row = base + lax.broadcasted_iota(jnp.int32, (1, block), 1)
    start = start_of(row, first, total)
    last_start = start_of(base + block - 1, first, total)

    @pl.when(fresh)
    def _():
        acc[...] = jnp.zeros_like(acc)
        sum_row[...] = jnp.zeros_like(sum_row)
        top_row[...] = jnp.full_like(top_row, NEGATIVE)

    def step(j, masked):
        at = place(j, block)
        key_rows = keys(j)
        for h in range(width // HD):
            part = slice(HD * h, HD * h + HD)
            scores = dot(key_rows, q_heads[h])
            if masked:
                back = (row - at) - lax.broadcasted_iota(jnp.int32, (block, block), 0)
                inside = back.astype(jnp.uint32) <= (row - start).astype(jnp.uint32)
                scores = jnp.where(inside, scores, NEGATIVE)
            before = top_row[h : h + 1, :]
            top = jnp.maximum(before, jnp.max(scores, axis=0, keepdims=True))
            fade = jnp.exp(before - top)
            exponent = jnp.exp(scores - top)
            mixed = dot(values_t(part, j), exponent.astype(BF16))
            sum_row[h : h + 1, :] = sum_row[h : h + 1, :] * fade + column_sum(exponent)
            acc[part, :] = acc[part, :] * fade + mixed
            top_row[h : h + 1, :] = top

    def loop(n, carry):
        j = last - n
        masked = (j == i) | (j * block < last_start)

        step(j, True)

        return carry

    lax.fori_loop(0, count, loop, 0)


def lowest_block(info, i, block):
    return start_of(i * block, info[1], info[2]) // block


def sequences(lengths, owners, info):
    here = lax.axis_index("dp")

    def entry(e, carry):
        first, seen, total = carry
        mine = owners[e] == here
        length = jnp.where(mine, lengths[e], 0)
        first = jnp.where(seen == 0, length, first)
        return first, seen + mine.astype(jnp.int32), total + length

    zero = jnp.int32(0)
    first, seen, total = lax.fori_loop(0, lengths.shape[0], entry, (zero, zero, zero))
    info[0] = lax.axis_index("tensor")
    info[1] = first
    info[2] = total
    info[3] = here % PARTS


def attend_near(
    lengths, owners, t0, t1, params, weights,
    info, unit_out, q_out, k_out, v_out, qt_out, kt_out, vt_out, acc, sum_row, top_row,
):
    sequences(lengths, owners, info)
    me = info[0]
    rows = t0.shape[0]
    for k, tok in enumerate((t0, t1)):
        at = place((me ^ k) % 2, rows)
        unit, q, key, v = project(tok, params, weights)
        unit_out[pl.ds(at, rows), :] = unit
        for out, turned, value in ((q_out, qt_out, q), (k_out, kt_out, key), (v_out, vt_out, v)):
            out[pl.ds(at, rows), :] = value
            turned[:, pl.ds(at, rows)] = value.T
    base = me // 2 * 2
    for n in range(2):
        i = base + n
        lanes = slice(n * rows, (n + 1) * rows)
        attend(
            info,
            i,
            i + 1 - jnp.maximum(lowest_block(info, i, rows), base),
            i,
            True,
            rows,
            qt_out[:, lanes],
            lambda j: k_out[pl.ds(place(j - base, rows), rows), :],
            lambda part, j: vt_out[part, pl.ds(place(j - base, rows), rows)],
            [ref.at[:, lanes] for ref in (acc, sum_row, top_row)],
        )


def attend_far(
    info, t2, t3, params, weights,
    unit_in, q_in, k_in, v_in, qt_in, kt_in, vt_in, acc_in, sum_in, top_in,
    unit_far, q_far, k_far, v_far, qt_far, kt_far, ot_far, lse_out, a0, a1, a2, a3,
    unit_new, q_new, k_new, v_new, qt_new, kt_new, keys, qt, vt, ot, acc, sum_row, top_row, done,
):
    me = info[0]
    rows = t2.shape[0]
    own = me // 2
    for k, tok in ((2, t2), (3, t3)):
        at = place((me ^ k) % 2, rows)
        unit, q, key, v = project(tok, params, weights)
        unit_new[pl.ds(at, rows), :] = unit
        q_new[pl.ds(at, rows), :] = q
        k_new[pl.ds(at, rows), :] = key
        v_new[pl.ds(at, rows), :] = v
        qt_new[:, pl.ds(at, rows)] = q.T
        kt_new[:, pl.ds(at, rows)] = key.T
        vt[:, pl.ds(place(me ^ k, rows), rows)] = v.T
    copies = []
    both = 2 * rows
    here, there = pl.ds(place(own, both), both), pl.ds(place(1 - own, both), both)
    for old, new, far in (
        (unit_in, unit_new, unit_far),
        (q_in, q_new, q_far),
        (k_in, k_new, k_far),
        (v_in, v_new, v_far),
    ):
        copies.append((old, far.at[here]))
        copies.append((new, far.at[there]))
    for old, new, far in ((qt_in, qt_new, qt_far), (kt_in, kt_new, kt_far)):
        copies.append((old, far.at[:, here]))
        copies.append((new, far.at[:, there]))
    copies.append((ot, ot_far))
    copies = [pltpu.make_async_copy(a, b, done.at[n]) for n, (a, b) in enumerate(copies)]
    for copy in copies[:-1]:
        copy.start()
    keys[here, :] = k_in[...]
    keys[there, :] = k_new[...]
    qt[:, here] = qt_in[...]
    qt[:, there] = qt_new[...]
    vt[:, here] = vt_in[...]

    def query_block(i, unused):
        other = i // 2 != own
        lanes = pl.ds(place(i, rows), rows)
        old = pl.ds(place(i % 2, rows), rows)
        lowest = lowest_block(info, i, rows)

        @pl.when(jnp.logical_not(other))
        def _():
            acc[...] = acc_in[:, old]
            sum_row[...] = sum_in[:, old]
            top_row[...] = top_in[:, old]

        attend(
            info,
            i,
            jnp.where(other, i + 1 - lowest, jnp.where(own == 1, jnp.maximum(2 - lowest, 0), 0)),
            jnp.where(other, i, 1),
            other,
            rows,
            qt[:, lanes],
            lambda j: keys[pl.ds(place(j, rows), rows), :],
            lambda part, j: vt[part, pl.ds(place(j, rows), rows)],
            (acc, sum_row, top_row),
        )
        for h in range(acc.shape[0] // HD):
            part = slice(HD * h, HD * h + HD)
            summed = sum_row[h : h + 1, :]
            ot[part, lanes] = acc[part, :] / summed
            lse_out[h : h + 1, lanes] = top_row[h : h + 1, :] + jnp.log(summed)
        return unused

    lax.fori_loop(0, 4, query_block, 0)
    copies[-1].start()
    for k, out in enumerate((a0, a1, a2, a3)):
        at = place(me ^ k, rows)
        out[...] = ot[:, pl.ds(at, rows)].T.astype(BF16)
    for copy in copies:
        copy.wait()


def live_rows(info, rows):
    row = info[0] * rows + lax.broadcasted_iota(jnp.int32, (rows, 1), 0)
    return (row < info[2]).astype(F32)


def put_parts(buf, base, grad, index, step, order, stride=None):
    for p in range(PARTS):
        at = base + order(p ^ index) * (step if stride is None else stride)
        buf[pl.ds(pl.multiple_of(at, 16), step), :] = grad[p * step : (p + 1) * step]


def hidden_block(pack, width, n2, gf_low):
    up, down = pack.at[0:width], pack.at[width + 16 : 2 * width + 16]
    pre = dot(n2, up[...]) + pack[width : width + 1, :].astype(F32)
    square = pre * pre
    th = jnp.tanh(GELU_C * pre * (1.0 + 0.044715 * square))
    half = 0.5 * (1.0 + th)
    hidden = (pre * half).astype(BF16)
    slope = half + 0.5 * GELU_C * pre * (1.0 - th * th) * (1.0 + 0.134145 * square)
    grad = dot(gf_low, down[...], 1, 1) * slope
    low = grad.astype(BF16)
    return hidden, low, column_sum(grad), dot(hidden, down[...]), dot(low, up[...], 1, 1)


def middle_first(
    info, p0, p1, p2, p3, o0, o1, o2, o3, tok, cot, w0, w1, params, gate_w, pass_w,
    n2_out, ffn_low, y_out, gate2_out, gate_out, mixed_out, ffn_out, gn2_out, vec, keep, send,
):
    me, index = info[0], info[3]
    gain, shift, out_b, gate_b, gain2, shift2, down_b, pass_b = [
        params[n : n + 1, :] for n in range(8)
    ]
    rows, width = tok.shape
    x = tok[...].astype(F32)
    unit, _ = normalized(x)
    n1 = (unit * gain + shift).astype(BF16)
    mixed = out_b
    for p, w in zip((p0, p1, p2, p3), (o0, o1, o2, o3)):
        mixed = mixed + dot(p[...], w[...])
    mixed_out[...] = mixed
    gate = jax.nn.sigmoid(dot(n1, gate_w[...]) + gate_b)
    gate_out[...] = gate
    y = gate * mixed + (1.0 - gate) * x
    y_out[...] = y
    unit2, _ = normalized(y)
    n2 = (unit2 * gain2 + shift2).astype(BF16)
    n2_out[...] = n2
    gate2 = jax.nn.sigmoid(dot(n2, pass_w[...]) + pass_b)
    gate2_out[...] = gate2
    gf = cot[...].astype(F32) * live_rows(info, rows) * gate2
    vec[...] = jnp.zeros_like(vec)
    vec[0:1, :] = column_sum(gf)
    gf_low = gf.astype(BF16)
    ffn_low[...] = gf_low
    n2_turned = n2.T
    ffn_turned = gf_low.T
    ffn, gn2 = down_b, 0.0
    for k, (pack, buf) in enumerate(((w0, keep), (w1, send))):
        hidden, low, columns, more_ffn, more_gn2 = hidden_block(pack, width, n2, gf_low)
        vec[pl.ds(8 + (me ^ k), 1), :] = columns
        ffn = ffn + more_ffn
        gn2 = gn2 + more_gn2
        step = width // PARTS
        put_parts(buf, 0, dot(ffn_turned, hidden).astype(BF16), index, step, reverse)
        put_parts(buf, width, dot(n2_turned, low).astype(BF16), index, step, reverse)
    ffn_out[...] = ffn
    gn2_out[...] = gn2


def middle_second(
    info, o0, o1, o2, o3, tok, cot, w2, w3, params, pass_w,
    n2_in, ffn_low, y_in, gate2_in, gate_in, mixed_in, ffn_in, gn2_in, vec_in,
    out, g0, g1, g2, g3, hid, pre_low, z2_low, z1_low, mixed_low, carry, vec,
    whole2, whole3,
):
    me = info[0]
    quarter = w2.shape[0] // WEIGHT_PARTS
    for part in range(WEIGHT_PARTS):
        at = place((info[3] ^ part) % WEIGHT_PARTS, quarter)
        for whole, parts in ((whole2, w2), (whole3, w3)):
            whole[pl.ds(at, quarter), :] = parts[part * quarter : (part + 1) * quarter]
    gain2 = params[4:5, :]
    rows, width = tok.shape
    n2, gf_low = n2_in[...], ffn_low[...]
    ffn, gn2 = ffn_in[...], gn2_in[...]
    vec[...] = vec_in[...]
    for n, pack in enumerate((whole2, whole3)):
        hidden, low, columns, more_ffn, more_gn2 = hidden_block(pack, width, n2, gf_low)
        hid[n] = hidden
        pre_low[n] = low
        vec[pl.ds(8 + (me ^ (2 + n)), 1), :] = columns
        ffn = ffn + more_ffn
        gn2 = gn2 + more_gn2
    live = live_rows(info, rows)
    gate2, y = gate2_in[...], y_in[...]
    out[...] = ((gate2 * ffn + (1.0 - gate2) * y) * live).astype(BF16)
    gy = cot[...].astype(F32) * live
    z2 = gy * gate2 * (ffn - y) * (1.0 - gate2)
    vec[1:2, :] = column_sum(z2)
    z2l = z2.astype(BF16)
    z2_low[...] = z2l
    gn2 = gn2 + dot(z2l, pass_w[...], 1, 1)
    unit2, scale2 = normalized(y)
    vec[2:3, :] = column_sum(gn2)
    vec[3:4, :] = column_sum(gn2 * unit2)
    g = gn2 * gain2
    gy1 = gy * (1.0 - gate2) + scale2 * (g - row_mean(g) - unit2 * row_mean(g * unit2))
    gate = gate_in[...]
    gm = gy1 * gate
    vec[4:5, :] = column_sum(gm)
    z1 = gm * (mixed_in[...] - tok[...].astype(F32)) * (1.0 - gate)
    vec[5:6, :] = column_sum(z1)
    z1_low[...] = z1.astype(BF16)
    gml = gm.astype(BF16)
    mixed_low[...] = gml
    carry[...] = gy1 * (1.0 - gate)
    for g_out, w in zip((g0, g1, g2, g3), (o0, o1, o2, o3)):
        g_out[...] = dot(gml, w[...], 1, 1).astype(BF16)


ORDER = [int(f"{p:03b}"[::-1], 2) for p in range(PARTS)]
UP_ORDER = [ORDER[p] for p in (0, 1, 4, 5, 2, 3, 6, 7)]
REST_ORDER = [((p >> 1) & 1) | ((p >> 2) << 1) | ((p & 1) << 2) for p in range(PARTS)]


def weight_grads(
    info, hid, pre_low, ffn_low, z2_low, n2, z1_low, mixed_low, tok, params, gate_w,
    p0, p1, p2, p3, vec_in,
    keep, send, vec,
    scratch_gate, scratch_pass,
):
    me, mine = info[0], info[3]
    gain, shift = params[0:1, :], params[1:2, :]
    width = tok.shape[1]
    heads = p0.shape[1]
    unit, _ = normalized(tok[...].astype(F32))
    n1 = (unit * gain + shift).astype(BF16)
    z1l = z1_low[...]
    step = width // PARTS
    small = heads // PARTS
    n2_turned = n2[...].T
    n1_turned = n1.T
    z2l = z2_low[...]
    gml = mixed_low[...]
    ffn_turned = ffn_low[...].T
    pieces = (p0, p1, p2, p3)
    scratch_gate[...] = dot(n1_turned, z1l)
    scratch_pass[...] = dot(n2_turned, z2l)
    for n, buf in enumerate((keep, send)):
        grad = dot(ffn_turned, hid[n]).astype(BF16)
        put_parts(buf, 0, grad, mine, step, reverse)
        grad = dot(n2_turned, pre_low[n]).astype(BF16)
        put_parts(buf, width, grad, mine, step, reverse)
    for k in range(4):
        buf = (keep, send)[k % 2]
        out_grad = dot(pieces[k][...], gml, 0, 0).astype(BF16)
        at = place(me ^ k, heads)
        rest = (out_grad,) + tuple(
            ref[pl.ds(at, heads), :].astype(BF16) for ref in (scratch_gate, scratch_pass)
        )
        for n, grad in enumerate(rest):
            base = 2 * width + (3 * (k // 2) + n) * small
            put_parts(buf, base, grad, mine, small, reverse_rest, 6 * small)
    dz = dot(z1l, gate_w[...], 1, 1)
    vec[...] = vec_in[...]
    vec[6:7, :] = column_sum(dz * unit)
    vec[7:8, :] = column_sum(dz)


def reverse_rest(part):
    return ((part & 2) << 1) | ((part & 1) << 1) | ((part >> 2) & 1)


def reverse(part):
    return ((part & 1) << 2) | (part & 2) | ((part >> 2) & 1)


def backward_blocks(lowest, info, q, k, v, qt, kt, lse, unit_low, weights, keep, send,
    up, upt, dqt, dk, dv, dots, moment, total_cols):
    me, first, total = info[0], info[1], info[2]
    rows = keep.shape[0]
    block = rows
    width = q.shape[1]
    heads = width // HD
    lane_head = lax.broadcasted_iota(jnp.int32, (block, width), 1) // HD
    row_head = lax.broadcasted_iota(jnp.int32, (width, block), 0) // HD

    def key_block(j, unused):
        at_k = place(j, block)
        keys = k[pl.ds(at_k, block), :]
        values = v[pl.ds(at_k, block), :]
        dk[...] = jnp.zeros_like(dk)
        dv[...] = jnp.zeros_like(dv)

        def step(at, masked):
            cols = pl.ds(at, block)
            scaled_t = qt[:, cols]
            scaled = q[pl.ds(at, block), :]
            ups = up[pl.ds(at, block), :]
            ups_t = upt[:, cols]
            for h in range(heads):
                part = slice(HD * h, HD * h + HD)
                scores = dot(keys, jnp.where(row_head == h, scaled_t, BF16(0)))
                if masked:
                    row = at + lax.broadcasted_iota(jnp.int32, (1, block), 1)
                    start = start_of(row, first, total)
                    col = at_k + lax.broadcasted_iota(jnp.int32, (block, block), 0)
                    scores = jnp.where((col >= start) & (col <= row), scores, NEGATIVE)
                probs = jnp.exp(scores - lse[h : h + 1, cols])
                grads = dot(values, jnp.where(row_head == h, ups_t, BF16(0)))
                score_grad = (probs * (grads - dots[h : h + 1, cols])).astype(BF16)
                dv[...] += dot(probs.astype(BF16), jnp.where(lane_head == h, ups, BF16(0)))
                dk[...] += dot(score_grad, jnp.where(lane_head == h, scaled, BF16(0)))
                dqt[part, cols] += dot(kt[part, pl.ds(at_k, block)], score_grad)

        def loop(i, carry):
            at = place(i, block)
            begin = start_of(at, first, total)
            last_start = start_of(at + block - 1, first, total)
            whole = (i > j) & (at_k >= last_start)

            @pl.when(whole)
            def _():
                step(at, False)

            @pl.when(jnp.logical_not(whole) & (at_k + block > begin))
            def _():
                step(at, True)

            return carry

        lax.fori_loop(j, 4, loop, 0)
        grads_t = (
            (dqt[:, pl.ds(at_k, block)] * 0.125).astype(BF16),
            dk[...].T.astype(BF16),
            dv[...].T.astype(BF16),
        )
        unit_rows = unit_low[pl.ds(at_k, block), :]
        spread = 0.0
        for c in range(3):
            spread = spread + dot(grads_t[c], weights[c], 0, 1)
            moment[c] += dot(grads_t[c], unit_rows)
            total_cols[c] += jnp.sum(grads_t[c].astype(F32), axis=1, keepdims=True)
        spread = spread.astype(BF16)
        even = (me ^ j) % 2 == 0

        @pl.when(even)
        def _():
            keep[...] = spread

        @pl.when(jnp.logical_not(even))
        def _():
            send[...] = spread

        return unused

    lax.fori_loop(lowest, lowest + 2, key_block, 0)


def attend_backward_first(
    info, q, k, v, qt, kt, ot, lse, gs, unit_low, weights,
    keep, send, up, upt, dots, dqt, moment, total_cols,
    dk, dv,
):
    me = info[0]
    rows = keep.shape[0]
    for n in range(4):
        at = place(me ^ n, rows)
        g = gs[n * rows : (n + 1) * rows, :]
        up[pl.ds(at, rows), :] = g
        upt[:, pl.ds(at, rows)] = g.T
    weighted = upt[...].astype(F32) * ot[...]
    for h in range(dots.shape[0]):
        dots[h : h + 1, :] = column_sum(weighted[HD * h : HD * h + HD])
    dqt[...] = jnp.zeros_like(dqt)
    moment[...] = jnp.zeros_like(moment)
    total_cols[...] = jnp.zeros_like(total_cols)
    backward_blocks(0, info, q, k, v, qt, kt, lse, unit_low, weights, keep, send,
        up, upt, dqt, dk, dv, dots, moment, total_cols)


def attend_backward_second(
    info, q, k, v, qt, kt, lse, unit_low, weights, up, upt, dots, dqt_in, moment_in, cols_in,
    params, vec_in,
    keep, send, heads_out, vec,
    dk, dv, dqt, moment, total_cols,
):
    mine = info[3]
    gain, shift = params[0:1, :], params[1:2, :]
    width = q.shape[1]
    half = dqt.shape[1] // 2
    dqt[:, half:] = dqt_in[:, half:]
    moment[...] = moment_in[...]
    total_cols[...] = cols_in[...]
    backward_blocks(2, info, q, k, v, qt, kt, lse, unit_low, weights, keep, send,
        up, upt, dqt, dk, dv, dots, moment, total_cols)
    step_rows = width // PARTS
    part_rows = 3 * step_rows
    gain_grad = 0.0
    shift_grad = 0.0
    for c in range(3):
        turned = weights[c].astype(F32).T
        gain_grad = gain_grad + column_sum(turned * moment[c])
        shift_grad = shift_grad + column_sum(turned * total_cols[c])
        grad = (moment[c] * gain + total_cols[c] * shift).astype(BF16)
        for p in range(PARTS):
            at = pl.multiple_of(reverse(p ^ mine) * part_rows + c * step_rows, 16)
            heads_out[pl.ds(at, step_rows), :] = grad[p * step_rows : (p + 1) * step_rows]
    pick = lax.broadcasted_iota(jnp.int32, vec_in.shape, 0)
    sums = vec_in[...] + jnp.where(pick == 6, gain_grad, 0.0) + jnp.where(pick == 7, shift_grad, 0.0)
    vec[...] = sums.astype(BF16)


def tokens_backward(tok, own, got, z1_low, gate_w, carry, params, out):
    unit, scale = normalized(tok[...].astype(F32))
    grad = own[...].astype(F32) + got[...].astype(F32) + dot(z1_low[...], gate_w[...], 1, 1)
    h = grad * params[0:1, :]
    out[...] = (
        carry[...] + scale * (h - row_mean(h) - unit * row_mean(h * unit))
    ).astype(BF16)


def each_part(info, refs, rows, order=ORDER):
    pos = 0
    for ref in refs:
        for n in range(ref.shape[0] // rows):
            yield order[pos] ^ info[3], ref, n * rows
            pos += 1


def unpack_ffn(info, d0, d1, d2, u0, u1, u2, down, up, turned):
    step = down.shape[0] // PARTS
    for p, ref, at in each_part(info, (d0, d1, d2), step):
        turned[pl.ds(place(p, step), step), :] = ref[at : at + step].astype(F32)
    for p, ref, at in each_part(info, (u0, u1, u2), step, UP_ORDER):
        up[pl.ds(place(p, step), step), :] = ref[at : at + step].astype(F32)
    down[...] = turned[...].T


def unpack_rest(info, s0, s1, s2, out, gates):
    rows = out.shape[0]
    step = rows // PARTS
    for p, ref, at in each_part(info, (s0, s1, s2), 3 * step, REST_ORDER):
        out[pl.ds(place(p, step), step), :] = ref[at : at + step].astype(F32)
        for n in range(2):
            first = at + (n + 1) * step
            gates[pl.ds(pl.multiple_of(n * rows + p * step, step), step), :] = ref[
                first : first + step
            ]


def unpack_heads(info, s0, s1, s2, heads, turned):
    step = heads.shape[2] // PARTS
    for p, ref, at in each_part(info, (s0, s1, s2), 3 * step):
        for c in range(3):
            turned[c, pl.ds(place(p, step), step), :] = ref[at + c * step : at + (c + 1) * step].astype(F32)
    for c in range(3):
        heads[c] = turned[c].T


def unpack_gates(info, s0, s1, s2, s3, gate, passed):
    rows = gate.shape[0] // 4
    for k, ref in enumerate((s0, s1, s2, s3)):
        at = place(info[0] ^ k, rows)
        gate[pl.ds(at, rows), :] = ref[0:rows].astype(F32)
        passed[pl.ds(at, rows), :] = ref[rows : 2 * rows].astype(F32)


def unpack_vectors(info, one, two, *outs):
    sums = one[...] + two[...]
    for n in range(8):
        outs[n][...] = sums[n : n + 1]
    pick = lax.broadcasted_iota(jnp.int32, sums.shape, 0) == 8 + info[0]
    outs[8][...] = column_sum(jnp.where(pick, sums, 0.0))


def swap_tensor(values, mask):
    return lax.ppermute(values, "tensor", [(i, i ^ mask) for i in range(4)])


def swap_dp(values, mask):
    return lax.ppermute(values, "dp", [(i, i ^ mask) for i in range(lax.axis_size("dp"))])


def fold(*terms):
    return sum(term.astype(F32) for term in terms).astype(BF16)


def scatter(values, axis, mask):
    half = values.shape[0] // 2
    got = yield values[half:], axis, mask
    return fold(values[:half], got)


def reduce_dp(values, masks, more=None):
    extra = 0 if more is None else more.shape[0]
    for mask in masks:
        half = values.shape[0] // 2
        sent = values[half:]
        if extra:
            sent = jnp.concatenate([sent, more])
        got = yield sent, "dp", mask
        values = fold(values[:half], got[:half])
        if extra:
            more = fold(more, got[half:])
    mask = 4
    while mask < lax.axis_size("dp"):
        size = values.shape[0]
        if mask == 4:
            sent = [values[size // 2 :], values[: size // 2]]
        else:
            sent = [values]
        if extra:
            sent = sent + [more]
        got = yield jnp.concatenate(sent), "dp", mask
        values = fold(values, got[:size])
        if extra:
            more = fold(more, got[size:])
        mask *= 2
    return (values, more) if extra else values


def gather_dp(values, masks=(2, 1)):
    s2 = yield values, "dp", masks[0]
    s3 = yield jnp.concatenate([values, s2]), "dp", masks[1]
    return values, s2, s3


def split_rest(values):
    step = values.shape[0] // PARTS
    shares = [values[n * step : (n + 1) * step] for n in range(PARTS)]
    return jnp.concatenate(shares[0::2]), jnp.concatenate(shares[1::2])


def run_chains(chains):
    results = [None] * len(chains)
    waiting = [None] * len(chains)
    alive = list(range(len(chains)))
    while alive:
        for n in list(alive):
            try:
                values, axis, mask = chains[n].send(waiting[n])
            except StopIteration as stop:
                results[n] = stop.value
                alive.remove(n)
                continue
            waiting[n] = (swap_dp if axis == "dp" else swap_tensor)(values, mask)
    return results


def body(
    tokens,
    norm_gain,
    norm_shift,
    heads_weight,
    output_weight,
    output_bias,
    gate_weight,
    gate_bias,
    second_gain,
    second_shift,
    up_weight,
    up_bias,
    down_weight,
    down_bias,
    pass_weight,
    pass_bias,
    lengths,
    owners,
    cotangent,
):
    rows, width = tokens.shape
    total_rows = 4 * rows
    head_width = heads_weight.shape[2]
    me = lax.axis_index("tensor")
    params = jnp.stack(
        [norm_gain, norm_shift, output_bias, gate_bias, second_gain, second_shift]
        + [down_bias, pass_bias]
    )
    split_heads = heads_weight.transpose(1, 0, 2)

    def kept(count):
        kinds = [shape(count, width)] + [shape(count, head_width)] * 3
        return kinds + [shape(head_width, count)] * 2

    tok2 = swap_tensor(tokens, 2)
    tok1 = swap_tensor(tokens, 1)
    state = [(head_width, 2 * rows), (8, 2 * rows), (8, 2 * rows)]
    info, *near = call(
        attend_near,
        "attend_near",
        (lengths, owners, tokens, tok1, params, split_heads),
        [shape(4, dtype=jnp.int32)]
        + kept(2 * rows)
        + [shape(head_width, 2 * rows)]
        + [shape(*dims, dtype=F32) for dims in state],
        scalars=2,
        micros=6,
        mib=12,
    )
    up_held, down_held, info = lax.optimization_barrier((up_weight, down_weight, info))
    bias_rows = jnp.broadcast_to(up_bias[None, :], (16, width))
    pack0 = jnp.concatenate([up_held, bias_rows, down_held, jnp.zeros((48, width), BF16)])
    quarter = pack0.shape[0] // WEIGHT_PARTS
    sent = lax.dynamic_slice_in_dim(
        pack0, lax.axis_index("dp") % WEIGHT_PARTS * quarter, quarter, 0
    )
    sent, out_held, tok2, *near = lax.optimization_barrier((sent, output_weight, tok2, *near))
    out2 = swap_tensor(out_held, 2)
    part0 = swap_tensor(sent, 2)
    tok3 = swap_tensor(tok2, 1)

    later = kept(total_rows) + [shape(head_width, total_rows, dtype=F32)]
    unit, q, key, v, qt, kt, ot, lse, a0, a1, a2, a3 = call(
        attend_far,
        "attend_far",
        (info, tok2, tok3, params, split_heads) + tuple(near),
        later
        + [shape(head_width // HD, total_rows, dtype=F32)]
        + [shape(rows, head_width)] * 4,
        [pltpu.VMEM(item.shape, item.dtype) for item in kept(2 * rows)]
        + [
            pltpu.VMEM((total_rows, head_width), BF16),
            pltpu.VMEM((head_width, total_rows), BF16),
            pltpu.VMEM((head_width, total_rows), BF16),
            pltpu.VMEM((head_width, total_rows), F32),
        ]
        + [pltpu.VMEM((dims[0], rows), F32) for dims in state]
        + [pltpu.SemaphoreType.DMA((13,))],
        micros=10,
        mib=20,
        far=range(len(later)),
    )
    a0, a1, a2, a3, out2, part0, pack0, out_held = lax.optimization_barrier(
        (a0, a1, a2, a3, out2, part0, pack0, output_weight)
    )
    pack1 = swap_tensor(pack0, 1)
    out1 = swap_tensor(out_held, 1)
    out3 = swap_tensor(out2, 1)
    p0, p1, p2, p3 = a0, swap_tensor(a1, 1), swap_tensor(a2, 2), swap_tensor(a3, 3)
    part1, part2 = swap_dp(part0, 1), swap_dp(part0, 2)
    p1, p2, p3, out3, part1, part2 = lax.optimization_barrier((p1, p2, p3, out3, part1, part2))
    part3 = swap_dp(part2, 1)
    outs = (output_weight, out1, out2, out3)
    square, square32 = shape(rows, width), shape(rows, width, dtype=F32)
    n2, ffn_low, y, gate2, gate, mixed, ffn, gn2, vec, keep0, send0 = call(
        middle_first,
        "middle_first",
        (info, p0, p1, p2, p3) + outs + (tokens, cotangent, pack0, pack1, params)
        + (gate_weight, pass_weight),
        [square] * 2
        + [square32] * 6
        + [shape(16, width, dtype=F32)]
        + [shape(2 * width, width)] * 2,
        micros=9,
        mib=20,
    )
    n2, part3, send0 = lax.optimization_barrier((n2, part3, send0))
    parts2 = jnp.concatenate([part0, part1, part2, part3])
    parts3 = swap_tensor(parts2, 1)
    got0 = swap_tensor(send0, 1)
    output, g0, g1, g2, g3, hid, pre_low, z2_low, z1_low, mixed_low, carry, vec = call(
        middle_second,
        "middle_second",
        (info,) + outs + (tokens, cotangent, parts2, parts3, params, pass_weight)
        + (n2, ffn_low, y, gate2, gate, mixed, ffn, gn2, vec),
        [square]
        + [shape(rows, head_width)] * 4
        + [shape(2, rows, width)] * 2
        + [square] * 3
        + [square32, shape(16, width, dtype=F32)],
        [pltpu.VMEM(pack0.shape, BF16)] * 2,
        micros=7,
        mib=20,
    )
    g1, g2, g3 = swap_tensor(g1, 1), swap_tensor(g2, 2), swap_tensor(g3, 3)
    keep, send, vec = call(
        weight_grads,
        "weight_grads",
        (info, hid, pre_low, ffn_low, z2_low, n2, z1_low, mixed_low, tokens, params)
        + (gate_weight, p0, p1, p2, p3, vec),
        [shape(2 * width + 6 * head_width, width)] * 2
        + [shape(16, width, dtype=F32)],
        [pltpu.VMEM((width, width), F32)] * 2,
        micros=4,
        mib=14,
    )
    g1, g2, g3, got0, keep, send, vec = lax.optimization_barrier(
        (g1, g2, g3, got0, keep, send, vec)
    )
    got = swap_tensor(send, 1)
    near = fold(keep0, got0)
    total = fold(keep, got)
    half = width // 2
    down0, up_keep = near[:width], near[width:]
    down2, up_send = total[:width], total[width : 2 * width]
    rest = total[2 * width :]
    down_send = jnp.concatenate([down0[half:], down2[half:]])
    down_keep = jnp.concatenate([down0[:half], down2[:half]])
    half = rest.shape[0] // 2
    down_send, up_send, rest_send, vec = lax.optimization_barrier(
        (down_send, up_send, rest[half:], vec)
    )
    down_got = swap_dp(down_send, 1)
    up_got = swap_tensor(up_send, 2)
    rest_got = swap_dp(rest_send, 2)
    blocks = [pltpu.VMEM((rows, head_width), F32)] * 2
    totals = [(head_width, total_rows), (3, head_width, width), (3, head_width, 1)]
    rows_keep0, rows_send0, up, upt, dots, dqt, moment, total_cols = call(
        attend_backward_first,
        "attend_backward_first",
        (info, q, key, v, qt, kt, ot, lse, jnp.concatenate([g0, g1, g2, g3]), unit, split_heads),
        [square] * 2
        + [shape(total_rows, head_width), shape(head_width, total_rows)]
        + [shape(head_width // HD, total_rows, dtype=F32)]
        + [shape(*dims, dtype=F32) for dims in totals],
        blocks,
        micros=12,
        mib=12,
    )
    rows_keep0, rows_send0, dqt, down_got, up_got, rest_got = lax.optimization_barrier(
        (rows_keep0, rows_send0, dqt, down_got, up_got, rest_got)
    )
    down_part = fold(down_keep, down_got)
    up_part = fold(up_keep, up_got)
    rest = fold(rest[:half], rest_got)
    half = down_part.shape[0] // 2
    down_send, up_send, dqt = lax.optimization_barrier((down_part[half:], up_part[half:], dqt))
    down_got = swap_tensor(down_send, 2)
    up_got = swap_dp(up_send, 1)
    rest_kept, rest_sent = split_rest(rest)
    rest_got = swap_tensor(rest_sent, 2)
    rows_got0 = swap_tensor(rows_send0, 1)
    keep1, send1, heads_sum, vec = call(
        attend_backward_second,
        "attend_backward_second",
        (info, q, key, v, qt, kt, lse, unit, split_heads, up, upt, dots, dqt, moment)
        + (total_cols, params, vec),
        [square] * 2 + [shape(3 * head_width, width), shape(16, width)],
        blocks + [pltpu.VMEM(dims, F32) for dims in totals],
        micros=7,
        mib=12,
    )
    down_got, up_got, rest_got, rows_got0, heads_sum, vec, keep1, send1 = lax.optimization_barrier(
        (down_got, up_got, rest_got, rows_got0, heads_sum, vec, keep1, send1)
    )

    down_part, up_part = fold(down_part[:half], down_got), fold(up_part[:half], up_got)
    step = width // PARTS
    both = jnp.concatenate(
        [
            piece[n * step : (n + 1) * step]
            for n in range(PARTS // 2)
            for piece in (down_part, up_part)
        ]
    )

    size = both.shape[0] // 2
    first_ffn = fold(both[:size], swap_dp(both[size:], 2))

    def heads_chain(values, vec):
        size = values.shape[0] // 2
        got = yield jnp.concatenate([values[size:], vec]), "dp", 1
        values, vec = fold(values[:size], got[:size]), fold(vec, got[size:])
        values, _ = lax.optimization_barrier((values, first_ffn))
        values, vec = yield from reduce_dp(values, (2,), vec)
        vec = vec.astype(F32)
        s2 = yield values, "dp", 2
        got = yield vec, "tensor", 1
        vec = vec + got
        got = yield vec, "tensor", 2
        vectors = call(
            unpack_vectors,
            "unpack_vectors",
            (info, vec, got),
            [shape(1, width, dtype=F32)] * 9,
        )
        s3 = yield jnp.concatenate([values, s2]), "dp", 1
        (heads_grad,) = call(
            unpack_heads,
            "unpack_heads",
            (info, values, s2, s3),
            [shape(3, width, head_width, dtype=F32)],
            [pltpu.VMEM((3, head_width, width), F32)],
        )
        return heads_grad, [v.reshape(width) for v in vectors]

    def rows_chain():
        got = yield send1, "tensor", 1
        lower, upper = fold(rows_keep0, rows_got0), fold(keep1, got)
        is_lower = me < 2
        near = jnp.where(is_lower, lower, upper)
        far = yield jnp.where(is_lower, upper, lower), "tensor", 2
        return call(
            tokens_backward,
            "tokens_backward",
            (tokens, near, far, z1_low, gate_weight, carry, params),
            [square],
            scalars=0,
        )[0]

    def rest_chain(values):
        values = yield from reduce_dp(values, (1,))
        parts = yield from gather_dp(values, (1, 2))
        out_grad, gates = call(
            unpack_rest,
            "unpack_rest",
            (info,) + parts,
            [shape(head_width, width, dtype=F32), shape(2 * head_width, width)],
        )
        gates2 = yield gates, "tensor", 2
        other = yield jnp.concatenate([gates, gates2]), "tensor", 1
        gate_grad, pass_grad = call(
            unpack_gates,
            "unpack_gates",
            (info, gates, other[: 2 * head_width], gates2, other[2 * head_width :]),
            [shape(width, width, dtype=F32)] * 2,
        )
        return out_grad, gate_grad, pass_grad

    def ffn_chain(values):
        values = yield from reduce_dp(values, ())
        d0 = jnp.concatenate([values[:step], values[2 * step : 3 * step]])
        u0 = jnp.concatenate([values[step : 2 * step], values[3 * step :]])
        d1 = yield d0, "dp", 2
        u1 = yield u0, "dp", 1
        d2 = yield jnp.concatenate([d0, d1]), "dp", 1
        u2 = yield jnp.concatenate([u0, u1]), "dp", 2
        return d0, d1, d2, u0, u1, u2

    (tokens_grad,) = run_chains([rows_chain()])
    (
        (out_grad, gate_grad, pass_grad),
        ffn_parts,
        (heads_grad, vectors),
    ) = run_chains(
        [
            rest_chain(fold(rest_kept, rest_got)),
            ffn_chain(first_ffn),
            heads_chain(heads_sum, vec),
        ]
    )
    down_grad, up_grad = call(
        unpack_ffn,
        "unpack_ffn",
        (info,) + ffn_parts,
        [shape(width, width, dtype=F32)] * 2,
        [pltpu.VMEM((width, width), F32)],
    )
    (
        down_bias_grad,
        pass_bias_grad,
        second_shift_grad,
        second_gain_grad,
        output_bias_grad,
        gate_bias_grad,
        norm_gain_grad,
        norm_shift_grad,
        up_bias_grad,
    ) = vectors
    return (
        output,
        tokens_grad,
        norm_gain_grad,
        norm_shift_grad,
        heads_grad.transpose(1, 0, 2),
        out_grad,
        output_bias_grad,
        gate_grad,
        gate_bias_grad,
        second_gain_grad,
        second_shift_grad,
        up_grad,
        up_bias_grad,
        down_grad,
        down_bias_grad,
        pass_grad,
        pass_bias_grad,
    )


def solution(mesh):
    placed = (
        P(("dp", "tensor"), None),
        P(),
        P(),
        P(None, None, "tensor"),
        P("tensor", None),
        P(),
        P(),
        P(),
        P(),
        P(),
        P(None, "tensor"),
        P("tensor"),
        P("tensor", None),
        P(),
        P(),
        P(),
        P(),
        P(),
        P(("dp", "tensor"), None),
    )
    return jax.shard_map(
        body,
        mesh=mesh,
        in_specs=placed,
        out_specs=(
            P(("dp", "tensor"), None),
            P(("dp", "tensor"), None),
            P(),
            P(),
            P(None, None, "tensor"),
            P("tensor", None),
            P(),
            P(),
            P(),
            P(),
            P(),
            P(None, "tensor"),
            P("tensor"),
            P("tensor", None),
            P(),
            P(),
            P(),
        ),
        check_vma=False,
    )
```
